32 devices in a mesh: dp: 32 (over z, y, x, core).
Axes of the slice: x: 2, y: 2, z: 4, core: 2. Of those that a mesh axis runs over, the one named last changes fastest.
Arguments:
- img_emb: bfloat16 [16384, 1152], P('dp'), may hold values from -6 to 6
- txt_emb: bfloat16 [16384, 1152], P('dp'), may hold values from -6 to 6
- img_proj: bfloat16 [1152, 1152], replicated, may hold values from -0.1875 to 0.1875
- txt_proj: bfloat16 [1152, 1152], replicated, may hold values from -0.1875 to 0.1875
- log_scale: float32 [1], replicated, may hold values from 1.1 to 2.1
- bias: float32 [1], replicated, may hold values from -3 to -1
Outputs:
- d_img_emb: bfloat16 [16384, 1152], P('dp')
- d_txt_emb: bfloat16 [16384, 1152], P('dp')
- d_img_proj: float32 [1152, 1152], replicated
- d_txt_proj: float32 [1152, 1152], replicated
The draws below stay inside these ranges and needn't reach their ends.
All inputs are finite; a program needn't handle non-finite values.
Results may differ from the reference program's by a relative error of at most 0.02.
Values may be sent and summed in bfloat16 or wider, within the bound.
No kernel may reach another device: no remote copies, remote signals or barrier semaphores. Data moves between devices by JAX's collectives and lax.ppermute only.
A program may use at most 128 MiB of HBM per device.

```python
import jax
import jax.numpy as jnp
from jax import lax

D = 1152
ROWS = 512
REACH = 3
TOTAL = 16384
N_DP = 32


def block_scale(key, extent, split, low, high):
    factor_of = 1.0
    for axis_at, blocks in split:
        steps = jax.random.uniform(jax.random.fold_in(jax.random.fold_in(key, 6), axis_at), (blocks,), jnp.float32, low / len(split), high / len(split))
        factor_of = factor_of * jnp.repeat(jnp.exp(steps), extent[axis_at] // blocks).reshape((-1,) + (1,) * (len(extent) - 1 - axis_at))
    return factor_of


def gaussian(stream_key, extent, spread, reach, cuts=(), kind=jnp.bfloat16):
    level = block_scale(stream_key, extent, cuts, -0.22, 0.18) if cuts else 1.0
    values = jax.random.normal(stream_key, extent, jnp.float32) * spread * level
    return jnp.minimum(jnp.maximum(values, -reach), reach).astype(kind)


def setup_inputs(seed: int = 0) -> dict:
    splits = jax.random.split(jax.random.key(seed), 7)
    return {
        "img_emb": gaussian(splits[0], (TOTAL, D), 1.0, 6.0, ((0, 32),)),
        "txt_emb": gaussian(splits[1], (TOTAL, D), 1.0, 6.0, ((0, 32),)),
        "img_proj": gaussian(splits[2], (D, D), D ** -0.5, 0.1875),
        "txt_proj": gaussian(splits[3], (D, D), D ** -0.5, 0.1875),
        "log_scale": jnp.clip(jax.random.uniform(splits[4], (1,), jnp.float32, 1.1, 2.1), 1.1, 2.1),
        "bias": jnp.clip(jax.random.uniform(splits[5], (1,), jnp.float32, -3.0, -1.0), -3.0, -1.0),
    }


def unit_rows(embeddings, projection):
    projected = jnp.dot(embeddings, projection, preferred_element_type=jnp.float32)
    row_norm = jnp.sqrt(lax.optimization_barrier(jnp.sum(projected * projected, axis=1, keepdims=True)) + 1e-06)
    return (projected / row_norm, row_norm)

def unit_back(grad_unit, unit_vals, row_norm):
    inner = lax.optimization_barrier(jnp.sum(unit_vals * grad_unit, axis=1, keepdims=True))
    return (grad_unit - unit_vals * inner) / row_norm

def pair_grads(image_block, text_block, logit_scale, logit_bias, own_block):
    logits = logit_scale * jnp.dot(image_block, text_block.T, preferred_element_type=jnp.float32) + logit_bias
    coefficients = jax.nn.sigmoid(logits)
    if own_block:
        count = logits.shape[0]
        diagonal_mask = jnp.arange(count)[:, None] == jnp.arange(count)[None, :]
        coefficients = jnp.where(diagonal_mask, coefficients - 1.0, coefficients)
    coefficients = coefficients.astype(jnp.bfloat16)
    image_term = logit_scale * jnp.dot(coefficients, text_block, preferred_element_type=jnp.float32)
    text_term = logit_scale * jnp.dot(coefficients.T, image_block, preferred_element_type=jnp.float32)
    return (image_term, text_term)

def reference(img_emb, txt_emb, img_proj, txt_proj, log_scale, bias):
    logit_scale = jnp.exp(log_scale[0])
    logit_bias = bias[0]
    img_unit, img_norm = unit_rows(img_emb, img_proj)
    txt_unit, txt_norm = unit_rows(txt_emb, txt_proj)
    img_blocks = img_unit.astype(jnp.bfloat16).reshape(N_DP, ROWS, D)
    txt_blocks = txt_unit.astype(jnp.bfloat16).reshape(N_DP, ROWS, D)

    def visit_block(text_grads, inputs):
        image_block, block_id = inputs
        image_total = jnp.zeros((ROWS, D), jnp.float32)
        for reach_step in range(-REACH, REACH + 1):
            partner = ((block_id + reach_step) % N_DP).astype(jnp.int32)
            text_block = lax.dynamic_index_in_dim(txt_blocks, partner, 0, keepdims=False)
            image_term, text_term = pair_grads(image_block, text_block, logit_scale, logit_bias, reach_step == 0)
            image_total = image_total + image_term
            current = lax.dynamic_index_in_dim(text_grads, partner, 0, keepdims=False)
            text_grads = lax.dynamic_update_index_in_dim(text_grads, current + text_term, partner, 0)
        return (text_grads, image_total)
    start_grads = jnp.zeros((N_DP, ROWS, D), jnp.float32)
    block_ids = jnp.arange(N_DP, dtype=jnp.int32)
    text_grads, image_grads = lax.scan(visit_block, start_grads, (img_blocks, block_ids))
    grad_img = image_grads.reshape(TOTAL, D)
    grad_txt = text_grads.reshape(TOTAL, D)
    img_du = unit_back(grad_img, img_unit, img_norm).astype(jnp.bfloat16)
    txt_du = unit_back(grad_txt, txt_unit, txt_norm).astype(jnp.bfloat16)
    d_img_emb = jnp.dot(img_du, img_proj.T, preferred_element_type=jnp.float32).astype(jnp.bfloat16)
    d_txt_emb = jnp.dot(txt_du, txt_proj.T, preferred_element_type=jnp.float32).astype(jnp.bfloat16)
    d_img_proj = jnp.dot(img_emb.T, img_du, preferred_element_type=jnp.float32)
    d_txt_proj = jnp.dot(txt_emb.T, txt_du, preferred_element_type=jnp.float32)
    return (d_img_emb, d_txt_emb, d_img_proj, d_txt_proj)
```

```python
import jax
import jax.numpy as jnp
from jax import lax
from jax.sharding import PartitionSpec as P

REACH = 3


def hop(value, size, chips, flip):
    pairs = []
    for i in range(size):
        chip, core = i // 2, i % 2
        to_chip = (chip + (chips if not callable(chips) else chips(core))) % (size // 2)
        pairs.append((i, 2 * to_chip + (1 - core if flip else core)))
    return lax.ppermute(value, "dp", pairs)


def row_norms(raw):
    return jnp.sqrt(jnp.sum(raw * raw, axis=1, keepdims=True) + 1e-06)


def coefficients(left, right, scale, bias):
    logits = scale * jnp.dot(left, right.T, preferred_element_type=jnp.float32) + bias
    return jax.nn.sigmoid(logits)


def body(img_emb, txt_emb, img_proj, txt_proj, log_scale, bias):
    size = lax.axis_size("dp")
    rows = img_emb.shape[0]
    scale = jnp.exp(log_scale[0])
    bias = bias[0]
    image_side = lax.axis_index("dp") % 2 == 0

    img_raw = jnp.dot(img_emb, img_proj, preferred_element_type=jnp.float32)
    txt_raw = jnp.dot(txt_emb, txt_proj, preferred_element_type=jnp.float32)
    img_z = (img_raw / row_norms(img_raw)).astype(jnp.bfloat16)
    txt_z = (txt_raw / row_norms(txt_raw)).astype(jnp.bfloat16)
    mine = jnp.where(image_side, img_z, txt_z)
    met = jnp.where(image_side, txt_z, img_z)

    met_other = hop(mine, size, 0, True)
    from_before = hop(met, size, 1, False), hop(mine, size, 1, True)
    from_after = hop(met, size, -1, False), hop(mine, size, -1, True)
    far = lambda core: 2 if core == 1 else -2
    far_other = hop(met, size, far, False)
    far_own = hop(mine, size, far, True)

    own_emb = jnp.where(image_side, img_emb, txt_emb)
    other_emb = hop(jnp.where(image_side, txt_emb, img_emb), size, 0, True)
    emb = jnp.concatenate([own_emb, other_emb], axis=0)
    weight = jnp.where(image_side, img_proj, txt_proj)
    raw = jnp.dot(emb, weight, preferred_element_type=jnp.float32)
    norm = row_norms(raw)
    unit = raw / norm
    z = unit.astype(jnp.bfloat16)

    row_at = lax.broadcasted_iota(jnp.int32, (2 * rows, rows), 0)
    col_at = lax.broadcasted_iota(jnp.int32, (2 * rows, rows), 1)

    def term(left, right, diagonal=None):
        coef = coefficients(left, right, scale, bias)
        if diagonal is not None:
            coef = jnp.where(row_at == col_at + diagonal, coef - 1.0, coef)
        return jnp.dot(coef.astype(jnp.bfloat16), right, preferred_element_type=jnp.float32)

    grad = term(z, met, 0) + term(z, met_other, rows)
    for block in (*from_before, *from_after):
        grad = grad + term(z, block)
    far_grad = jnp.concatenate([term(z[:rows], far_own), term(z[rows:], far_other)], axis=0)
    grad = scale * (grad + far_grad)

    inner = jnp.sum(unit * grad, axis=1, keepdims=True)
    du = ((grad - unit * inner) / norm).astype(jnp.bfloat16)

    part = jnp.dot(emb.T, du, preferred_element_type=jnp.float32).astype(jnp.bfloat16)
    groups = [list(range(core, size, 2)) for core in range(2)]
    d_weight = lax.psum(part, "dp", axis_index_groups=groups)
    d_weight_other = hop(d_weight, size, 0, True)
    d_img_proj = jnp.where(image_side, d_weight, d_weight_other).astype(jnp.float32)
    d_txt_proj = jnp.where(image_side, d_weight_other, d_weight).astype(jnp.float32)

    d_emb = jnp.dot(du, weight.T, preferred_element_type=jnp.float32).astype(jnp.bfloat16)
    d_emb_other = hop(d_emb[rows:], size, 0, True)
    d_img_emb = jnp.where(image_side, d_emb[:rows], d_emb_other)
    d_txt_emb = jnp.where(image_side, d_emb_other, d_emb[:rows])
    return (d_img_emb, d_txt_emb, d_img_proj, d_txt_proj)


def solution(mesh):
    return jax.shard_map(
        body,
        mesh=mesh,
        in_specs=(P("dp", None), P("dp", None), P(), P(), P(), P()),
        out_specs=(P("dp", None), P("dp", None), P(), P()),
        check_vma=False,
    )
```

```python
import functools

import jax
import jax.numpy as jnp
from jax import lax
from jax.experimental import pallas as pl
from jax.experimental.pallas import tpu as pltpu
from jax.sharding import PartitionSpec as P

REACH = 3
BF16, F32 = jnp.bfloat16, jnp.float32
TILE = 256
VMEM = pl.BlockSpec(memory_space=pltpu.VMEM)
SMEM = pl.BlockSpec(memory_space=pltpu.SMEM)
PARAMS = pltpu.CompilerParams(vmem_limit_bytes=40 * 1024 * 1024)


def dot_t(left, right):
    return lax.dot_general(left, right, (((1,), (1,)), ((), ())), preferred_element_type=F32)


def dot(left, right):
    return lax.dot_general(left, right, (((1,), (0,)), ((), ())), preferred_element_type=F32)


def hop(value, size, chips, flip):
    pairs = []
    for i in range(size):
        chip, core = i // 2, i % 2
        pairs.append((i, 2 * ((chip + chips(core)) % (size // 2)) + (1 - core if flip else core)))
    return lax.ppermute(value, "dp", pairs)


def swap(value, size, mask):
    return lax.ppermute(value, "dp", [(i, i ^ mask) for i in range(size)])


def first_kernel(role, img_emb, txt_emb, img_proj, txt_proj, mine, met):
    rows = img_emb.shape[0]

    def unit(emb, proj, store):
        for at in range(0, rows, TILE):
            raw = dot(emb[at : at + TILE, :], proj[...])
            norm = jnp.sqrt(jnp.sum(raw * raw, axis=1, keepdims=True) + 1e-06)
            store(at, (raw / norm).astype(BF16))

    def store_img(at, z):
        @pl.when(role[0] == 0)
        def _():
            mine[at : at + TILE, :] = z

        @pl.when(role[0] != 0)
        def _():
            met[at : at + TILE, :] = z

    def store_txt(at, z):
        @pl.when(role[0] == 0)
        def _():
            met[at : at + TILE, :] = z

        @pl.when(role[0] != 0)
        def _():
            mine[at : at + TILE, :] = z

    unit(img_emb, img_proj, store_img)
    unit(txt_emb, txt_proj, store_txt)


def first_units(role, img_emb, txt_emb, img_proj, txt_proj):
    out = jax.ShapeDtypeStruct(img_emb.shape, BF16)
    return pl.pallas_call(
        first_kernel,
        out_shape=(out, out),
        in_specs=[SMEM] + [VMEM] * 4,
        out_specs=(VMEM, VMEM),
        compiler_params=PARAMS,
        name="first_units",
    )(role, img_emb, txt_emb, img_proj, txt_proj)


def pair_term(z, block, scale, bias, diagonal):
    half = dot_t(z, block) * (0.5 * scale) + 0.5 * bias
    coef = 0.5 * jnp.tanh(half) + 0.5
    if diagonal is not None:
        row_at = lax.broadcasted_iota(jnp.int32, coef.shape, 0) + diagonal
        col_at = lax.broadcasted_iota(jnp.int32, coef.shape, 1)
        coef = jnp.where(row_at == col_at, coef - 1.0, coef)
    return dot(coef.astype(BF16), block)


def own_chip_kernel(scale, bias, z, met, met_other, grad):
    step = pl.program_id(0)
    per_block = met.shape[0] // TILE
    here = step * TILE
    near = pair_term(z[...], met[...], scale[0], bias[0], here)
    other = pair_term(z[...], met_other[...], scale[0], bias[0], here - per_block * TILE)
    grad[...] = near + other


def first_phase_kernel(scale, bias, z, one, two, far_own, far_other, grad_in, grad):
    step = pl.program_id(0)
    per_block = one.shape[0] // TILE
    total = grad_in[...] + pair_term(z[...], one[...], scale[0], bias[0], None)
    total = total + pair_term(z[...], two[...], scale[0], bias[0], None)

    @pl.when(step < per_block)
    def _():
        grad[...] = total + pair_term(z[...], far_own[...], scale[0], bias[0], None)

    @pl.when(step >= per_block)
    def _():
        grad[...] = total + pair_term(z[...], far_other[...], scale[0], bias[0], None)


def row_tiles(columns):
    return pl.BlockSpec((TILE, columns), lambda i: (i, 0))


def whole(array):
    return pl.BlockSpec(array.shape, lambda i: (0,) * array.ndim)


def call_tiles(kernel, scale, bias, z, blocks, grads, name):
    rows, columns = z.shape
    return pl.pallas_call(
        kernel,
        grid=(rows // TILE,),
        out_shape=jax.ShapeDtypeStruct((rows, columns), F32),
        in_specs=[SMEM, SMEM, row_tiles(columns)]
        + [whole(b) for b in blocks]
        + [row_tiles(columns)] * len(grads),
        out_specs=row_tiles(columns),
        compiler_params=PARAMS,
        name=name,
    )(scale, bias, z, *blocks, *grads)


def last_phase_kernel(
    starts, scale, bias, z, one, two, grad_in, unit, norm, emb_t, du, *rest
):
    (plane, line), du_all = (rest[:4], rest[4:8]), rest[8]
    step = pl.program_id(0)
    grad = grad_in[...] + pair_term(z[...], one[...], scale[0], bias[0], None)
    grad = scale[0] * (grad + pair_term(z[...], two[...], scale[0], bias[0], None))
    units = unit[...]
    inner = jnp.sum(units * grad, axis=1, keepdims=True)
    rounded = ((grad - units * inner) / norm[...]).astype(BF16)
    du[...] = rounded
    du_all[pl.ds(pl.multiple_of(step * TILE, TILE), TILE), :] = rounded

    @pl.when(step == pl.num_programs(0) - 1)
    def _():
        for m, out in enumerate((*plane, *line)):
            height = out.shape[0]
            part = emb_t[pl.ds(pl.multiple_of(starts[m], 32), height), :]
            out[...] = dot(part, du_all[...]).astype(out.dtype)


def last_phase(starts, scale, bias, z, one, two, grad, unit, norm, emb_t):
    rows, columns = z.shape
    heights = [columns // 6] * 4 + [columns // 12] * 4
    pieces = [
        jax.ShapeDtypeStruct((h, columns), F32 if m % 4 == 0 else BF16)
        for m, h in enumerate(heights)
    ]
    return pl.pallas_call(
        last_phase_kernel,
        grid=(rows // TILE,),
        out_shape=(jax.ShapeDtypeStruct((rows, columns), BF16), *pieces),
        in_specs=[
            SMEM,
            SMEM,
            SMEM,
            row_tiles(columns),
            whole(one),
            whole(two),
            row_tiles(columns),
            row_tiles(columns),
            row_tiles(1),
            whole(emb_t),
        ],
        out_specs=(row_tiles(columns), *[whole(p) for p in pieces]),
        scratch_shapes=[pltpu.VMEM((rows, columns), BF16)],
        compiler_params=PARAMS,
        name="last_phase",
    )(starts, scale, bias, z, one, two, grad, unit, norm, emb_t)


def rows_back_kernel(du, weight, own, other):
    step = pl.program_id(0)
    back = dot_t(du[...], weight[...]).astype(BF16)

    @pl.when(step < pl.num_programs(0) // 2)
    def _():
        own[...] = back

    @pl.when(step >= pl.num_programs(0) // 2)
    def _():
        other[...] = back


def rows_back(du, weight):
    rows, columns = du.shape
    half = rows // 2 // TILE
    out = jax.ShapeDtypeStruct((rows // 2, columns), BF16)
    return pl.pallas_call(
        rows_back_kernel,
        grid=(rows // TILE,),
        out_shape=(out, out),
        in_specs=[row_tiles(columns), whole(weight)],
        out_specs=(
            pl.BlockSpec((TILE, columns), lambda i: (jnp.minimum(i, half - 1), 0)),
            pl.BlockSpec((TILE, columns), lambda i: (jnp.maximum(i - half, 0), 0)),
        ),
        compiler_params=PARAMS,
        name="rows_back",
    )(du, weight)


def add_split_kernel(starts, keep_a, a1, a2, a3, keep_b, b1, b2, b3, *rest):
    outs_a, outs_b, sum_a, sum_b = rest[:4], rest[4:8], rest[8], rest[9]
    sum_a[...] = (keep_a[...] + a1[...].astype(F32)) + (a2[...].astype(F32) + a3[...].astype(F32))
    sum_b[...] = (keep_b[...] + b1[...].astype(F32)) + (b2[...].astype(F32) + b3[...].astype(F32))
    for m in range(4):
        at = pl.multiple_of(starts[m], 16)
        outs_a[m][...] = sum_a[pl.ds(at, outs_a[m].shape[0]), :].astype(outs_a[m].dtype)
        at = pl.multiple_of(starts[4 + m], 8)
        outs_b[m][...] = sum_b[pl.ds(at, outs_b[m].shape[0]), :].astype(outs_b[m].dtype)


def add_split(starts, part_a, part_b):
    columns = part_a[0].shape[1]
    outs = []
    for part in (part_a, part_b):
        height = part[0].shape[0] // 4
        outs += [jax.ShapeDtypeStruct((height, columns), F32 if m == 0 else BF16) for m in range(4)]
    return pl.pallas_call(
        add_split_kernel,
        out_shape=tuple(outs),
        in_specs=[SMEM] + [VMEM] * 8,
        out_specs=(VMEM,) * 8,
        scratch_shapes=[pltpu.VMEM(part_a[0].shape, F32), pltpu.VMEM(part_b[0].shape, F32)],
        compiler_params=PARAMS,
        name="add_split",
    )(starts, *part_a, *part_b)


def add_kernel(keep_a, a1, a2, a3, keep_b, b1, b2, b3, out_a, out_b):
    total = (keep_a[...] + a1[...].astype(F32)) + (a2[...].astype(F32) + a3[...].astype(F32))
    out_a[...] = total.astype(BF16)
    total = (keep_b[...] + b1[...].astype(F32)) + (b2[...].astype(F32) + b3[...].astype(F32))
    out_b[...] = total.astype(BF16)


def add_last(part_a, part_b):
    return pl.pallas_call(
        add_kernel,
        out_shape=tuple(jax.ShapeDtypeStruct(p[0].shape, BF16) for p in (part_a, part_b)),
        in_specs=[VMEM] * 8,
        out_specs=(VMEM,) * 2,
        compiler_params=PARAMS,
        name="add_last",
    )(*part_a, *part_b)


def join_kernel(starts, *refs):
    parts_a, parts_b, out_a, out_b, all_a, all_b = refs[:4], refs[4:8], *refs[8:]
    for m in range(4):
        height = parts_a[m].shape[0]
        all_a[pl.ds(pl.multiple_of(starts[m], 8), height), :] = parts_a[m][...].astype(F32)
        height = parts_b[m].shape[0]
        all_b[pl.ds(pl.multiple_of(starts[4 + m], 8), height), :] = parts_b[m][...].astype(F32)
    out_a[...] = all_a[...].astype(BF16)
    out_b[...] = all_b[...].astype(BF16)


def join(starts, parts_a, parts_b):
    columns = parts_a[0].shape[1]
    shapes = [(4 * parts_a[0].shape[0], columns), (4 * parts_b[0].shape[0], columns)]
    return pl.pallas_call(
        join_kernel,
        out_shape=tuple(jax.ShapeDtypeStruct(s, BF16) for s in shapes),
        in_specs=[SMEM] + [VMEM] * 8,
        out_specs=(VMEM,) * 2,
        scratch_shapes=[pltpu.VMEM(s, F32) for s in shapes],
        compiler_params=PARAMS,
        name="join",
    )(starts, *parts_a, *parts_b)


def join_all_kernel(starts, *refs):
    out = refs[8]
    for m in range(8):
        height = refs[m].shape[0]
        out[pl.ds(pl.multiple_of(starts[m], 32), height), :] = refs[m][...]


def join_all(starts, parts):
    columns = parts[0].shape[1]
    return pl.pallas_call(
        join_all_kernel,
        out_shape=jax.ShapeDtypeStruct((sum(p.shape[0] for p in parts), columns), BF16),
        in_specs=[SMEM] + [VMEM] * 8,
        out_specs=VMEM,
        compiler_params=PARAMS,
        name="join_all",
    )(starts, *parts)


def starts_of(index, height, first=0):
    return [first + (index ^ m) * height for m in range(4)]


def body(img_emb, txt_emb, img_proj, txt_proj, log_scale, bias):
    size = lax.axis_size("dp")
    rows, columns = img_emb.shape
    scale = jnp.exp(log_scale)
    here = lax.axis_index("dp").astype(jnp.int32)
    role = here % 2
    image_side = role == 0
    in_plane = (here // 2) % 4
    in_line = (here // 8) % 4

    mine, met = first_units(role.reshape(1), img_emb, txt_emb, img_proj, txt_proj)

    still, ahead, behind = (lambda core: 0), (lambda core: 1), (lambda core: -1)
    far = lambda core: 2 if core == 1 else -2
    far_other = hop(met, size, far, False)
    far_own = hop(mine, size, far, True)
    before_one = hop(met, size, ahead, False)
    before_two = hop(mine, size, ahead, True)
    met_other = hop(mine, size, still, True)

    late_img, late_txt, met_other = lax.optimization_barrier((img_emb, txt_emb, met_other))
    own_emb = jnp.where(image_side, late_img, late_txt)
    other_emb = hop(jnp.where(image_side, late_txt, late_img), size, still, True)
    emb = jnp.concatenate([own_emb, other_emb], axis=0)
    weight = jnp.where(image_side, img_proj, txt_proj)
    raw = jnp.dot(emb, weight, preferred_element_type=F32)
    norm = jnp.sqrt(jnp.sum(raw * raw, axis=1, keepdims=True) + 1e-06)
    unit = raw / norm
    z = unit.astype(BF16)
    emb_t = lax.optimization_barrier(emb).T

    grad = call_tiles(own_chip_kernel, scale, bias, z, (met, met_other), (), "own_chip")
    before_one, before_two, far_own, far_other, met, mine = lax.optimization_barrier(
        (before_one, before_two, far_own, far_other, met, mine)
    )
    after_one = hop(met, size, behind, False)
    after_two = hop(mine, size, behind, True)
    grad = call_tiles(
        first_phase_kernel,
        scale,
        bias,
        z,
        (before_one, before_two, far_own, far_other),
        (grad,),
        "first_phase",
    )

    sixth = columns // 6
    starts = jnp.stack(starts_of(in_plane, sixth) + starts_of(in_line, sixth // 2, 4 * sixth))
    du, *pieces = last_phase(
        starts, scale, bias, z, after_one, after_two, grad, unit, norm, emb_t
    )
    plane_masks, line_masks = (2, 4, 6), (8, 16, 24)

    def exchange(sends, masks):
        return [swap(s, size, m) for s, m in zip(sends, masks)]

    part_b = [pieces[4], *exchange(pieces[5:], line_masks)]
    part_a = [pieces[0], *exchange(pieces[1:4], plane_masks)]
    d_emb, d_emb_send = rows_back(du, weight)
    part_a, part_b, d_emb, d_emb_send = lax.optimization_barrier((part_a, part_b, d_emb, d_emb_send))
    inner = jnp.stack(starts_of(in_line, sixth // 4) + starts_of(in_plane, sixth // 8))
    pieces = add_split(inner, part_a, part_b)
    part_a = [pieces[0], *exchange(pieces[1:4], line_masks)]
    part_b = [pieces[4], *exchange(pieces[5:], plane_masks)]
    d_emb_other = swap(d_emb_send, size, 1)
    d_img_emb = jnp.where(image_side, d_emb, d_emb_other)
    d_txt_emb = jnp.where(image_side, d_emb_other, d_emb)
    part_a, part_b, d_img_emb, d_txt_emb = lax.optimization_barrier(
        (part_a, part_b, d_img_emb, d_txt_emb)
    )
    shard_a, shard_b = add_last(part_a, part_b)
    if size > 32:
        groups = [[i for i in range(size) if i % 32 == k] for k in range(32)]
        shard_a, shard_b = lax.psum((shard_a, shard_b), "dp", axis_index_groups=groups)
    parts_a = [shard_a, *exchange([shard_a] * 3, line_masks)]
    parts_b = [shard_b, *exchange([shard_b] * 3, plane_masks)]
    piece_a, piece_b = join(inner, parts_a, parts_b)
    parts = [piece_a, *exchange([piece_a] * 3, plane_masks)]
    parts += [piece_b, *exchange([piece_b] * 3, line_masks)]
    d_weight = join_all(starts, parts)
    d_weight_other = swap(d_weight, size, 1)
    d_img_proj = jnp.where(image_side, d_weight, d_weight_other).astype(F32)
    d_txt_proj = jnp.where(image_side, d_weight_other, d_weight).astype(F32)
    return (d_img_emb, d_txt_emb, d_img_proj, d_txt_proj)


def solution(mesh):
    return jax.shard_map(
        body,
        mesh=mesh,
        in_specs=(P("dp", None), P("dp", None), P(), P(), P(), P()),
        out_specs=(P("dp", None), P("dp", None), P(), P()),
        check_vma=False,
    )
```

```python
import functools

import jax
import jax.numpy as jnp
from jax import lax
from jax.experimental import pallas as pl
from jax.experimental.pallas import tpu as pltpu
from jax.sharding import PartitionSpec as P

REACH = 3
BF16, F32 = jnp.bfloat16, jnp.float32
TILE = 512
VMEM = pl.BlockSpec(memory_space=pltpu.VMEM)
SMEM = pl.BlockSpec(memory_space=pltpu.SMEM)
HBM = pl.BlockSpec(memory_space=pltpu.HBM)


def params(mib):
    return pltpu.CompilerParams(vmem_limit_bytes=mib * 1024 * 1024)


def dot_t(left, right):
    return lax.dot_general(left, right, (((1,), (1,)), ((), ())), preferred_element_type=F32)


def dot(left, right):
    return lax.dot_general(left, right, (((1,), (0,)), ((), ())), preferred_element_type=F32)


def shift(value, size, chips):
    pairs = []
    for i in range(size):
        chip, core = i // 2, i % 2
        pairs.append((i, 2 * ((chip + chips(chip, core)) % (size // 2)) + core))
    return lax.ppermute(value, "dp", pairs)


def swap(value, size, mask):
    return lax.ppermute(value, "dp", [(i, i ^ mask) for i in range(size)])


def first_kernel(role, img_emb, txt_emb, img_proj, txt_proj, mine, met, emb_v, proj_v, sems):
    copies = [
        pltpu.make_async_copy(src, dst, sems.at[at])
        for at, (src, dst) in enumerate(
            (
                (img_proj, proj_v.at[0]),
                (img_emb, emb_v.at[0]),
                (txt_proj, proj_v.at[1]),
                (txt_emb, emb_v.at[1]),
            )
        )
    ]
    for copy in copies:
        copy.start()
    for side in range(2):
        copies[2 * side].wait()
        copies[2 * side + 1].wait()
        raw = dot(emb_v[side], proj_v[side])
        z = (raw * lax.rsqrt(jnp.sum(raw * raw, axis=1, keepdims=True) + 1e-06)).astype(BF16)

        @pl.when(role[0] == side)
        def _():
            mine[...] = z

        @pl.when(role[0] != side)
        def _():
            met[...] = z


def first_units(role, img_emb, txt_emb, img_proj, txt_proj):
    out = jax.ShapeDtypeStruct(img_emb.shape, BF16)
    return pl.pallas_call(
        first_kernel,
        out_shape=(out, out),
        in_specs=[SMEM] + [HBM] * 4,
        out_specs=(VMEM, VMEM),
        scratch_shapes=[
            pltpu.VMEM((2, *img_emb.shape), BF16),
            pltpu.VMEM((2, *img_proj.shape), BF16),
            pltpu.SemaphoreType.DMA((4,)),
        ],
        compiler_params=params(60),
        name="first_units",
    )(role, img_emb, txt_emb, img_proj, txt_proj)


def second_kernel(role, *refs):
    sides, (unit, inverse, z, weight, emb_t, emb_v, sems) = (refs[:3], refs[3:6]), refs[6:]
    rows = emb_v.shape[1]
    for side in range(2):

        @pl.when(role[0] == side)
        def _():
            copies = [
                pltpu.make_async_copy(src, dst, sems.at[at])
                for at, (src, dst) in enumerate(
                    zip(sides[side], (weight, emb_v.at[0], emb_v.at[1]))
                )
            ]
            for copy in copies:
                copy.start()
            for copy in copies:
                copy.wait()

    for half in range(2):
        here = slice(half * rows, (half + 1) * rows)
        raw = dot(emb_v[half], weight[...])
        scale = lax.rsqrt(jnp.sum(raw * raw, axis=1, keepdims=True) + 1e-06)
        inverse[here, :] = scale
        units = raw * scale
        unit[here, :] = units
        z[here, :] = units.astype(BF16)
        emb_t[:, here] = emb_v[half].T


def second_units(role, img_emb, txt_emb, img_other, txt_other, img_proj, txt_proj):
    rows, columns = img_emb.shape
    return pl.pallas_call(
        second_kernel,
        out_shape=(
            jax.ShapeDtypeStruct((2 * rows, columns), F32),
            jax.ShapeDtypeStruct((2 * rows, 1), F32),
            jax.ShapeDtypeStruct((2 * rows, columns), BF16),
            jax.ShapeDtypeStruct(img_proj.shape, BF16),
            jax.ShapeDtypeStruct((columns, 2 * rows), BF16),
        ),
        in_specs=[SMEM] + [HBM] * 6,
        out_specs=(VMEM,) * 5,
        scratch_shapes=[
            pltpu.VMEM((2, rows, columns), BF16),
            pltpu.SemaphoreType.DMA((3,)),
        ],
        compiler_params=params(44),
        name="second_units",
    )(role, img_proj, img_emb, img_other, txt_proj, txt_emb, txt_other)


def pair_term(z, block, scale, bias, diagonal):
    half = dot_t(z, block) * (0.5 * scale) + 0.5 * bias
    coef = 0.5 * jnp.tanh(half) + 0.5
    if diagonal is not None:
        row_at = lax.broadcasted_iota(jnp.int32, coef.shape, 0) + diagonal
        col_at = lax.broadcasted_iota(jnp.int32, coef.shape, 1)
        coef = jnp.where(row_at == col_at, coef - 1.0, coef)
    return dot(coef.astype(BF16), block)


def own_chip_kernel(scale, bias, z, met, met_other, grad):
    step = pl.program_id(0)
    per_block = met.shape[0] // TILE
    here = step * TILE
    near = pair_term(z[...], met[...], scale[0], bias[0], here)
    other = pair_term(z[...], met_other[...], scale[0], bias[0], here - per_block * TILE)
    grad[...] = near + other


def first_phase_kernel(scale, bias, z, one, two, far_own, far_other, grad_in, grad):
    step = pl.program_id(0)
    per_block = one.shape[0] // TILE
    total = grad_in[...] + pair_term(z[...], one[...], scale[0], bias[0], None)
    total = total + pair_term(z[...], two[...], scale[0], bias[0], None)

    @pl.when(step < per_block)
    def _():
        grad[...] = total + pair_term(z[...], far_own[...], scale[0], bias[0], None)

    @pl.when(step >= per_block)
    def _():
        grad[...] = total + pair_term(z[...], far_other[...], scale[0], bias[0], None)


def row_tiles(columns):
    return pl.BlockSpec((TILE, columns), lambda i: (i, 0))


def whole(array):
    return pl.BlockSpec(
        array.shape, lambda i: (0,) * len(array.shape), pipeline_mode=pl.Buffered(1)
    )


def call_tiles(kernel, scale, bias, z, blocks, grads, name, mib):
    rows, columns = z.shape
    return pl.pallas_call(
        kernel,
        grid=(rows // TILE,),
        out_shape=jax.ShapeDtypeStruct((rows, columns), F32),
        in_specs=[SMEM, SMEM, row_tiles(columns)]
        + [whole(b) for b in blocks]
        + [row_tiles(columns)] * len(grads),
        out_specs=row_tiles(columns),
        compiler_params=params(mib),
        name=name,
    )(scale, bias, z, *blocks, *grads)


def last_phase_kernel(
    starts, scale, bias, z, one, two, grad_in, unit, inverse, emb_t, du, *rest
):
    pieces, (du_all, emb_v, sem) = rest[:8], rest[8:]
    step = pl.program_id(0)
    fetch = pltpu.make_async_copy(emb_t, emb_v, sem)

    @pl.when(step == 0)
    def _():
        fetch.start()

    grad = grad_in[...] + pair_term(z[...], one[...], scale[0], bias[0], None)
    grad = scale[0] * (grad + pair_term(z[...], two[...], scale[0], bias[0], None))
    units = unit[...]
    inner = jnp.sum(units * grad, axis=1, keepdims=True)
    rounded = ((grad - units * inner) * inverse[...]).astype(BF16)
    du[...] = rounded
    du_all[pl.ds(pl.multiple_of(step * TILE, TILE), TILE), :] = rounded

    @pl.when(step == pl.num_programs(0) - 1)
    def _():
        fetch.wait()
        for m, out in enumerate(pieces):
            height = out.shape[0]
            part = emb_v[pl.ds(pl.multiple_of(starts[m], 32), height), :]
            out[...] = dot(part, du_all[...]).astype(out.dtype)


def last_phase(starts, scale, bias, z, one, two, grad, unit, inverse, emb_t):
    rows, columns = z.shape
    heights = [columns // 6] * 4 + [columns // 12] * 4
    pieces = [
        jax.ShapeDtypeStruct((h, columns), F32 if m % 4 == 0 else BF16)
        for m, h in enumerate(heights)
    ]
    return pl.pallas_call(
        last_phase_kernel,
        grid=(rows // TILE,),
        out_shape=(jax.ShapeDtypeStruct((rows, columns), BF16), *pieces),
        in_specs=[
            SMEM,
            SMEM,
            SMEM,
            row_tiles(columns),
            whole(one),
            whole(two),
            row_tiles(columns),
            row_tiles(columns),
            row_tiles(1),
            HBM,
        ],
        out_specs=(row_tiles(columns), *[whole(p) for p in pieces]),
        scratch_shapes=[
            pltpu.VMEM((rows, columns), BF16),
            pltpu.VMEM(emb_t.shape, BF16),
            pltpu.SemaphoreType.DMA,
        ],
        compiler_params=params(44),
        name="last_phase",
    )(starts, scale, bias, z, one, two, grad, unit, inverse, emb_t)


def rows_back_kernel(du, weight, own, other):
    step = pl.program_id(0)
    back = dot_t(du[...], weight[...]).astype(BF16)

    @pl.when(step < pl.num_programs(0) // 2)
    def _():
        own[...] = back

    @pl.when(step >= pl.num_programs(0) // 2)
    def _():
        other[...] = back


def rows_back(du, weight):
    rows, columns = du.shape
    half = rows // 2 // TILE
    out = jax.ShapeDtypeStruct((rows // 2, columns), BF16)
    return pl.pallas_call(
        rows_back_kernel,
        grid=(rows // TILE,),
        out_shape=(out, out),
        in_specs=[row_tiles(columns), whole(weight)],
        out_specs=(
            pl.BlockSpec((TILE, columns), lambda i: (jnp.minimum(i, half - 1), 0)),
            pl.BlockSpec((TILE, columns), lambda i: (jnp.maximum(i - half, 0), 0)),
        ),
        compiler_params=params(14),
        name="rows_back",
    )(du, weight)


def add_split_kernel(starts, keep_a, a1, a2, a3, keep_b, b1, b2, b3, *rest):
    outs_a, outs_b, sum_a, sum_b = rest[:4], rest[4:8], rest[8], rest[9]
    sum_a[...] = (keep_a[...] + a1[...].astype(F32)) + (a2[...].astype(F32) + a3[...].astype(F32))
    sum_b[...] = (keep_b[...] + b1[...].astype(F32)) + (b2[...].astype(F32) + b3[...].astype(F32))
    for m in range(4):
        at = pl.multiple_of(starts[m], 16)
        outs_a[m][...] = sum_a[pl.ds(at, outs_a[m].shape[0]), :].astype(outs_a[m].dtype)
        at = pl.multiple_of(starts[4 + m], 8)
        outs_b[m][...] = sum_b[pl.ds(at, outs_b[m].shape[0]), :].astype(outs_b[m].dtype)


def add_split(starts, part_a, part_b):
    columns = part_a[0].shape[1]
    outs = []
    for part in (part_a, part_b):
        height = part[0].shape[0] // 4
        outs += [jax.ShapeDtypeStruct((height, columns), F32 if m == 0 else BF16) for m in range(4)]
    return pl.pallas_call(
        add_split_kernel,
        out_shape=tuple(outs),
        in_specs=[SMEM] + [VMEM] * 8,
        out_specs=(VMEM,) * 8,
        scratch_shapes=[pltpu.VMEM(part_a[0].shape, F32), pltpu.VMEM(part_b[0].shape, F32)],
        compiler_params=params(12),
        name="add_split",
    )(starts, *part_a, *part_b)


def add_kernel(keep_a, a1, a2, a3, keep_b, b1, b2, b3, out_a, out_b):
    total = (keep_a[...] + a1[...].astype(F32)) + (a2[...].astype(F32) + a3[...].astype(F32))
    out_a[...] = total.astype(BF16)
    total = (keep_b[...] + b1[...].astype(F32)) + (b2[...].astype(F32) + b3[...].astype(F32))
    out_b[...] = total.astype(BF16)


def add_last(part_a, part_b):
    return pl.pallas_call(
        add_kernel,
        out_shape=tuple(jax.ShapeDtypeStruct(p[0].shape, BF16) for p in (part_a, part_b)),
        in_specs=[VMEM] * 8,
        out_specs=(VMEM,) * 2,
        compiler_params=params(12),
        name="add_last",
    )(*part_a, *part_b)


def join_kernel(starts, *refs):
    parts_a, parts_b, out_a, out_b, all_a, all_b = refs[:4], refs[4:8], *refs[8:]
    for m in range(4):
        height = parts_a[m].shape[0]
        all_a[pl.ds(pl.multiple_of(starts[m], 8), height), :] = parts_a[m][...].astype(F32)
        height = parts_b[m].shape[0]
        all_b[pl.ds(pl.multiple_of(starts[4 + m], 8), height), :] = parts_b[m][...].astype(F32)
    out_a[...] = all_a[...].astype(BF16)
    out_b[...] = all_b[...].astype(BF16)


def join(starts, parts_a, parts_b):
    columns = parts_a[0].shape[1]
    shapes = [(4 * parts_a[0].shape[0], columns), (4 * parts_b[0].shape[0], columns)]
    return pl.pallas_call(
        join_kernel,
        out_shape=tuple(jax.ShapeDtypeStruct(s, BF16) for s in shapes),
        in_specs=[SMEM] + [VMEM] * 8,
        out_specs=(VMEM,) * 2,
        scratch_shapes=[pltpu.VMEM(s, F32) for s in shapes],
        compiler_params=params(12),
        name="join",
    )(starts, *parts_a, *parts_b)


def join_all_kernel(starts, *refs):
    out = refs[8]
    for m in range(8):
        height = refs[m].shape[0]
        out[pl.ds(pl.multiple_of(starts[m], 32), height), :] = refs[m][...]


def join_all(starts, parts):
    columns = parts[0].shape[1]
    return pl.pallas_call(
        join_all_kernel,
        out_shape=jax.ShapeDtypeStruct((sum(p.shape[0] for p in parts), columns), BF16),
        in_specs=[SMEM] + [VMEM] * 8,
        out_specs=VMEM,
        compiler_params=params(12),
        name="join_all",
    )(starts, *parts)


def starts_of(index, height, first=0):
    return [first + (index ^ m) * height for m in range(4)]


def body(img_emb, txt_emb, img_proj, txt_proj, log_scale, bias):
    size = lax.axis_size("dp")
    rows, columns = img_emb.shape
    scale = jnp.exp(log_scale)
    here = lax.axis_index("dp").astype(jnp.int32)
    role = here % 2
    image_side = role == 0
    in_plane = (here // 2) % 4
    in_line = (here // 8) % 4

    img_other, txt_other = swap(img_emb, size, 1), swap(txt_emb, size, 1)
    mine, met = first_units(role.reshape(1), img_emb, txt_emb, img_proj, txt_proj)

    pair = lambda value: swap(value, size, 2)
    met_other = swap(mine, size, 1)
    pair_met = pair(met)
    far_other = shift(met, size, lambda chip, core: 2 if core else -2)
    pair_other = pair(met_other)
    far_own = shift(met_other, size, lambda chip, core: -2 if core else 2)

    unit, inverse, z, weight, emb_t = second_units(
        role.reshape(1), img_emb, txt_emb, img_other, txt_other, img_proj, txt_proj
    )
    grad = call_tiles(own_chip_kernel, scale, bias, z, (met, met_other), (), "own_chip", 16)
    pair_met, pair_other, far_own, far_other, grad, emb_t = lax.optimization_barrier(
        (pair_met, pair_other, far_own, far_other, grad, emb_t)
    )
    even_chip_is_core = (here // 2) % 2 == role
    relay_far = pair(jnp.where(even_chip_is_core, far_other, far_own))
    relay_pair = shift(
        jnp.where(even_chip_is_core, pair_met, pair_other),
        size,
        lambda chip, core: -2 if chip % 2 else 2,
    )
    grad = call_tiles(
        first_phase_kernel,
        scale,
        bias,
        z,
        (pair_met, pair_other, far_own, far_other),
        (grad,),
        "first_phase",
        24,
    )

    sixth = columns // 6
    starts = jnp.stack(starts_of(in_plane, sixth) + starts_of(in_line, sixth // 2, 4 * sixth))
    du, *pieces = last_phase(
        starts, scale, bias, z, relay_far, relay_pair, grad, unit, inverse, emb_t
    )
    plane_masks, line_masks = (2, 4, 6), (8, 16, 24)

    def exchange(sends, masks):
        return [swap(s, size, m) for s, m in zip(sends, masks)]

    part_b = [pieces[4], *exchange(pieces[5:], line_masks)]
    part_a = [pieces[0], *exchange(pieces[1:4], plane_masks)]
    d_emb, d_emb_send = rows_back(du, weight)
    part_a, part_b, d_emb, d_emb_send = lax.optimization_barrier((part_a, part_b, d_emb, d_emb_send))
    inner = jnp.stack(starts_of(in_line, sixth // 4) + starts_of(in_plane, sixth // 8))
    pieces = add_split(inner, part_a, part_b)
    part_a = [pieces[0], *exchange(pieces[1:4], line_masks)]
    part_b = [pieces[4], *exchange(pieces[5:], plane_masks)]
    d_emb_other = swap(d_emb_send, size, 1)
    d_img_emb = jnp.where(image_side, d_emb, d_emb_other)
    d_txt_emb = jnp.where(image_side, d_emb_other, d_emb)
    part_a, part_b, d_img_emb, d_txt_emb = lax.optimization_barrier(
        (part_a, part_b, d_img_emb, d_txt_emb)
    )
    shard_a, shard_b = add_last(part_a, part_b)
    if size > 32:
        groups = [[i for i in range(size) if i % 32 == k] for k in range(32)]
        shard_a, shard_b = lax.psum((shard_a, shard_b), "dp", axis_index_groups=groups)
    parts_a = [shard_a, *exchange([shard_a] * 3, line_masks)]
    parts_b = [shard_b, *exchange([shard_b] * 3, plane_masks)]
    piece_a, piece_b = join(inner, parts_a, parts_b)
    parts = [piece_a, *exchange([piece_a] * 3, plane_masks)]
    parts += [piece_b, *exchange([piece_b] * 3, line_masks)]
    d_weight = join_all(starts, parts)
    d_weight_other = swap(d_weight, size, 1)
    d_img_proj = jnp.where(image_side, d_weight, d_weight_other).astype(F32)
    d_txt_proj = jnp.where(image_side, d_weight_other, d_weight).astype(F32)
    return (d_img_emb, d_txt_emb, d_img_proj, d_txt_proj)


def solution(mesh):
    return jax.shard_map(
        body,
        mesh=mesh,
        in_specs=(P("dp", None), P("dp", None), P(), P(), P(), P()),
        out_specs=(P("dp", None), P("dp", None), P(), P()),
        check_vma=False,
    )
```

```python
import functools

import jax
import jax.numpy as jnp
from jax import lax
from jax.experimental import pallas as pl
from jax.experimental.pallas import tpu as pltpu
from jax.sharding import PartitionSpec as P

REACH = 3
BF16, F32 = jnp.bfloat16, jnp.float32
TILE = 512
CHUNKS = 3
SIDE, IN_PLANE, IN_LINE, RELAY = range(4)
VMEM = pl.BlockSpec(memory_space=pltpu.VMEM)
SMEM = pl.BlockSpec(memory_space=pltpu.SMEM)
HBM = pl.BlockSpec(memory_space=pltpu.HBM)
ANY = pl.BlockSpec(memory_space=pl.ANY)


def params(mib):
    return pltpu.CompilerParams(vmem_limit_bytes=mib * 1024 * 1024)


def dot_t(left, right):
    return lax.dot_general(left, right, (((1,), (1,)), ((), ())), preferred_element_type=F32)


def dot(left, right):
    return lax.dot_general(left, right, (((1,), (0,)), ((), ())), preferred_element_type=F32)


def shift(value, size, chips):
    pairs = []
    for i in range(size):
        chip, core = i // 2, i % 2
        pairs.append((i, 2 * ((chip + chips(chip, core)) % (size // 2)) + core))
    return lax.ppermute(value, "dp", pairs)


def swap(value, size, mask):
    return lax.ppermute(value, "dp", [(i, i ^ mask) for i in range(size)])


def first_kernel(place, img_emb, txt_emb, img_proj, txt_proj, mine, met, emb_v, proj_v, raw, sems):
    chunk = raw.shape[1] // CHUNKS
    parts = [slice(c * chunk, (c + 1) * chunk) for c in range(CHUNKS)]
    copies = []
    for side, (emb, proj) in enumerate(((img_emb, img_proj), (txt_emb, txt_proj))):
        pairs = [(emb, emb_v.at[side])]
        pairs += [(proj.at[:, part], proj_v.at[side, :, part]) for part in parts]
        for src, dst in pairs:
            copies.append(pltpu.make_async_copy(src, dst, sems.at[len(copies)]))
    for copy in copies:
        copy.start()
    for side in range(2):
        emb_copy, *proj_copies = copies[side * (CHUNKS + 1) : (side + 1) * (CHUNKS + 1)]
        emb_copy.wait()
        total = 1e-06
        for part, copy in zip(parts, proj_copies):
            copy.wait()
            piece = dot(emb_v[side], proj_v[side, :, part])
            raw[:, part] = piece
            total = total + jnp.sum(piece * piece, axis=1, keepdims=True)
        scale = lax.rsqrt(total)

        @pl.when(place[SIDE] == side)
        def _():
            mine[...] = (raw[...] * scale).astype(BF16)

        @pl.when(place[SIDE] != side)
        def _():
            met[...] = (raw[...] * scale).astype(BF16)


def first_units(place, img_emb, txt_emb, img_proj, txt_proj):
    out = jax.ShapeDtypeStruct(img_emb.shape, BF16)
    return pl.pallas_call(
        first_kernel,
        out_shape=(out, out),
        in_specs=[SMEM] + [HBM] * 4,
        out_specs=(VMEM, VMEM),
        scratch_shapes=[
            pltpu.VMEM((2, *img_emb.shape), BF16),
            pltpu.VMEM((2, *img_proj.shape), BF16),
            pltpu.VMEM(img_emb.shape, F32),
            pltpu.SemaphoreType.DMA((2 * (CHUNKS + 1),)),
        ],
        compiler_params=params(60),
        name="first_units",
    )(place, img_emb, txt_emb, img_proj, txt_proj)


def second_kernel(place, *refs):
    sides, (unit, inverse, z, weight, emb_t, emb_v, sems) = (refs[:3], refs[3:6]), refs[6:]
    rows = emb_v.shape[1]
    for side in range(2):

        @pl.when(place[SIDE] == side)
        def _():
            copies = [
                pltpu.make_async_copy(src, dst, sems.at[at])
                for at, (src, dst) in enumerate(
                    zip(sides[side], (weight, emb_v.at[0], emb_v.at[1]))
                )
            ]
            for copy in copies:
                copy.start()
            for copy in copies:
                copy.wait()

    for half in range(2):
        here = slice(half * rows, (half + 1) * rows)
        raw = dot(emb_v[half], weight[...])
        scale = lax.rsqrt(jnp.sum(raw * raw, axis=1, keepdims=True) + 1e-06)
        inverse[here, :] = scale
        units = raw * scale
        unit[here, :] = units
        z[here, :] = units.astype(BF16)
        emb_t[:, here] = emb_v[half].T


def second_units(place, img_emb, txt_emb, img_other, txt_other, img_proj, txt_proj):
    rows, columns = img_emb.shape
    return pl.pallas_call(
        second_kernel,
        out_shape=(
            jax.ShapeDtypeStruct((2 * rows, columns), F32),
            jax.ShapeDtypeStruct((2 * rows, 1), F32),
            jax.ShapeDtypeStruct((2 * rows, columns), BF16),
            jax.ShapeDtypeStruct(img_proj.shape, BF16),
            jax.ShapeDtypeStruct((columns, 2 * rows), BF16),
        ),
        in_specs=[SMEM] + [HBM] * 6,
        out_specs=(VMEM,) * 5,
        scratch_shapes=[
            pltpu.VMEM((2, rows, columns), BF16),
            pltpu.SemaphoreType.DMA((3,)),
        ],
        compiler_params=params(18),
        name="second_units",
    )(place, img_proj, img_emb, img_other, txt_proj, txt_emb, txt_other)


def piece_at(digit, m, height, first=0):
    return pl.ds(pl.multiple_of(first + (digit ^ m) * height, 8), height)


def pick_kernel(at, place, *refs):
    sources, outs, sems = (refs[:2], refs[2:4]), refs[4:6], refs[6]
    for flag in range(2):

        @pl.when(place[at] == flag)
        def _():
            copies = [
                pltpu.make_async_copy(pair[flag], out, sems.at[k])
                for k, (pair, out) in enumerate(zip(sources, outs))
            ]
            for copy in copies:
                copy.start()
            for copy in copies:
                copy.wait()


def pick(place, at, first, second, name):
    return pl.pallas_call(
        functools.partial(pick_kernel, at),
        out_shape=tuple(jax.ShapeDtypeStruct(p[0].shape, p[0].dtype) for p in (first, second)),
        in_specs=[SMEM] + [ANY] * 4,
        out_specs=(ANY, ANY),
        scratch_shapes=[pltpu.SemaphoreType.DMA((2,))],
        compiler_params=params(1),
        name=name,
    )(place, *first, *second)


def pair_term(z, block, scale, bias, diagonal):
    half = dot_t(z, block) * (0.5 * scale) + 0.5 * bias
    coef = 0.5 * jnp.tanh(half) + 0.5
    if diagonal is not None:
        row_at = lax.broadcasted_iota(jnp.int32, coef.shape, 0) + diagonal
        col_at = lax.broadcasted_iota(jnp.int32, coef.shape, 1)
        coef = jnp.where(row_at == col_at, coef - 1.0, coef)
    return dot(coef.astype(BF16), block)


def own_chip_kernel(scale, bias, z, met, met_other, grad):
    step = pl.program_id(0)
    per_block = met.shape[0] // TILE
    here = step * TILE
    near = pair_term(z[...], met[...], scale[0], bias[0], here)
    other = pair_term(z[...], met_other[...], scale[0], bias[0], here - per_block * TILE)
    grad[...] = near + other


def first_phase_kernel(scale, bias, z, one, two, far_own, far_other, grad_in, grad):
    step = pl.program_id(0)
    per_block = one.shape[0] // TILE
    total = grad_in[...] + pair_term(z[...], one[...], scale[0], bias[0], None)
    total = total + pair_term(z[...], two[...], scale[0], bias[0], None)

    @pl.when(step < per_block)
    def _():
        grad[...] = total + pair_term(z[...], far_own[...], scale[0], bias[0], None)

    @pl.when(step >= per_block)
    def _():
        grad[...] = total + pair_term(z[...], far_other[...], scale[0], bias[0], None)


def row_tiles(columns):
    return pl.BlockSpec((TILE, columns), lambda i: (i, 0))


def whole(array):
    return pl.BlockSpec(
        array.shape, lambda i: (0,) * len(array.shape), pipeline_mode=pl.Buffered(1)
    )


def call_tiles(kernel, scale, bias, z, blocks, grads, name, mib):
    rows, columns = z.shape
    return pl.pallas_call(
        kernel,
        grid=(rows // TILE,),
        out_shape=jax.ShapeDtypeStruct((rows, columns), F32),
        in_specs=[SMEM, SMEM, row_tiles(columns)]
        + [whole(b) for b in blocks]
        + [row_tiles(columns)] * len(grads),
        out_specs=row_tiles(columns),
        compiler_params=params(mib),
        name=name,
    )(scale, bias, z, *blocks, *grads)


def last_phase_kernel(
    place, scale, bias, z, one, two, grad_in, unit, inverse, emb_t, du, *rest
):
    pieces, (du_all, emb_v, sem) = rest[:8], rest[8:]
    step = pl.program_id(0)
    fetch = pltpu.make_async_copy(emb_t, emb_v, sem)

    @pl.when(step == 0)
    def _():
        fetch.start()

    grad = grad_in[...] + pair_term(z[...], one[...], scale[0], bias[0], None)
    grad = scale[0] * (grad + pair_term(z[...], two[...], scale[0], bias[0], None))
    units = unit[...]
    inner = jnp.sum(units * grad, axis=1, keepdims=True)
    rounded = ((grad - units * inner) * inverse[...]).astype(BF16)
    du[...] = rounded
    du_all[pl.ds(pl.multiple_of(step * TILE, TILE), TILE), :] = rounded

    @pl.when(step == pl.num_programs(0) - 1)
    def _():
        fetch.wait()
        first = 0
        for group, digit in ((pieces[:4], IN_PLANE), (pieces[4:], IN_LINE)):
            for m, out in enumerate(group):
                part = emb_v[piece_at(place[digit], m, out.shape[0], first), :]
                out[...] = dot(part, du_all[...]).astype(out.dtype)
            first += 4 * group[0].shape[0]


def last_phase(place, scale, bias, z, one, two, grad, unit, inverse, emb_t):
    rows, columns = z.shape
    heights = [columns // 6] * 4 + [columns // 12] * 4
    pieces = [
        jax.ShapeDtypeStruct((h, columns), F32 if m % 4 == 0 else BF16)
        for m, h in enumerate(heights)
    ]
    return pl.pallas_call(
        last_phase_kernel,
        grid=(rows // TILE,),
        out_shape=(jax.ShapeDtypeStruct((rows, columns), BF16), *pieces),
        in_specs=[
            SMEM,
            SMEM,
            SMEM,
            row_tiles(columns),
            whole(one),
            whole(two),
            row_tiles(columns),
            row_tiles(columns),
            row_tiles(1),
            HBM,
        ],
        out_specs=(row_tiles(columns), *[whole(p) for p in pieces]),
        scratch_shapes=[
            pltpu.VMEM((rows, columns), BF16),
            pltpu.VMEM(emb_t.shape, BF16),
            pltpu.SemaphoreType.DMA,
        ],
        compiler_params=params(28),
        name="last_phase",
    )(place, scale, bias, z, one, two, grad, unit, inverse, emb_t)


def rows_back_kernel(du, weight, own, other):
    step = pl.program_id(0)
    back = dot_t(du[...], weight[...]).astype(BF16)

    @pl.when(step < pl.num_programs(0) // 2)
    def _():
        own[...] = back

    @pl.when(step >= pl.num_programs(0) // 2)
    def _():
        other[...] = back


def rows_back(du, weight):
    rows, columns = du.shape
    half = rows // 2 // TILE
    out = jax.ShapeDtypeStruct((rows // 2, columns), BF16)
    return pl.pallas_call(
        rows_back_kernel,
        grid=(rows // TILE,),
        out_shape=(out, out),
        in_specs=[row_tiles(columns), whole(weight)],
        out_specs=(
            pl.BlockSpec((TILE, columns), lambda i: (jnp.minimum(i, half - 1), 0)),
            pl.BlockSpec((TILE, columns), lambda i: (jnp.maximum(i - half, 0), 0)),
        ),
        compiler_params=params(8),
        name="rows_back",
    )(du, weight)


def summed(keep, one, two, three):
    return (keep[...] + one[...].astype(F32)) + (two[...].astype(F32) + three[...].astype(F32))


def add_split_kernel(digits, place, *refs):
    for part, digit in enumerate(digits):
        outs, total = refs[8 + 4 * part : 12 + 4 * part], refs[16 + part]
        total[...] = summed(*refs[4 * part : 4 * part + 4])
        for m, out in enumerate(outs):
            out[...] = total[piece_at(place[digit], m, out.shape[0]), :].astype(out.dtype)


def add_split(place, digits, part_a, part_b):
    columns = part_a[0].shape[1]
    outs = []
    for part in (part_a, part_b):
        height = part[0].shape[0] // 4
        outs += [jax.ShapeDtypeStruct((height, columns), F32 if m == 0 else BF16) for m in range(4)]
    return pl.pallas_call(
        functools.partial(add_split_kernel, digits),
        out_shape=tuple(outs),
        in_specs=[SMEM] + [VMEM] * 8,
        out_specs=(VMEM,) * 8,
        scratch_shapes=[pltpu.VMEM(part_a[0].shape, F32), pltpu.VMEM(part_b[0].shape, F32)],
        compiler_params=params(6),
        name="add_split",
    )(place, *part_a, *part_b)


def add_kernel(*refs):
    refs[8][...] = summed(*refs[:4]).astype(BF16)
    refs[9][...] = summed(*refs[4:8]).astype(BF16)


def add_last(part_a, part_b):
    return pl.pallas_call(
        add_kernel,
        out_shape=tuple(jax.ShapeDtypeStruct(p[0].shape, BF16) for p in (part_a, part_b)),
        in_specs=[VMEM] * 8,
        out_specs=(VMEM,) * 2,
        compiler_params=params(3),
        name="add_last",
    )(*part_a, *part_b)


def join_kernel(digits, place, *refs):
    for part, digit in enumerate(digits):
        out, whole_part = refs[8 + part], refs[10 + part]
        for m, piece in enumerate(refs[4 * part : 4 * part + 4]):
            rows = piece_at(place[digit], m, piece.shape[0])
            whole_part[rows, :] = piece[...].astype(F32)
        out[...] = whole_part[...].astype(BF16)


def join(place, digits, parts_a, parts_b):
    columns = parts_a[0].shape[1]
    shapes = [(4 * parts_a[0].shape[0], columns), (4 * parts_b[0].shape[0], columns)]
    return pl.pallas_call(
        functools.partial(join_kernel, digits),
        out_shape=tuple(jax.ShapeDtypeStruct(s, BF16) for s in shapes),
        in_specs=[SMEM] + [VMEM] * 8,
        out_specs=(VMEM,) * 2,
        scratch_shapes=[pltpu.VMEM(s, F32) for s in shapes],
        compiler_params=params(4),
        name="join",
    )(place, *parts_a, *parts_b)


def join_all_kernel(digits, place, *refs):
    out, first = refs[8], 0
    for part, digit in enumerate(digits):
        for m, piece in enumerate(refs[4 * part : 4 * part + 4]):
            out[piece_at(place[digit], m, piece.shape[0], first), :] = piece[...]
        first += 4 * refs[4 * part].shape[0]


def join_all(place, digits, parts_a, parts_b):
    parts = [*parts_a, *parts_b]
    columns = parts[0].shape[1]
    return pl.pallas_call(
        functools.partial(join_all_kernel, digits),
        out_shape=jax.ShapeDtypeStruct((sum(p.shape[0] for p in parts), columns), BF16),
        in_specs=[SMEM] + [VMEM] * 8,
        out_specs=VMEM,
        compiler_params=params(3),
        name="join_all",
    )(place, *parts)


def widen_kernel(own, place, weight, *refs):
    img_out, txt_out, wide, sems = refs[-4:]
    height = weight.shape[0] // 4
    parts = [slice(k * height, (k + 1) * height) for k in range(4)]
    for side, out in enumerate((img_out, txt_out)):

        @pl.when((place[SIDE] == side) == own)
        def _():
            copies = [
                pltpu.make_async_copy(wide.at[part, :], out.at[part, :], sems.at[k])
                for k, part in enumerate(parts)
            ]
            for part, copy in zip(parts, copies):
                wide[part, :] = weight[part, :].astype(F32)
                copy.start()
            for copy in copies:
                copy.wait()


def widen(place, weight, outs):
    out = jax.ShapeDtypeStruct(weight.shape, F32)
    return pl.pallas_call(
        functools.partial(widen_kernel, not outs),
        out_shape=(out, out),
        in_specs=[SMEM, VMEM] + [ANY] * len(outs),
        out_specs=(ANY, ANY),
        scratch_shapes=[pltpu.VMEM(weight.shape, F32), pltpu.SemaphoreType.DMA((4,))],
        input_output_aliases={2: 0, 3: 1} if outs else {},
        compiler_params=params(12),
        name="widen_other" if outs else "widen_own",
    )(place, weight, *outs)


def body(img_emb, txt_emb, img_proj, txt_proj, log_scale, bias):
    size = lax.axis_size("dp")
    rows, columns = img_emb.shape
    scale = jnp.exp(log_scale)
    here = lax.axis_index("dp").astype(jnp.int32)
    side, chip = here % 2, here // 2
    place = jnp.stack([side, chip % 4, (chip // 4) % 4, (chip + side + 1) % 2])
    place, scale = lax.optimization_barrier((place, scale))

    img_other, txt_other = swap(img_emb, size, 1), swap(txt_emb, size, 1)
    mine, met = first_units(place, img_emb, txt_emb, img_proj, txt_proj)

    pair = lambda value: swap(value, size, 2)
    met_other = swap(mine, size, 1)
    pair_met = pair(met)
    far_other = shift(met, size, lambda chip, core: 2 if core else -2)
    pair_other = pair(met_other)
    far_own = shift(met_other, size, lambda chip, core: -2 if core else 2)

    unit, inverse, z, weight, emb_t = second_units(
        place, img_emb, txt_emb, img_other, txt_other, img_proj, txt_proj
    )
    grad = call_tiles(own_chip_kernel, scale, bias, z, (met, met_other), (), "own_chip", 8)
    pair_met, pair_other, far_own, far_other, grad, emb_t = lax.optimization_barrier(
        (pair_met, pair_other, far_own, far_other, grad, emb_t)
    )
    relay_far, relay_pair = pick(
        place, RELAY, (far_own, far_other), (pair_other, pair_met), "relay_pick"
    )
    relay_far = pair(relay_far)
    relay_pair = shift(relay_pair, size, lambda chip, core: -2 if chip % 2 else 2)
    grad = call_tiles(
        first_phase_kernel,
        scale,
        bias,
        z,
        (pair_met, pair_other, far_own, far_other),
        (grad,),
        "first_phase",
        12,
    )

    du, *pieces = last_phase(
        place, scale, bias, z, relay_far, relay_pair, grad, unit, inverse, emb_t
    )
    plane_masks, line_masks = (2, 4, 6), (8, 16, 24)

    def exchange(sends, masks):
        return [swap(s, size, m) for s, m in zip(sends, masks)]

    part_b = [pieces[4], *exchange(pieces[5:], line_masks)]
    part_a = [pieces[0], *exchange(pieces[1:4], plane_masks)]
    d_emb, d_emb_send = rows_back(du, weight)
    part_a, part_b, d_emb, d_emb_send = lax.optimization_barrier((part_a, part_b, d_emb, d_emb_send))
    pieces = add_split(place, (IN_LINE, IN_PLANE), part_a, part_b)
    part_a = [pieces[0], *exchange(pieces[1:4], line_masks)]
    part_b = [pieces[4], *exchange(pieces[5:], plane_masks)]
    d_emb_other = swap(d_emb_send, size, 1)
    d_img_emb, d_txt_emb = pick(
        place, SIDE, (d_emb, d_emb_other), (d_emb_other, d_emb), "rows_pick"
    )
    part_a, part_b, d_img_emb, d_txt_emb = lax.optimization_barrier(
        (part_a, part_b, d_img_emb, d_txt_emb)
    )
    shard_a, shard_b = add_last(part_a, part_b)
    if size > 32:
        groups = [[i for i in range(size) if i % 32 == k] for k in range(32)]
        shard_a, shard_b = lax.psum((shard_a, shard_b), "dp", axis_index_groups=groups)
    parts_a = [shard_a, *exchange([shard_a] * 3, line_masks)]
    parts_b = [shard_b, *exchange([shard_b] * 3, plane_masks)]
    piece_a, piece_b = join(place, (IN_LINE, IN_PLANE), parts_a, parts_b)
    parts_a = [piece_a, *exchange([piece_a] * 3, plane_masks)]
    parts_b = [piece_b, *exchange([piece_b] * 3, line_masks)]
    d_weight = join_all(place, (IN_PLANE, IN_LINE), parts_a, parts_b)
    d_weight_other = swap(d_weight, size, 1)
    outs = widen(place, d_weight, ())
    d_img_proj, d_txt_proj = widen(place, d_weight_other, outs)
    return (d_img_emb, d_txt_emb, d_img_proj, d_txt_proj)


def solution(mesh):
    return jax.shard_map(
        body,
        mesh=mesh,
        in_specs=(P("dp", None), P("dp", None), P(), P(), P(), P()),
        out_specs=(P("dp", None), P("dp", None), P(), P()),
        check_vma=False,
    )
```

```python
import functools

import jax
import jax.numpy as jnp
from jax import lax
from jax.experimental import pallas as pl
from jax.experimental.pallas import tpu as pltpu
from jax.sharding import PartitionSpec as P

REACH = 3
BF16, F32 = jnp.bfloat16, jnp.float32
TILE = 512
CHUNKS = 3
SIDE, IN_PLANE, IN_LINE, RELAY = range(4)
VMEM = pl.BlockSpec(memory_space=pltpu.VMEM)
SMEM = pl.BlockSpec(memory_space=pltpu.SMEM)
HBM = pl.BlockSpec(memory_space=pltpu.HBM)
ANY = pl.BlockSpec(memory_space=pl.ANY)


def params(mib):
    return pltpu.CompilerParams(vmem_limit_bytes=mib * 1024 * 1024)


def dot_t(left, right):
    return lax.dot_general(left, right, (((1,), (1,)), ((), ())), preferred_element_type=F32)


def dot(left, right):
    return lax.dot_general(left, right, (((1,), (0,)), ((), ())), preferred_element_type=F32)


def shift(value, size, chips):
    pairs = []
    for i in range(size):
        chip, core = i // 2, i % 2
        pairs.append((i, 2 * ((chip + chips(chip, core)) % (size // 2)) + core))
    return lax.ppermute(value, "dp", pairs)


def swap(value, size, mask):
    return lax.ppermute(value, "dp", [(i, i ^ mask) for i in range(size)])


def chunks_of(columns):
    width = columns // CHUNKS
    return [slice(c * width, (c + 1) * width) for c in range(CHUNKS)]


def met_kernel(place, txt_emb, txt_proj, img_emb, img_proj, met, emb_v, proj_v, raw, sems):
    parts = chunks_of(raw.shape[1])
    for side, (emb, proj) in enumerate(((txt_emb, txt_proj), (img_emb, img_proj))):

        @pl.when(place[SIDE] == side)
        def _():
            copies = [pltpu.make_async_copy(emb, emb_v, sems.at[CHUNKS])]
            for c, part in enumerate(parts):
                copies.append(
                    pltpu.make_async_copy(proj.at[:, part], proj_v.at[:, part], sems.at[c])
                )
            for copy in copies:
                copy.start()
            copies[0].wait()
            for copy, part in zip(copies[1:], parts):
                copy.wait()
                raw[:, part] = dot(emb_v[...], proj_v[:, part])

    values = raw[...]
    scale = lax.rsqrt(jnp.sum(values * values, axis=1, keepdims=True) + 1e-06)
    met[...] = (values * scale).astype(BF16)


def met_units(place, img_emb, txt_emb, img_proj, txt_proj, name):
    return pl.pallas_call(
        met_kernel,
        out_shape=jax.ShapeDtypeStruct(img_emb.shape, BF16),
        in_specs=[SMEM] + [HBM] * 4,
        out_specs=VMEM,
        scratch_shapes=[
            pltpu.VMEM(img_emb.shape, BF16),
            pltpu.VMEM(img_proj.shape, BF16),
            pltpu.VMEM(img_emb.shape, F32),
            pltpu.SemaphoreType.DMA((CHUNKS + 1,)),
        ],
        compiler_params=params(58),
        name=name,
    )(place, txt_emb, txt_proj, img_emb, img_proj)


def second_kernel(place, *refs):
    sides, (unit, inverse, z, weight, emb_t, emb_v, sems) = (refs[:3], refs[3:6]), refs[6:]
    rows = emb_v.shape[1]
    for side in range(2):

        @pl.when(place[SIDE] == side)
        def _():
            copies = [
                pltpu.make_async_copy(src, dst, sems.at[at])
                for at, (src, dst) in enumerate(
                    zip(sides[side], (weight, emb_v.at[0], emb_v.at[1]))
                )
            ]
            for copy in copies:
                copy.start()
            for copy in copies:
                copy.wait()

    for half in range(2):
        here = slice(half * rows, (half + 1) * rows)
        raw = dot(emb_v[half], weight[...])
        scale = lax.rsqrt(jnp.sum(raw * raw, axis=1, keepdims=True) + 1e-06)
        inverse[here, :] = scale
        units = raw * scale
        unit[here, :] = units
        z[here, :] = units.astype(BF16)
        emb_t[:, here] = emb_v[half].T


def second_units(place, img_emb, txt_emb, img_other, txt_other, img_proj, txt_proj):
    rows, columns = img_emb.shape
    return pl.pallas_call(
        second_kernel,
        out_shape=(
            jax.ShapeDtypeStruct((2 * rows, columns), F32),
            jax.ShapeDtypeStruct((2 * rows, 1), F32),
            jax.ShapeDtypeStruct((2 * rows, columns), BF16),
            jax.ShapeDtypeStruct(img_proj.shape, BF16),
            jax.ShapeDtypeStruct((columns, 2 * rows), BF16),
        ),
        in_specs=[SMEM] + [HBM] * 6,
        out_specs=(VMEM,) * 5,
        scratch_shapes=[
            pltpu.VMEM((2, rows, columns), BF16),
            pltpu.SemaphoreType.DMA((3,)),
        ],
        compiler_params=params(18),
        name="second_units",
    )(place, img_proj, img_emb, img_other, txt_proj, txt_emb, txt_other)


def piece_at(digit, m, height, first=0):
    return pl.ds(pl.multiple_of(first + (digit ^ m) * height, 8), height)


def pick_kernel(at, place, *refs):
    sources, outs, sems = (refs[:2], refs[2:4]), refs[4:6], refs[6]
    for flag in range(2):

        @pl.when(place[at] == flag)
        def _():
            copies = [
                pltpu.make_async_copy(pair[flag], out, sems.at[k])
                for k, (pair, out) in enumerate(zip(sources, outs))
            ]
            for copy in copies:
                copy.start()
            for copy in copies:
                copy.wait()


def pick(place, at, first, second, name):
    return pl.pallas_call(
        functools.partial(pick_kernel, at),
        out_shape=tuple(jax.ShapeDtypeStruct(p[0].shape, p[0].dtype) for p in (first, second)),
        in_specs=[SMEM] + [ANY] * 4,
        out_specs=(ANY, ANY),
        scratch_shapes=[pltpu.SemaphoreType.DMA((2,))],
        compiler_params=params(1),
        name=name,
    )(place, *first, *second)


def pair_term(z, block, scale, bias, diagonal):
    half = dot_t(z, block) * (0.5 * scale) + 0.5 * bias
    coef = 0.5 * jnp.tanh(half) + 0.5
    if diagonal is not None:
        row_at = lax.broadcasted_iota(jnp.int32, coef.shape, 0) + diagonal
        col_at = lax.broadcasted_iota(jnp.int32, coef.shape, 1)
        coef = jnp.where(row_at == col_at, coef - 1.0, coef)
    return dot(coef.astype(BF16), block)


def own_chip_kernel(scale, bias, z, met, met_other, grad):
    step = pl.program_id(0)
    per_block = met.shape[0] // TILE
    here = step * TILE
    near = pair_term(z[...], met[...], scale[0], bias[0], here)
    other = pair_term(z[...], met_other[...], scale[0], bias[0], here - per_block * TILE)
    grad[...] = near + other


def first_phase_kernel(scale, bias, z, one, two, far_own, far_other, grad_in, grad):
    step = pl.program_id(0)
    per_block = one.shape[0] // TILE
    total = grad_in[...] + pair_term(z[...], one[...], scale[0], bias[0], None)
    total = total + pair_term(z[...], two[...], scale[0], bias[0], None)

    @pl.when(step < per_block)
    def _():
        grad[...] = total + pair_term(z[...], far_own[...], scale[0], bias[0], None)

    @pl.when(step >= per_block)
    def _():
        grad[...] = total + pair_term(z[...], far_other[...], scale[0], bias[0], None)


def row_tiles(columns):
    return pl.BlockSpec((TILE, columns), lambda i: (i, 0))


def whole(array):
    return pl.BlockSpec(
        array.shape, lambda i: (0,) * len(array.shape), pipeline_mode=pl.Buffered(1)
    )


def call_tiles(kernel, scale, bias, z, blocks, grads, name, mib):
    rows, columns = z.shape
    return pl.pallas_call(
        kernel,
        grid=(rows // TILE,),
        out_shape=jax.ShapeDtypeStruct((rows, columns), F32),
        in_specs=[SMEM, SMEM, row_tiles(columns)]
        + [whole(b) for b in blocks]
        + [row_tiles(columns)] * len(grads),
        out_specs=row_tiles(columns),
        compiler_params=params(mib),
        name=name,
    )(scale, bias, z, *blocks, *grads)


def last_phase_kernel(
    place, scale, bias, z, one, two, grad_in, unit, inverse, emb_t, du, *rest
):
    pieces, (du_all, emb_v, sem) = rest[:4], rest[4:]
    step = pl.program_id(0)
    fetch = pltpu.make_async_copy(emb_t, emb_v, sem)

    @pl.when(step == 0)
    def _():
        fetch.start()

    grad = grad_in[...] + pair_term(z[...], one[...], scale[0], bias[0], None)
    grad = scale[0] * (grad + pair_term(z[...], two[...], scale[0], bias[0], None))
    units = unit[...]
    inner = jnp.sum(units * grad, axis=1, keepdims=True)
    rounded = ((grad - units * inner) * inverse[...]).astype(BF16)
    du[...] = rounded
    du_all[pl.ds(pl.multiple_of(step * TILE, TILE), TILE), :] = rounded

    @pl.when(step == pl.num_programs(0) - 1)
    def _():
        fetch.wait()
        for m, out in enumerate(pieces):
            part = emb_v[piece_at(place[IN_PLANE], m, out.shape[0]), :]
            out[...] = dot(part, du_all[...]).astype(out.dtype)


def last_phase(place, scale, bias, z, one, two, grad, unit, inverse, emb_t):
    rows, columns = z.shape
    pieces = [
        jax.ShapeDtypeStruct((columns // 6, columns), F32 if m == 0 else BF16) for m in range(4)
    ]
    return pl.pallas_call(
        last_phase_kernel,
        grid=(rows // TILE,),
        out_shape=(jax.ShapeDtypeStruct((rows, columns), BF16), *pieces),
        in_specs=[
            SMEM,
            SMEM,
            SMEM,
            row_tiles(columns),
            whole(one),
            whole(two),
            row_tiles(columns),
            row_tiles(columns),
            row_tiles(1),
            HBM,
        ],
        out_specs=(row_tiles(columns), *[whole(p) for p in pieces]),
        scratch_shapes=[
            pltpu.VMEM((rows, columns), BF16),
            pltpu.VMEM(emb_t.shape, BF16),
            pltpu.SemaphoreType.DMA,
        ],
        compiler_params=params(28),
        name="last_phase",
    )(place, scale, bias, z, one, two, grad, unit, inverse, emb_t)


def line_part_kernel(emb_t, du, out):
    count, height = out.shape[:2]
    first = emb_t.shape[0] - count * height
    for m in range(count):
        rows = slice(first + m * height, first + (m + 1) * height)
        out[m] = dot(emb_t[rows, :], du[...]).astype(BF16)


def line_part(emb_t, du):
    columns = du.shape[1]
    return pl.pallas_call(
        line_part_kernel,
        out_shape=jax.ShapeDtypeStruct((4, columns // 12, columns), BF16),
        in_specs=[VMEM] * 2,
        out_specs=VMEM,
        compiler_params=params(4),
        name="line_part",
    )(emb_t, du)


def rows_back_kernel(du, weight, own, other):
    step = pl.program_id(0)
    back = dot_t(du[...], weight[...]).astype(BF16)

    @pl.when(step < pl.num_programs(0) // 2)
    def _():
        own[...] = back

    @pl.when(step >= pl.num_programs(0) // 2)
    def _():
        other[...] = back


def rows_back(du, weight):
    rows, columns = du.shape
    half = rows // 2 // TILE
    out = jax.ShapeDtypeStruct((rows // 2, columns), BF16)
    return pl.pallas_call(
        rows_back_kernel,
        grid=(rows // TILE,),
        out_shape=(out, out),
        in_specs=[row_tiles(columns), whole(weight)],
        out_specs=(
            pl.BlockSpec((TILE, columns), lambda i: (jnp.minimum(i, half - 1), 0)),
            pl.BlockSpec((TILE, columns), lambda i: (jnp.maximum(i - half, 0), 0)),
        ),
        compiler_params=params(8),
        name="rows_back",
    )(du, weight)


def summed(keep, one, two, three):
    return (keep.astype(F32) + one.astype(F32)) + (two.astype(F32) + three.astype(F32))


def add_split_kernel(place, a0, a1, a2, a3, b, *refs):
    outs, out_b, total = refs[:4], refs[4], refs[5]
    total[...] = summed(a0[...], a1[...], a2[...], a3[...])
    for m, out in enumerate(outs):
        out[...] = total[piece_at(place[IN_LINE], m, out.shape[0]), :].astype(out.dtype)
    out_b[...] = summed(b[0], b[1], b[2], b[3]).astype(BF16)


def add_split(place, part_a, part_b):
    rows, columns = part_a[0].shape
    outs = [
        jax.ShapeDtypeStruct((rows // 4, columns), F32 if m == 0 else BF16) for m in range(4)
    ]
    outs.append(jax.ShapeDtypeStruct(part_b.shape[1:], BF16))
    return pl.pallas_call(
        add_split_kernel,
        out_shape=tuple(outs),
        in_specs=[SMEM] + [VMEM] * 5,
        out_specs=(VMEM,) * 5,
        scratch_shapes=[pltpu.VMEM((rows, columns), F32)],
        compiler_params=params(6),
        name="add_split",
    )(place, *part_a, part_b)


def add_kernel(a0, a1, a2, a3, b, out_a, out_b):
    out_a[...] = summed(a0[...], a1[...], a2[...], a3[...]).astype(BF16)
    out_b[...] = summed(b[0], b[1], b[2], b[3]).astype(BF16)


def add_last(part_a, part_b):
    shapes = part_a[0].shape, part_b.shape[1:]
    return pl.pallas_call(
        add_kernel,
        out_shape=tuple(jax.ShapeDtypeStruct(s, BF16) for s in shapes),
        in_specs=[VMEM] * 5,
        out_specs=(VMEM,) * 2,
        compiler_params=params(3),
        name="add_last",
    )(*part_a, part_b)


def join_kernel(digit, first, place, a0, a1, a2, a3, b, out, total):
    for m, piece in enumerate((a0, a1, a2, a3)):
        total[piece_at(place[digit], m, piece.shape[0]), :] = piece[...].astype(F32)
    if first is None:
        out[...] = total[...].astype(BF16)
    else:
        out[:first, :] = total[...].astype(BF16)
        out[first:, :] = b[...]


def join(place, digit, parts_a, part_b, with_b, name):
    rows, columns = 4 * parts_a[0].shape[0], parts_a[0].shape[1]
    height = rows + part_b.shape[0] if with_b else rows
    return pl.pallas_call(
        functools.partial(join_kernel, digit, rows if with_b else None),
        out_shape=jax.ShapeDtypeStruct((height, columns), BF16),
        in_specs=[SMEM] + [VMEM] * 5,
        out_specs=VMEM,
        scratch_shapes=[pltpu.VMEM((rows, columns), F32)],
        compiler_params=params(8),
        name=name,
    )(place, *parts_a, part_b)


def widen_kernel(own, place, weight, *refs):
    img_out, txt_out, wide, sems = refs[-4:]
    height = weight.shape[0] // 4
    parts = [slice(k * height, (k + 1) * height) for k in range(4)]
    for side, out in enumerate((img_out, txt_out)):

        @pl.when((place[SIDE] == side) == own)
        def _():
            copies = [
                pltpu.make_async_copy(wide.at[part, :], out.at[part, :], sems.at[k])
                for k, part in enumerate(parts)
            ]
            for part, copy in zip(parts, copies):
                wide[part, :] = weight[part, :].astype(F32)
                copy.start()
            for copy in copies:
                copy.wait()


def widen(place, weight, outs):
    out = jax.ShapeDtypeStruct(weight.shape, F32)
    return pl.pallas_call(
        functools.partial(widen_kernel, not outs),
        out_shape=(out, out),
        in_specs=[SMEM, VMEM] + [ANY] * len(outs),
        out_specs=(ANY, ANY),
        scratch_shapes=[pltpu.VMEM(weight.shape, F32), pltpu.SemaphoreType.DMA((4,))],
        input_output_aliases={2: 0, 3: 1} if outs else {},
        compiler_params=params(12),
        name="widen_other" if outs else "widen_own",
    )(place, weight, *outs)


def body(img_emb, txt_emb, img_proj, txt_proj, log_scale, bias):
    size = lax.axis_size("dp")
    rows, columns = img_emb.shape
    scale = jnp.exp(log_scale)
    here = lax.axis_index("dp").astype(jnp.int32)
    side, chip = here % 2, here // 2
    place = jnp.stack([side, chip % 4, (chip // 4) % 4, (chip + side + 1) % 2])
    place, scale = lax.optimization_barrier((place, scale))

    img_other, txt_other = swap(img_emb, size, 1), swap(txt_emb, size, 1)
    met = met_units(place, img_emb, txt_emb, img_proj, txt_proj, "own_met")

    pair = lambda value: swap(value, size, 2)
    pair_met = pair(met)
    far_other = shift(met, size, lambda chip, core: 2 if core else -2)
    met_other = met_units(place, img_other, txt_other, img_proj, txt_proj, "other_met")
    pair_other = pair(met_other)
    far_own = shift(met_other, size, lambda chip, core: -2 if core else 2)

    unit, inverse, z, weight, emb_t = second_units(
        place, img_emb, txt_emb, img_other, txt_other, img_proj, txt_proj
    )
    grad = call_tiles(own_chip_kernel, scale, bias, z, (met, met_other), (), "own_chip", 8)
    pair_met, pair_other, far_own, far_other, grad, emb_t = lax.optimization_barrier(
        (pair_met, pair_other, far_own, far_other, grad, emb_t)
    )
    relay_far, relay_pair = pick(
        place, RELAY, (far_own, far_other), (pair_other, pair_met), "relay_pick"
    )
    relay_far = pair(relay_far)
    relay_pair = shift(relay_pair, size, lambda chip, core: -2 if chip % 2 else 2)
    grad = call_tiles(
        first_phase_kernel,
        scale,
        bias,
        z,
        (pair_met, pair_other, far_own, far_other),
        (grad,),
        "first_phase",
        12,
    )

    du, *pieces = last_phase(
        place, scale, bias, z, relay_far, relay_pair, grad, unit, inverse, emb_t
    )
    plane_masks, line_masks = (2, 4, 6), (8, 16, 24)
    base = [i for i in range(size) if i % 8 < 2]
    plane = [[i + 2 * k for k in range(4)] for i in base]
    base = [i for i in range(size) if i % 32 < 8]
    line = [[i + 8 * k for k in range(4)] for i in base]

    def exchange(sends, masks):
        return [swap(s, size, m) for s, m in zip(sends, masks)]

    def exchange_all(part, groups):
        return lax.all_to_all(part, "dp", 0, 0, axis_index_groups=groups)

    def gather(piece, groups):
        full = exchange_all(jnp.broadcast_to(piece[None], (4, *piece.shape)), groups)
        return full.reshape(-1, columns)

    part_a = [pieces[0], *exchange(pieces[1:], plane_masks)]
    part_b = exchange_all(line_part(emb_t, du), line)
    d_emb, d_emb_send = rows_back(du, weight)
    part_a, part_b, d_emb, d_emb_send = lax.optimization_barrier((part_a, part_b, d_emb, d_emb_send))
    *pieces, sum_b = add_split(place, part_a, part_b)
    part_a = [pieces[0], *exchange(pieces[1:], line_masks)]
    part_b = exchange_all(sum_b.reshape(4, -1, columns), plane)
    d_emb_other = swap(d_emb_send, size, 1)
    d_img_emb, d_txt_emb = pick(
        place, SIDE, (d_emb, d_emb_other), (d_emb_other, d_emb), "rows_pick"
    )
    part_a, part_b, d_img_emb, d_txt_emb = lax.optimization_barrier(
        (part_a, part_b, d_img_emb, d_txt_emb)
    )
    shard_a, shard_b = add_last(part_a, part_b)
    if size > 32:
        groups = [[i for i in range(size) if i % 32 == k] for k in range(32)]
        shard_a, shard_b = lax.psum((shard_a, shard_b), "dp", axis_index_groups=groups)
    parts_a = [shard_a, *exchange([shard_a] * 3, line_masks)]
    piece_b = gather(shard_b, plane)
    parts_a, piece_b = lax.optimization_barrier((parts_a, piece_b))
    piece_a = join(place, IN_LINE, parts_a, piece_b, False, "join")
    parts_a = [piece_a, *exchange([piece_a] * 3, plane_masks)]
    full_b = gather(piece_b, line)
    d_weight = join(place, IN_PLANE, parts_a, full_b, True, "join_all")
    d_weight_other = swap(d_weight, size, 1)
    outs = widen(place, d_weight, ())
    d_img_proj, d_txt_proj = widen(place, d_weight_other, outs)
    return (d_img_emb, d_txt_emb, d_img_proj, d_txt_proj)


def solution(mesh):
    return jax.shard_map(
        body,
        mesh=mesh,
        in_specs=(P("dp", None), P("dp", None), P(), P(), P(), P()),
        out_specs=(P("dp", None), P("dp", None), P(), P()),
        check_vma=False,
    )
```

```python
import functools

import jax
import jax.numpy as jnp
from jax import lax
from jax.experimental import pallas as pl
from jax.experimental.pallas import tpu as pltpu
from jax.sharding import PartitionSpec as P

BF16, F32 = jnp.bfloat16, jnp.float32
CORE, FIRST, SECOND, RELAY = range(4)
VMEM = pl.BlockSpec(memory_space=pltpu.VMEM)
SMEM = pl.BlockSpec(memory_space=pltpu.SMEM)
HBM = pl.BlockSpec(memory_space=pltpu.HBM)
ANY = pl.BlockSpec(memory_space=pl.ANY)

TINY = pl.CostEstimate(flops=1, bytes_accessed=1, transcendentals=0)


def params(mib):
    return pltpu.CompilerParams(vmem_limit_bytes=mib * 1024 * 1024)


def like(shape, dtype):
    return jax.ShapeDtypeStruct(tuple(shape), dtype)


def dot_t(left, right):
    return lax.dot_general(left, right, (((1,), (1,)), ((), ())), preferred_element_type=F32)


def dot(left, right):
    return lax.dot_general(left, right, (((1,), (0,)), ((), ())), preferred_element_type=F32)


def send(value, size, target):
    pairs = []
    for i in range(size):
        chip, core = target(i // 2, i % 2)
        pairs.append((i, 2 * (chip % (size // 2)) + core))
    return lax.ppermute(value, "dp", pairs)


def to_other_core(value, size):
    return send(value, size, lambda chip, core: (chip, 1 - core))


def to_pair(value, size):
    return send(value, size, lambda chip, core: (chip ^ 1, core))


def to_far(value, size):
    return send(value, size, lambda chip, core: (chip + 2, 0) if core else (chip - 2, 1))


def relay(value, size):
    def target(chip, core):
        if core != chip % 2:
            return chip ^ 1, core
        return (chip - 2 if chip % 2 else chip + 2), 1 - core

    return send(value, size, target)


def exchange(sends, size, masks):
    return [
        send(value, size, lambda chip, core, k=k: (chip ^ masks[core][k], core))
        for k, value in enumerate(sends)
    ]


def loads(emb, proj, emb_v, proj_v, sems):
    cut = proj.shape[0] // 256 * 128 + 128
    parts = [slice(0, cut), slice(cut, proj.shape[0])]
    copies = [pltpu.make_async_copy(emb, emb_v, sems.at[0])]
    for k, part in enumerate(parts):
        copies.append(
            pltpu.make_async_copy(proj.at[part, :], proj_v.at[part, :], sems.at[1 + k])
        )
    for copy in copies:
        copy.start()
    return parts, copies


def project(parts, copies, emb_v, proj_v):
    copies[0].wait()
    copies[1].wait()
    raw = dot(emb_v[:, parts[0]], proj_v[parts[0], :])
    copies[2].wait()
    return raw + dot(emb_v[:, parts[1]], proj_v[parts[1], :])


def z_kernel(emb, proj, z, emb_v, proj_v, sems):
    raw = project(*loads(emb, proj, emb_v, proj_v, sems), emb_v, proj_v)
    scale = lax.rsqrt(jnp.sum(raw * raw, axis=1, keepdims=True) + 1e-06)
    z[...] = (raw * scale).astype(BF16)


def units_kernel(emb, proj, z, unit, inverse, emb_t, emb_v, proj_v, sems):
    raw = project(*loads(emb, proj, emb_v, proj_v, sems), emb_v, proj_v)
    scale = lax.rsqrt(jnp.sum(raw * raw, axis=1, keepdims=True) + 1e-06)
    inverse[...] = scale
    units = raw * scale
    unit[...] = units
    z[...] = units.astype(BF16)
    emb_t[...] = emb_v[...].T


def unit_rows(emb, proj, whole, mib, name):
    rows, columns = emb.shape
    outs = [like(emb.shape, BF16)]
    if whole:
        outs += [like(emb.shape, F32), like((rows, 1), F32), like((columns, rows), BF16)]
    return pl.pallas_call(
        units_kernel if whole else z_kernel,
        out_shape=tuple(outs),
        in_specs=[HBM] * 2,
        out_specs=(VMEM,) * len(outs),
        scratch_shapes=[
            pltpu.VMEM(emb.shape, BF16),
            pltpu.VMEM(proj.shape, BF16),
            pltpu.SemaphoreType.DMA((3,)),
        ],
        cost_estimate=TINY,
        compiler_params=params(mib),
        name=name,
    )(emb, proj)


def pair_term(z, block, scale, bias, diagonal=False):
    half = dot_t(z, block) * (0.5 * scale) + 0.5 * bias
    coef = 0.5 * jnp.tanh(half) + 0.5
    if diagonal:
        row_at = lax.broadcasted_iota(jnp.int32, coef.shape, 0)
        col_at = lax.broadcasted_iota(jnp.int32, coef.shape, 1)
        coef = jnp.where(row_at == col_at, coef - 1.0, coef)
    return dot(coef.astype(BF16), block)


def own_chip_kernel(scale, bias, z, own, other, grad):
    grad[...] = pair_term(z[...], own[...], scale[0], bias[0], True)
    grad[...] += pair_term(z[...], other[...], scale[0], bias[0])


def middle_kernel(scale, bias, z, grad_in, one, two, three, grad):
    grad[...] = grad_in[...] + pair_term(z[...], one[...], scale[0], bias[0])
    for block in (two, three):
        grad[...] += pair_term(z[...], block[...], scale[0], bias[0])


def terms(kernel, scale, bias, z, *arrays, mib, name):
    return pl.pallas_call(
        kernel,
        out_shape=like(z.shape, F32),
        in_specs=[SMEM, SMEM] + [VMEM] * (1 + len(arrays)),
        out_specs=VMEM,
        cost_estimate=TINY,
        compiler_params=params(mib),
        name=name,
    )(scale, bias, z, *arrays)


def last_kernel(place, scale, bias, z, grad_in, one, two, unit, inverse, emb_t, du, keep, give, more):
    grad = grad_in[...] + pair_term(z[...], one[...], scale[0], bias[0])
    grad = scale[0] * (grad + pair_term(z[...], two[...], scale[0], bias[0]))
    units = unit[...]
    inner = jnp.sum(units * grad, axis=1, keepdims=True)
    du[...] = ((grad - units * inner) * inverse[...]).astype(BF16)
    half, part = keep.shape[0], give.shape[0]
    there = (1 - place[CORE]) * half
    for out, first in ((give, there), (more, there + part), (keep, place[CORE] * half)):
        rows = pl.ds(pl.multiple_of(first, 32), out.shape[0])
        out[...] = dot(emb_t[rows, :], du[...]).astype(out.dtype)


def last_terms(place, scale, bias, z, grad, one, two, unit, inverse, emb_t, name):
    half, part = ((z.shape[1] // parts, z.shape[1]) for parts in (2, 4))
    return pl.pallas_call(
        last_kernel,
        out_shape=(like(z.shape, BF16), like(half, F32), like(part, BF16), like(part, BF16)),
        in_specs=[SMEM] * 3 + [VMEM] * 7,
        out_specs=(VMEM,) * 4,
        cost_estimate=TINY,
        compiler_params=params(26),
        name=name,
    )(place, scale, bias, z, grad, one, two, unit, inverse, emb_t)


def rows_back_kernel(du, proj, out, proj_v, sem):
    copy = pltpu.make_async_copy(proj, proj_v, sem)
    copy.start()
    copy.wait()
    out[...] = dot_t(du[...], proj_v[...]).astype(BF16)


def rows_back(du, proj, name):
    return pl.pallas_call(
        rows_back_kernel,
        out_shape=like(du.shape, BF16),
        in_specs=[VMEM, HBM],
        out_specs=VMEM,
        scratch_shapes=[pltpu.VMEM(proj.shape, BF16), pltpu.SemaphoreType.DMA],
        cost_estimate=TINY,
        compiler_params=params(10),
        name=name,
    )(du, proj)


def pick_kernel(place, one, two, out, sem):
    for flag, source in enumerate((one, two)):

        @pl.when(place[RELAY] == flag)
        def _():
            copy = pltpu.make_async_copy(source, out, sem)
            copy.start()
            copy.wait()


def pick(place, one, two, name):
    return pl.pallas_call(
        pick_kernel,
        out_shape=like(one.shape, one.dtype),
        in_specs=[SMEM, ANY, ANY],
        out_specs=ANY,
        scratch_shapes=[pltpu.SemaphoreType.DMA],
        cost_estimate=TINY,
        compiler_params=params(1),
        name=name,
    )(place, one, two)


def split_kernel(place, keep, other, more, *refs):
    outs, total = refs[:4], refs[4]
    part = other.shape[0]
    total[:part, :] = keep[:part, :] + other[...].astype(F32)
    total[part:, :] = keep[part:, :] + more[...].astype(F32)
    for m, out in enumerate(outs):
        height = out.shape[0]
        rows = pl.ds(pl.multiple_of((place[FIRST] ^ m) * height, 16), height)
        out[...] = total[rows, :].astype(out.dtype)


def summed(refs):
    one, two, three, four = (ref[...].astype(F32) for ref in refs)
    return (one + two) + (three + four)


def split_again_kernel(place, *refs):
    outs, total, parts = refs[4:8], refs[8], refs[9]
    total[...] = summed(refs[:4])
    height = outs[0].shape[0]
    for k in range(4):
        parts[k, :height, :] = total[k * height : (k + 1) * height, :]
    for m, out in enumerate(outs):
        out[...] = parts[place[SECOND] ^ m, :height, :].astype(out.dtype)


def add_kernel(*refs):
    refs[4][...] = summed(refs[:4]).astype(BF16)


def join_kernel(place, *refs):
    out, total, parts = refs[4:]
    height = refs[0].shape[0]
    for m, ref in enumerate(refs[:4]):
        parts[place[SECOND] ^ m, :height, :] = ref[...].astype(F32)
    for k in range(4):
        total[k * height : (k + 1) * height, :] = parts[k, :height, :]
    out[...] = total[...].astype(BF16)


def join_half_kernel(place, *refs):
    for m, ref in enumerate(refs[:4]):
        height = ref.shape[0]
        rows = pl.ds(pl.multiple_of((place[FIRST] ^ m) * height, 16), height)
        refs[4][rows, :] = ref[...]


def small_call(kernel, place, arrays, outs, scratch, mib, name):
    return pl.pallas_call(
        kernel,
        out_shape=tuple(outs),
        in_specs=([] if place is None else [SMEM]) + [VMEM] * len(arrays),
        out_specs=(VMEM,) * len(outs),
        scratch_shapes=[pltpu.VMEM(shape, F32) for shape in scratch],
        cost_estimate=TINY,
        compiler_params=params(mib),
        name=name,
    )(*([] if place is None else [place]), *arrays)


def four(height, columns):
    return [like((height, columns), F32 if m == 0 else BF16) for m in range(4)]


def padded(height, columns):
    return (4, -(-height // 8) * 8, columns)


def widen_kernel(own, place, half, *refs):
    out, wide, sems = refs[-3:]
    rows = half.shape[0]
    step = rows // 4
    for core in range(2):

        @pl.when((place[CORE] == core) == own)
        def _():
            copies = []
            for k in range(4):
                part = slice(k * step, (k + 1) * step)
                goal = slice(core * rows + k * step, core * rows + (k + 1) * step)
                wide[part, :] = half[part, :].astype(F32)
                copies.append(
                    pltpu.make_async_copy(wide.at[part, :], out.at[goal, :], sems.at[k])
                )
                copies[-1].start()
            for copy in copies:
                copy.wait()


def widen(place, half, out, name):
    return pl.pallas_call(
        functools.partial(widen_kernel, out is None),
        out_shape=like((2 * half.shape[0], half.shape[1]), F32),
        in_specs=[SMEM, VMEM] + ([] if out is None else [ANY]),
        out_specs=ANY,
        scratch_shapes=[pltpu.VMEM(half.shape, F32), pltpu.SemaphoreType.DMA((4,))],
        input_output_aliases={} if out is None else {2: 0},
        cost_estimate=TINY,
        compiler_params=params(6),
        name=name,
    )(place, half, *([] if out is None else [out]))


def after(values, *others):
    return lax.optimization_barrier((values, others))[0]


def body(img_emb, txt_emb, img_proj, txt_proj, log_scale, bias):
    size = lax.axis_size("dp")
    columns = img_emb.shape[1]
    here = lax.axis_index("dp").astype(jnp.int32)
    core, chip = here % 2, here // 2
    in_plane, in_line = chip % 4, (chip // 4) % 4
    place = jnp.stack(
        [
            core,
            jnp.where(core == 0, in_plane, in_line),
            jnp.where(core == 0, in_line, in_plane),
            (chip + core) % 2,
        ]
    )
    place, scale = lax.optimization_barrier((place, jnp.exp(log_scale)))
    plane, line = (1, 2, 3), (4, 8, 12)
    first_masks, second_masks = (plane, line), (line, plane)
    quarter, shard = columns // 8, columns // 32

    (txt_z,) = unit_rows(after(txt_emb, place), txt_proj, False, 58, "txt_z")
    txt_pair = to_pair(txt_z, size)
    txt_far = to_far(txt_z, size)
    txt_other = to_other_core(txt_z, size)
    img_z, img_unit, img_inverse, img_emb_t = unit_rows(
        after(img_emb, txt_z), img_proj, True, 16, "img_units"
    )
    img_grad = terms(
        own_chip_kernel, scale, bias, img_z, txt_z, txt_other, mib=14, name="img_own_chip"
    )
    _, txt_unit, txt_inverse, txt_emb_t = unit_rows(
        after(txt_emb, img_grad), txt_proj, True, 16, "txt_units"
    )
    txt_pair, txt_far = after((txt_pair, txt_far), txt_unit)
    txt_relay = relay(pick(place, txt_pair, txt_far, "txt_pick"), size)
    txt_pair_other = to_other_core(txt_pair, size)
    img_grad = terms(
        middle_kernel,
        scale,
        bias,
        img_z,
        img_grad,
        txt_pair,
        txt_far,
        txt_pair_other,
        mib=18,
        name="img_middle",
    )

    img_sent, txt_relay = lax.optimization_barrier((img_z, after(txt_relay, img_grad)))
    txt_relay_other = to_other_core(txt_relay, size)
    img_pair = to_pair(img_sent, size)
    img_far = to_far(img_sent, size)
    img_other = to_other_core(img_sent, size)
    img_du, img_keep, *img_give = last_terms(
        place,
        scale,
        bias,
        img_z,
        img_grad,
        txt_relay,
        txt_relay_other,
        img_unit,
        img_inverse,
        img_emb_t,
        "img_last",
    )

    def scatter_first(keep, give, name):
        got = [to_other_core(part, size) for part in give]
        mine, *sends = small_call(
            split_kernel,
            place,
            [keep, *got],
            four(quarter, columns),
            [(4 * quarter, columns)],
            8,
            name,
        )
        return mine, [mine, *exchange(sends, size, first_masks)]

    def scatter_second(parts, name):
        mine, *sends = small_call(
            split_again_kernel,
            place,
            parts,
            four(shard, columns),
            [(quarter, columns), padded(shard, columns)],
            5,
            name,
        )
        return mine, [mine, *exchange(sends, size, second_masks)]

    def gather_second(parts, name):
        (mine,) = small_call(add_kernel, None, parts, [like((shard, columns), BF16)], [], 2, name)
        if size > 32:
            groups = [[i for i in range(size) if i % 32 == k] for k in range(32)]
            mine = lax.psum(mine, "dp", axis_index_groups=groups)
        return mine, [mine, *exchange([mine] * 3, size, second_masks)]

    def gather_first(parts, name):
        (mine,) = small_call(
            join_kernel,
            place,
            parts,
            [like((quarter, columns), BF16)],
            [(quarter, columns), padded(shard, columns)],
            5,
            name,
        )
        return mine, [mine, *exchange([mine] * 3, size, first_masks)]

    def whole_sum(parts, name):
        half_shape = [like((4 * quarter, columns), BF16)]
        (half,) = small_call(join_half_kernel, place, parts, half_shape, [], 4, name + "_half")
        other = to_other_core(half, size)
        out = widen(place, half, None, name + "_own")
        return widen(place, other, out, name + "_other")

    done, img_parts = scatter_first(img_keep, img_give, "img_split")
    txt_grad = terms(
        own_chip_kernel,
        scale,
        bias,
        after(txt_z, done),
        img_sent,
        img_other,
        mib=14,
        name="txt_own_chip",
    )
    d_img_emb = rows_back(after(img_du, done), img_proj, "img_rows")
    img_pair, img_far = after((img_pair, img_far), txt_grad, d_img_emb, img_parts)
    picked = pick(place, img_pair, img_far, "img_pick")
    img_relay = relay(picked, size)
    img_pair_other = to_other_core(img_pair, size)
    _, img_parts = scatter_second(after(img_parts, picked), "img_split_again")
    txt_grad = terms(
        middle_kernel,
        scale,
        bias,
        txt_z,
        txt_grad,
        img_pair,
        img_far,
        img_pair_other,
        mib=18,
        name="txt_middle",
    )
    done, img_parts = gather_second(after(img_parts, txt_grad), "img_add")
    img_relay = after(img_relay, done)
    img_relay_other = to_other_core(img_relay, size)
    txt_du, txt_keep, *txt_give = last_terms(
        place,
        scale,
        bias,
        txt_z,
        txt_grad,
        img_relay,
        img_relay_other,
        txt_unit,
        txt_inverse,
        txt_emb_t,
        "txt_last",
    )
    done, txt_parts = scatter_first(after(txt_keep, img_parts[1]), txt_give, "txt_split")
    d_txt_emb = rows_back(after(txt_du, done), txt_proj, "txt_rows")
    done, txt_parts = scatter_second(after(txt_parts, d_txt_emb), "txt_split_again")
    _, img_parts = gather_first(after(img_parts, done), "img_join")
    _, txt_parts = gather_second(txt_parts, "txt_add")
    done, txt_parts = gather_first(after(txt_parts, img_parts), "txt_join")
    d_img_proj = whole_sum(after(img_parts, done), "img_sum")
    d_txt_proj = whole_sum(after(txt_parts, d_img_proj), "txt_sum")
    return (d_img_emb, d_txt_emb, d_img_proj, d_txt_proj)


def solution(mesh):
    return jax.shard_map(
        body,
        mesh=mesh,
        in_specs=(P("dp", None), P("dp", None), P(), P(), P(), P()),
        out_specs=(P("dp", None), P("dp", None), P(), P()),
        check_vma=False,
    )
```

```python
import functools

import jax
import jax.numpy as jnp
from jax import lax
from jax.experimental import pallas as pl
from jax.experimental.pallas import tpu as pltpu
from jax.sharding import PartitionSpec as P

REACH = 3
BF16, F32 = jnp.bfloat16, jnp.float32
TILE = 512
SIDE, IN_PLANE, IN_LINE, RELAY, X, Y, Z_LOW, Z_HIGH = range(8)
VMEM = pl.BlockSpec(memory_space=pltpu.VMEM)
SMEM = pl.BlockSpec(memory_space=pltpu.SMEM)
HBM = pl.BlockSpec(memory_space=pltpu.HBM)
ANY = pl.BlockSpec(memory_space=pl.ANY)


def params(mib):
    return pltpu.CompilerParams(vmem_limit_bytes=mib * 1024 * 1024)


def dot_t(left, right):
    return lax.dot_general(left, right, (((1,), (1,)), ((), ())), preferred_element_type=F32)


def dot(left, right):
    return lax.dot_general(left, right, (((1,), (0,)), ((), ())), preferred_element_type=F32)


def shift(value, size, chips):
    pairs = []
    for i in range(size):
        chip, core = i // 2, i % 2
        pairs.append((i, 2 * ((chip + chips(chip, core)) % (size // 2)) + core))
    return lax.ppermute(value, "dp", pairs)


def swap(value, size, mask):
    return lax.ppermute(value, "dp", [(i, i ^ mask) for i in range(size)])


def met_kernel(place, txt_emb, txt_proj, img_emb, img_proj, met, emb_v, proj_v, sems):
    cut = proj_v.shape[0] // 256 * 128 + 128
    parts = [slice(0, cut), slice(cut, proj_v.shape[0])]

    def copies_of(emb, proj):
        copies = [pltpu.make_async_copy(emb, emb_v, sems.at[2])]
        for k, part in enumerate(parts):
            copies.append(
                pltpu.make_async_copy(proj.at[part, :], proj_v.at[part, :], sems.at[k])
            )
        return copies

    for side, (emb, proj) in enumerate(((txt_emb, txt_proj), (img_emb, img_proj))):

        @pl.when(place[SIDE] == side)
        def _():
            copies = copies_of(emb, proj)
            for copy in copies:
                copy.start()
            for copy in copies[:2]:
                copy.wait()

    raw = dot(emb_v[:, parts[0]], proj_v[parts[0], :])
    for side, (emb, proj) in enumerate(((txt_emb, txt_proj), (img_emb, img_proj))):

        @pl.when(place[SIDE] == side)
        def _():
            copies_of(emb, proj)[2].wait()

    raw = raw + dot(emb_v[:, parts[1]], proj_v[parts[1], :])
    scale = lax.rsqrt(jnp.sum(raw * raw, axis=1, keepdims=True) + 1e-06)
    met[...] = (raw * scale).astype(BF16)


def met_units(place, img_emb, txt_emb, img_proj, txt_proj, name):
    return pl.pallas_call(
        met_kernel,
        out_shape=jax.ShapeDtypeStruct(img_emb.shape, BF16),
        in_specs=[SMEM] + [HBM] * 4,
        out_specs=VMEM,
        scratch_shapes=[
            pltpu.VMEM(img_emb.shape, BF16),
            pltpu.VMEM(img_proj.shape, BF16),
            pltpu.SemaphoreType.DMA((3,)),
        ],
        compiler_params=params(58),
        name=name,
    )(place, txt_emb, txt_proj, img_emb, img_proj)


def second_kernel(place, *refs):
    sides, (unit, inverse, z, weight, emb_t, emb_v, sems) = (refs[:3], refs[3:6]), refs[6:]
    rows = emb_v.shape[1]
    for side in range(2):

        @pl.when(place[SIDE] == side)
        def _():
            copies = [
                pltpu.make_async_copy(src, dst, sems.at[at])
                for at, (src, dst) in enumerate(
                    zip(sides[side], (weight, emb_v.at[0], emb_v.at[1]))
                )
            ]
            for copy in copies:
                copy.start()
            for copy in copies:
                copy.wait()

    for half in range(2):
        here = slice(half * rows, (half + 1) * rows)
        raw = dot(emb_v[half], weight[...])
        scale = lax.rsqrt(jnp.sum(raw * raw, axis=1, keepdims=True) + 1e-06)
        inverse[here, :] = scale
        units = raw * scale
        unit[here, :] = units
        z[here, :] = units.astype(BF16)
        emb_t[:, here] = emb_v[half].T


def second_units(place, img_emb, txt_emb, img_other, txt_other, img_proj, txt_proj):
    rows, columns = img_emb.shape
    return pl.pallas_call(
        second_kernel,
        out_shape=(
            jax.ShapeDtypeStruct((2 * rows, columns), F32),
            jax.ShapeDtypeStruct((2 * rows, 1), F32),
            jax.ShapeDtypeStruct((2 * rows, columns), BF16),
            jax.ShapeDtypeStruct(img_proj.shape, BF16),
            jax.ShapeDtypeStruct((columns, 2 * rows), BF16),
        ),
        in_specs=[SMEM] + [HBM] * 6,
        out_specs=(VMEM,) * 5,
        scratch_shapes=[
            pltpu.VMEM((2, rows, columns), BF16),
            pltpu.SemaphoreType.DMA((3,)),
        ],
        compiler_params=params(18),
        name="second_units",
    )(place, img_proj, img_emb, img_other, txt_proj, txt_emb, txt_other)


def piece_at(digit, m, height, first=0):
    return pl.ds(pl.multiple_of(first + (digit ^ m) * height, 8), height)


def pick_kernel(at, place, *refs):
    sources, outs, sems = (refs[:2], refs[2:4]), refs[4:6], refs[6]
    for flag in range(2):

        @pl.when(place[at] == flag)
        def _():
            copies = [
                pltpu.make_async_copy(pair[flag], out, sems.at[k])
                for k, (pair, out) in enumerate(zip(sources, outs))
            ]
            for copy in copies:
                copy.start()
            for copy in copies:
                copy.wait()


def pick(place, at, first, second, name):
    return pl.pallas_call(
        functools.partial(pick_kernel, at),
        out_shape=tuple(jax.ShapeDtypeStruct(p[0].shape, p[0].dtype) for p in (first, second)),
        in_specs=[SMEM] + [ANY] * 4,
        out_specs=(ANY, ANY),
        scratch_shapes=[pltpu.SemaphoreType.DMA((2,))],
        compiler_params=params(1),
        name=name,
    )(place, *first, *second)


def pair_term(z, block, scale, bias, diagonal):
    half = dot_t(z, block) * (0.5 * scale) + 0.5 * bias
    coef = 0.5 * jnp.tanh(half) + 0.5
    if diagonal is not None:
        row_at = lax.broadcasted_iota(jnp.int32, coef.shape, 0) + diagonal
        col_at = lax.broadcasted_iota(jnp.int32, coef.shape, 1)
        coef = jnp.where(row_at == col_at, coef - 1.0, coef)
    return dot(coef.astype(BF16), block)


def own_chip_kernel(scale, bias, z, met, met_other, grad):
    step = pl.program_id(0)
    per_block = met.shape[0] // TILE
    here = step * TILE
    near = pair_term(z[...], met[...], scale[0], bias[0], here)
    other = pair_term(z[...], met_other[...], scale[0], bias[0], here - per_block * TILE)
    grad[...] = near + other


def first_phase_kernel(scale, bias, z, one, two, far_own, far_other, grad_in, grad):
    step = pl.program_id(0)
    per_block = one.shape[0] // TILE
    total = grad_in[...] + pair_term(z[...], one[...], scale[0], bias[0], None)
    total = total + pair_term(z[...], two[...], scale[0], bias[0], None)

    @pl.when(step < per_block)
    def _():
        grad[...] = total + pair_term(z[...], far_own[...], scale[0], bias[0], None)

    @pl.when(step >= per_block)
    def _():
        grad[...] = total + pair_term(z[...], far_other[...], scale[0], bias[0], None)


def row_tiles(columns):
    return pl.BlockSpec((TILE, columns), lambda i: (i, 0))


def whole(array):
    return pl.BlockSpec(
        array.shape, lambda i: (0,) * len(array.shape), pipeline_mode=pl.Buffered(1)
    )


def call_tiles(kernel, scale, bias, z, blocks, grads, name, mib):
    rows, columns = z.shape
    return pl.pallas_call(
        kernel,
        grid=(rows // TILE,),
        out_shape=jax.ShapeDtypeStruct((rows, columns), F32),
        in_specs=[SMEM, SMEM, row_tiles(columns)]
        + [whole(b) for b in blocks]
        + [row_tiles(columns)] * len(grads),
        out_specs=row_tiles(columns),
        compiler_params=params(mib),
        name=name,
    )(scale, bias, z, *blocks, *grads)


def last_phase_kernel(
    place, scale, bias, z, one, two, grad_in, unit, inverse, emb_t, du, *rest
):
    half, (du_all, emb_v, sem) = rest[0], rest[1:]
    step = pl.program_id(0)
    fetch = pltpu.make_async_copy(emb_t, emb_v, sem)

    @pl.when(step == 0)
    def _():
        fetch.start()

    grad = grad_in[...] + pair_term(z[...], one[...], scale[0], bias[0], None)
    grad = scale[0] * (grad + pair_term(z[...], two[...], scale[0], bias[0], None))
    units = unit[...]
    inner = jnp.sum(units * grad, axis=1, keepdims=True)
    rounded = ((grad - units * inner) * inverse[...]).astype(BF16)
    du[...] = rounded
    du_all[pl.ds(pl.multiple_of(step * TILE, TILE), TILE), :] = rounded

    @pl.when(step == pl.num_programs(0) - 1)
    def _():
        fetch.wait()
        height = half.shape[0]
        first = emb_v.shape[0] - 2 * height
        rows = piece_at(place[Z_LOW], 1, height, first)
        half[...] = dot(emb_v[rows, :], du_all[...]).astype(BF16)


def last_phase(place, scale, bias, z, one, two, grad, unit, inverse, emb_t):
    rows, columns = z.shape
    half = jax.ShapeDtypeStruct((columns // 6, columns), BF16)
    return pl.pallas_call(
        last_phase_kernel,
        grid=(rows // TILE,),
        out_shape=(jax.ShapeDtypeStruct((rows, columns), BF16), half),
        in_specs=[
            SMEM,
            SMEM,
            SMEM,
            row_tiles(columns),
            whole(one),
            whole(two),
            row_tiles(columns),
            row_tiles(columns),
            row_tiles(1),
            HBM,
        ],
        out_specs=(row_tiles(columns), whole(half)),
        scratch_shapes=[
            pltpu.VMEM((rows, columns), BF16),
            pltpu.VMEM(emb_t.shape, BF16),
            pltpu.SemaphoreType.DMA,
        ],
        compiler_params=params(28),
        name="last_phase",
    )(place, scale, bias, z, one, two, grad, unit, inverse, emb_t)


def other_parts_kernel(place, emb_t, du, keep_b, *pieces):
    height = keep_b.shape[0]
    for m, out in enumerate(pieces):
        rows = piece_at(place[IN_PLANE], m, height)
        out[...] = dot(emb_t[rows, :], du[...]).astype(out.dtype)
    rows = piece_at(place[Z_LOW], 0, height, emb_t.shape[0] - 2 * height)
    keep_b[...] = dot(emb_t[rows, :], du[...])


def other_parts(place, emb_t, du):
    shape = (emb_t.shape[0] // 6, emb_t.shape[0])
    kinds = [F32, F32, BF16, BF16, BF16]
    return pl.pallas_call(
        other_parts_kernel,
        out_shape=tuple(jax.ShapeDtypeStruct(shape, kind) for kind in kinds),
        in_specs=[SMEM] + [VMEM] * 2,
        out_specs=(VMEM,) * 5,
        compiler_params=params(8),
        name="other_parts",
    )(place, emb_t, du)


def rows_back_kernel(du, weight, own, other):
    step = pl.program_id(0)
    back = dot_t(du[...], weight[...]).astype(BF16)

    @pl.when(step < pl.num_programs(0) // 2)
    def _():
        own[...] = back

    @pl.when(step >= pl.num_programs(0) // 2)
    def _():
        other[...] = back


def rows_back(du, weight):
    rows, columns = du.shape
    half = rows // 2 // TILE
    out = jax.ShapeDtypeStruct((rows // 2, columns), BF16)
    return pl.pallas_call(
        rows_back_kernel,
        grid=(rows // TILE,),
        out_shape=(out, out),
        in_specs=[row_tiles(columns), whole(weight)],
        out_specs=(
            pl.BlockSpec((TILE, columns), lambda i: (jnp.minimum(i, half - 1), 0)),
            pl.BlockSpec((TILE, columns), lambda i: (jnp.maximum(i - half, 0), 0)),
        ),
        compiler_params=params(8),
        name="rows_back",
    )(du, weight)


def summed(refs):
    one, two, three, four = (ref[...].astype(F32) for ref in refs)
    return (one + two) + (three + four)


def small_call(kernel, place, arrays, outs, scratch, mib, name):
    return pl.pallas_call(
        kernel,
        out_shape=tuple(jax.ShapeDtypeStruct(shape, kind) for shape, kind in outs),
        in_specs=[SMEM] + [VMEM] * len(arrays),
        out_specs=(VMEM,) * len(outs),
        scratch_shapes=[pltpu.VMEM(shape, F32) for shape in scratch],
        compiler_params=params(mib),
        name=name,
    )(place, *arrays)


def add_split_kernel(place, *refs):
    total = refs[8]
    total[...] = summed(refs[:4])
    for m, out in enumerate(refs[4:8]):
        out[...] = total[piece_at(place[IN_LINE], m, out.shape[0]), :].astype(out.dtype)


def add_split(place, parts, name):
    rows, columns = parts[0].shape
    outs = [((rows // 4, columns), F32 if m == 0 else BF16) for m in range(4)]
    return small_call(add_split_kernel, place, parts, outs, [(rows, columns)], 4, name)


def add_all_kernel(place, *refs):
    refs[4][...] = summed(refs[:4]).astype(BF16)


def add_all(place, parts, name):
    return small_call(add_all_kernel, place, parts, [(parts[0].shape, BF16)], [], 2, name)[0]


def join_four_kernel(digit, place, *refs):
    out, total = refs[4:]
    for m, piece in enumerate(refs[:4]):
        total[piece_at(place[digit], m, piece.shape[0]), :] = piece[...].astype(F32)
    out[...] = total[...].astype(BF16)


def join_four(place, digit, parts, name):
    shape = (4 * parts[0].shape[0], parts[0].shape[1])
    kernel = functools.partial(join_four_kernel, digit)
    return small_call(kernel, place, parts, [(shape, BF16)], [shape], 7, name)[0]


def add_halve_kernel(bit, place, keep, got, mine, give, total):
    total[...] = keep[...] + got[...].astype(F32)
    for m, out in enumerate((mine, give)):
        out[...] = total[piece_at(place[bit], m, out.shape[0]), :].astype(out.dtype)


def add_halve(place, bit, keep, got, name):
    rows, columns = keep.shape
    outs = [((rows // 2, columns), kind) for kind in (F32, BF16)]
    kernel = functools.partial(add_halve_kernel, bit)
    return small_call(kernel, place, [keep, got], outs, [keep.shape], 3, name)


def add_two_kernel(place, keep, got, out):
    out[...] = (keep[...] + got[...].astype(F32)).astype(BF16)


def add_two(place, keep, got, name):
    return small_call(add_two_kernel, place, [keep, got], [(keep.shape, BF16)], [], 2, name)[0]


def join_two_kernel(bit, place, mine, got, out, total):
    for m, piece in enumerate((mine, got)):
        total[piece_at(place[bit], m, piece.shape[0]), :] = piece[...].astype(F32)
    out[...] = total[...].astype(BF16)


def join_two(place, bit, mine, got, name):
    shape = (2 * mine.shape[0], mine.shape[1])
    kernel = functools.partial(join_two_kernel, bit)
    return small_call(kernel, place, [mine, got], [(shape, BF16)], [shape], 5, name)[0]


def widen_kernel(own, first, place, weight, *refs):
    img_out, txt_out, wide, sems = refs[-4:]
    height = weight.shape[0] // 4
    for side, out in enumerate((img_out, txt_out)):

        @pl.when((place[SIDE] == side) == own)
        def _():
            copies = []
            for k in range(4):
                part = slice(k * height, (k + 1) * height)
                goal = slice(first + k * height, first + (k + 1) * height)
                wide[part, :] = weight[part, :].astype(F32)
                copies.append(
                    pltpu.make_async_copy(wide.at[part, :], out.at[goal, :], sems.at[k])
                )
                copies[-1].start()
            for copy in copies:
                copy.wait()


def widen(place, weight, first, own, outs, name):
    columns = weight.shape[1]
    out = jax.ShapeDtypeStruct((columns, columns), F32)
    return pl.pallas_call(
        functools.partial(widen_kernel, own, first),
        out_shape=(out, out),
        in_specs=[SMEM, VMEM] + [ANY] * len(outs),
        out_specs=(ANY, ANY),
        scratch_shapes=[pltpu.VMEM(weight.shape, F32), pltpu.SemaphoreType.DMA((4,))],
        input_output_aliases={2: 0, 3: 1} if outs else {},
        compiler_params=params(8),
        name=name,
    )(place, weight, *outs)


def body(img_emb, txt_emb, img_proj, txt_proj, log_scale, bias):
    size = lax.axis_size("dp")
    rows, columns = img_emb.shape
    scale = jnp.exp(log_scale)
    here = lax.axis_index("dp").astype(jnp.int32)
    side, chip = here % 2, here // 2
    bits = [(chip // n) % 2 for n in (1, 2, 4, 8)]
    place = jnp.stack([side, chip % 4, (chip // 4) % 4, (chip + side + 1) % 2, *bits])
    place, scale = lax.optimization_barrier((place, scale))

    img_other, txt_other = swap(img_emb, size, 1), swap(txt_emb, size, 1)
    met = met_units(place, img_emb, txt_emb, img_proj, txt_proj, "own_met")

    pair = lambda value: swap(value, size, 2)
    pair_met = pair(met)
    far_other = shift(met, size, lambda chip, core: 2 if core else -2)
    met_other = met_units(place, img_other, txt_other, img_proj, txt_proj, "other_met")
    pair_other = pair(met_other)
    far_own = shift(met_other, size, lambda chip, core: -2 if core else 2)

    unit, inverse, z, weight, emb_t = second_units(
        place, img_emb, txt_emb, img_other, txt_other, img_proj, txt_proj
    )
    grad = call_tiles(own_chip_kernel, scale, bias, z, (met, met_other), (), "own_chip", 8)
    pair_met, pair_other, far_own, far_other, grad, emb_t = lax.optimization_barrier(
        (pair_met, pair_other, far_own, far_other, grad, emb_t)
    )
    relay_far, relay_pair = pick(
        place, RELAY, (far_own, far_other), (pair_other, pair_met), "relay_pick"
    )
    relay_far = pair(relay_far)
    relay_pair = shift(relay_pair, size, lambda chip, core: -2 if chip % 2 else 2)
    grad = call_tiles(
        first_phase_kernel,
        scale,
        bias,
        z,
        (pair_met, pair_other, far_own, far_other),
        (grad,),
        "first_phase",
        12,
    )

    du, give_b = last_phase(
        place, scale, bias, z, relay_far, relay_pair, grad, unit, inverse, emb_t
    )

    def exchange(sends, masks):
        return [swap(s, size, m) for s, m in zip(sends, masks)]

    plane_masks, line_masks = (2, 4, 6), (8, 16, 24)
    x_bit, y_bit, low_bit, high_bit = (X, 2), (Y, 4), (Z_LOW, 8), (Z_HIGH, 16)

    def halve(keep, got, bit, name):
        keep, give = add_halve(place, bit[0], keep, got, name)
        return keep, swap(give, size, bit[1]), give

    def gather(mine, bit):
        return mine, swap(mine, size, bit[1])

    together = lax.optimization_barrier
    got_b = swap(give_b, size, low_bit[1])
    keep_b, *pieces = other_parts(place, emb_t, du)
    parts_a = [pieces[0], *exchange(pieces[1:], plane_masks)]
    keep_b, got_b, give_b = halve(keep_b, got_b, high_bit, "b_high")
    du, _ = together((du, give_b))
    d_emb, d_emb_send = rows_back(du, weight)
    parts_a, got_b, d_emb_send = together((parts_a, got_b, d_emb_send))
    d_emb_other = swap(d_emb_send, size, 1)
    pieces = add_split(place, parts_a, "a_split")
    parts_a = [pieces[0], *exchange(pieces[:0:-1], line_masks[::-1])]
    keep_b, got_b, _ = halve(keep_b, got_b, x_bit, "b_x")
    d_img_emb, d_txt_emb = pick(
        place, SIDE, (d_emb, d_emb_other), (d_emb_other, d_emb), "rows_pick"
    )
    keep_b, got_b, give_b = halve(keep_b, got_b, y_bit, "b_y")
    parts_a, d_img_emb, d_txt_emb, _ = together((parts_a, d_img_emb, d_txt_emb, give_b))

    parts_a, got_b = together((parts_a, got_b))
    shard_a = add_all(place, parts_a, "a_last")
    shard_b = add_two(place, keep_b, got_b, "b_last")
    if size > 32:
        groups = [[i for i in range(size) if i % 32 == k] for k in range(32)]
        shard_a, shard_b = lax.psum((shard_a, shard_b), "dp", axis_index_groups=groups)
    parts_a = [shard_a, *exchange([shard_a] * 3, line_masks)]
    shard_b = join_two(place, y_bit[0], *gather(shard_b, y_bit), "b_join_y")
    got_b = swap(shard_b, size, x_bit[1])
    parts_a, _ = together((parts_a, shard_b))

    parts_a, got_b = together((parts_a, got_b))
    piece_a = join_four(place, IN_LINE, parts_a, "a_join")
    parts_a = [piece_a, *exchange([piece_a] * 3, plane_masks)]
    shard_b = join_two(place, x_bit[0], shard_b, got_b, "b_join_x")
    shard_b = join_two(place, high_bit[0], *gather(shard_b, high_bit), "b_join_high")
    got_b = swap(shard_b, size, low_bit[1])
    parts_a, got_b = together((parts_a, got_b))

    shard_b = join_two(place, low_bit[0], shard_b, got_b, "b_join_low")
    first_b = columns - shard_b.shape[0]
    other_b = swap(shard_b, size, 1)
    outs = widen(place, shard_b, first_b, True, (), "b_own")
    outs = widen(place, other_b, first_b, False, outs, "b_other")
    whole_a = join_four(place, IN_PLANE, parts_a, "a_join_all")
    other_a = swap(whole_a, size, 1)
    outs = widen(place, whole_a, 0, True, outs, "a_own")
    d_img_proj, d_txt_proj = widen(place, other_a, 0, False, outs, "a_other")
    return (d_img_emb, d_txt_emb, d_img_proj, d_txt_proj)


def solution(mesh):
    return jax.shard_map(
        body,
        mesh=mesh,
        in_specs=(P("dp", None), P("dp", None), P(), P(), P(), P()),
        out_specs=(P("dp", None), P("dp", None), P(), P()),
        check_vma=False,
    )
```

```python
import functools

import jax
import jax.numpy as jnp
from jax import lax
from jax.experimental import pallas as pl
from jax.experimental.pallas import tpu as pltpu
from jax.sharding import PartitionSpec as P

REACH = 3
BF16, F32 = jnp.bfloat16, jnp.float32
TILE = 512
SIDE, IN_PLANE, IN_LINE, SAME, X, Y, Z_LOW, Z_HIGH = range(8)
VMEM = pl.BlockSpec(memory_space=pltpu.VMEM)
SMEM = pl.BlockSpec(memory_space=pltpu.SMEM)
HBM = pl.BlockSpec(memory_space=pltpu.HBM)
ANY = pl.BlockSpec(memory_space=pl.ANY)


def params(mib):
    return pltpu.CompilerParams(vmem_limit_bytes=mib * 1024 * 1024)


def dot_t(left, right):
    return lax.dot_general(left, right, (((1,), (1,)), ((), ())), preferred_element_type=F32)


def dot(left, right):
    return lax.dot_general(left, right, (((1,), (0,)), ((), ())), preferred_element_type=F32)


def shift(value, size, chips):
    pairs = []
    for i in range(size):
        chip, core = i // 2, i % 2
        pairs.append((i, 2 * ((chip + chips(chip, core)) % (size // 2)) + core))
    return lax.ppermute(value, "dp", pairs)


def swap(value, size, mask):
    return lax.ppermute(value, "dp", [(i, i ^ mask) for i in range(size)])


def raw_kernel(place, img_emb, txt_emb, one, two, sems):
    for same, pair in enumerate(((img_emb, txt_emb), (txt_emb, img_emb))):

        @pl.when(place[SAME] == same)
        def _():
            copies = [
                pltpu.make_async_copy(src, dst, sems.at[k])
                for k, (src, dst) in enumerate(zip(pair, (one, two)))
            ]
            for copy in copies:
                copy.start()
            for copy in copies:
                copy.wait()


def raw_blocks(place, img_emb, txt_emb):
    out = jax.ShapeDtypeStruct(img_emb.shape, BF16)
    return pl.pallas_call(
        raw_kernel,
        out_shape=(out, out),
        in_specs=[SMEM] + [HBM] * 2,
        out_specs=(HBM, HBM),
        scratch_shapes=[pltpu.SemaphoreType.DMA((2,))],
        compiler_params=params(58),
        name="raw_blocks",
    )(place, img_emb, txt_emb)


def met_kernel(own_chip, place, *refs):
    sides, projs, (z_one, z_two, emb_v, proj_v, sems) = (refs[:2], refs[2:4]), refs[4:6], refs[6:]
    cut = proj_v.shape[0] // 256 * 128 + 128
    parts = [slice(0, cut), slice(cut, proj_v.shape[0])]
    for side, (embs, proj) in enumerate(zip(sides, projs)):

        @pl.when(place[SIDE] == side)
        def _():
            first = 1 - place[SAME] if own_chip else 0
            copies = [pltpu.make_async_copy(embs[0], emb_v.at[first], sems.at[2])]
            for k, part in enumerate(parts):
                copies.append(
                    pltpu.make_async_copy(proj.at[part, :], proj_v.at[part, :], sems.at[k])
                )
            copies.append(pltpu.make_async_copy(embs[1], emb_v.at[1 - first], sems.at[3]))
            for copy in copies:
                copy.start()
            for copy in copies:
                copy.wait()

    for k, z in enumerate((z_one, z_two)):
        raw = dot(emb_v[k], proj_v[...])
        scale = lax.rsqrt(jnp.sum(raw * raw, axis=1, keepdims=True) + 1e-06)
        z[...] = (raw * scale).astype(BF16)


def met_units(place, text_side, image_side, img_proj, txt_proj, own_chip, mib, name):
    out = jax.ShapeDtypeStruct(text_side[0].shape, BF16)
    return pl.pallas_call(
        functools.partial(met_kernel, own_chip),
        out_shape=(out, out),
        in_specs=[SMEM] + [HBM] * 6,
        out_specs=(VMEM, VMEM),
        scratch_shapes=[
            pltpu.VMEM((2, *out.shape), BF16),
            pltpu.VMEM(img_proj.shape, BF16),
            pltpu.SemaphoreType.DMA((4,)),
        ],
        compiler_params=params(mib),
        name=name,
    )(place, *text_side, *image_side, txt_proj, img_proj)


def second_kernel(place, *refs):
    sides, (unit, inverse, z, weight, emb_t, emb_v, sems) = (refs[:3], refs[3:6]), refs[6:]
    rows = emb_v.shape[1]
    for side in range(2):

        @pl.when(place[SIDE] == side)
        def _():
            copies = [
                pltpu.make_async_copy(src, dst, sems.at[at])
                for at, (src, dst) in enumerate(
                    zip(sides[side], (weight, emb_v.at[1 - place[SAME]], emb_v.at[place[SAME]]))
                )
            ]
            for copy in copies:
                copy.start()
            for copy in copies:
                copy.wait()

    for half in range(2):
        here = slice(half * rows, (half + 1) * rows)
        raw = dot(emb_v[half], weight[...])
        scale = lax.rsqrt(jnp.sum(raw * raw, axis=1, keepdims=True) + 1e-06)
        inverse[here, :] = scale
        units = raw * scale
        unit[here, :] = units
        z[here, :] = units.astype(BF16)
        emb_t[:, here] = emb_v[half].T


def second_units(place, img_emb, txt_emb, img_other, txt_other, img_proj, txt_proj):
    rows, columns = img_emb.shape
    return pl.pallas_call(
        second_kernel,
        out_shape=(
            jax.ShapeDtypeStruct((2 * rows, columns), F32),
            jax.ShapeDtypeStruct((2 * rows, 1), F32),
            jax.ShapeDtypeStruct((2 * rows, columns), BF16),
            jax.ShapeDtypeStruct(img_proj.shape, BF16),
            jax.ShapeDtypeStruct((columns, 2 * rows), BF16),
        ),
        in_specs=[SMEM] + [HBM] * 6,
        out_specs=(VMEM,) * 5,
        scratch_shapes=[
            pltpu.VMEM((2, rows, columns), BF16),
            pltpu.SemaphoreType.DMA((3,)),
        ],
        compiler_params=params(18),
        name="second_units",
    )(place, img_proj, img_emb, img_other, txt_proj, txt_emb, txt_other)


def piece_at(digit, m, height, first=0):
    return pl.ds(pl.multiple_of(first + (digit ^ m) * height, 8), height)


def pick_kernel(at, place, *refs):
    sources, outs, sems = (refs[:2], refs[2:4]), refs[4:6], refs[6]
    for flag in range(2):

        @pl.when(place[at] == flag)
        def _():
            copies = [
                pltpu.make_async_copy(pair[flag], out, sems.at[k])
                for k, (pair, out) in enumerate(zip(sources, outs))
            ]
            for copy in copies:
                copy.start()
            for copy in copies:
                copy.wait()


def pick(place, at, first, second, name):
    return pl.pallas_call(
        functools.partial(pick_kernel, at),
        out_shape=tuple(jax.ShapeDtypeStruct(p[0].shape, p[0].dtype) for p in (first, second)),
        in_specs=[SMEM] + [ANY] * 4,
        out_specs=(ANY, ANY),
        scratch_shapes=[pltpu.SemaphoreType.DMA((2,))],
        compiler_params=params(1),
        name=name,
    )(place, *first, *second)


def pair_term(z, block, scale, bias, diagonal):
    half = dot_t(z, block) * (0.5 * scale) + 0.5 * bias
    coef = 0.5 * jnp.tanh(half) + 0.5
    if diagonal is not None:
        row_at = lax.broadcasted_iota(jnp.int32, coef.shape, 0) + diagonal
        col_at = lax.broadcasted_iota(jnp.int32, coef.shape, 1)
        coef = jnp.where(row_at == col_at, coef - 1.0, coef)
    return dot(coef.astype(BF16), block)


def own_chip_kernel(scale, bias, z, met, met_other, grad):
    step = pl.program_id(0)
    per_block = met.shape[0] // TILE
    here = step * TILE
    near = pair_term(z[...], met[...], scale[0], bias[0], here)
    other = pair_term(z[...], met_other[...], scale[0], bias[0], here - per_block * TILE)
    grad[...] = near + other


def first_phase_kernel(scale, bias, z, one, two, far_own, far_other, grad_in, grad):
    step = pl.program_id(0)
    per_block = one.shape[0] // TILE
    total = grad_in[...] + pair_term(z[...], one[...], scale[0], bias[0], None)
    total = total + pair_term(z[...], two[...], scale[0], bias[0], None)

    @pl.when(step < per_block)
    def _():
        grad[...] = total + pair_term(z[...], far_own[...], scale[0], bias[0], None)

    @pl.when(step >= per_block)
    def _():
        grad[...] = total + pair_term(z[...], far_other[...], scale[0], bias[0], None)


def row_tiles(columns):
    return pl.BlockSpec((TILE, columns), lambda i: (i, 0))


def whole(array):
    return pl.BlockSpec(
        array.shape, lambda i: (0,) * len(array.shape), pipeline_mode=pl.Buffered(1)
    )


def call_tiles(kernel, scale, bias, z, blocks, grads, name, mib):
    rows, columns = z.shape
    return pl.pallas_call(
        kernel,
        grid=(rows // TILE,),
        out_shape=jax.ShapeDtypeStruct((rows, columns), F32),
        in_specs=[SMEM, SMEM, row_tiles(columns)]
        + [whole(b) for b in blocks]
        + [row_tiles(columns)] * len(grads),
        out_specs=row_tiles(columns),
        compiler_params=params(mib),
        name=name,
    )(scale, bias, z, *blocks, *grads)


def last_phase_kernel(
    place, scale, bias, z, one, two, grad_in, unit, inverse, emb_t, du, *rest
):
    half, (du_all, emb_v, sem) = rest[0], rest[1:]
    step = pl.program_id(0)
    fetch = pltpu.make_async_copy(emb_t, emb_v, sem)

    @pl.when(step == 0)
    def _():
        fetch.start()

    grad = grad_in[...] + pair_term(z[...], one[...], scale[0], bias[0], None)
    grad = scale[0] * (grad + pair_term(z[...], two[...], scale[0], bias[0], None))
    units = unit[...]
    inner = jnp.sum(units * grad, axis=1, keepdims=True)
    rounded = ((grad - units * inner) * inverse[...]).astype(BF16)
    du[...] = rounded
    du_all[pl.ds(pl.multiple_of(step * TILE, TILE), TILE), :] = rounded

    @pl.when(step == pl.num_programs(0) - 1)
    def _():
        fetch.wait()
        height = half.shape[0]
        first = emb_v.shape[0] - 2 * height
        rows = piece_at(place[Z_LOW], 1, height, first)
        half[...] = dot(emb_v[rows, :], du_all[...]).astype(BF16)


def last_phase(place, scale, bias, z, one, two, grad, unit, inverse, emb_t):
    rows, columns = z.shape
    half = jax.ShapeDtypeStruct((columns // 6, columns), BF16)
    return pl.pallas_call(
        last_phase_kernel,
        grid=(rows // TILE,),
        out_shape=(jax.ShapeDtypeStruct((rows, columns), BF16), half),
        in_specs=[
            SMEM,
            SMEM,
            SMEM,
            row_tiles(columns),
            whole(one),
            whole(two),
            row_tiles(columns),
            row_tiles(columns),
            row_tiles(1),
            HBM,
        ],
        out_specs=(row_tiles(columns), whole(half)),
        scratch_shapes=[
            pltpu.VMEM((rows, columns), BF16),
            pltpu.VMEM(emb_t.shape, BF16),
            pltpu.SemaphoreType.DMA,
        ],
        compiler_params=params(28),
        name="last_phase",
    )(place, scale, bias, z, one, two, grad, unit, inverse, emb_t)


def other_parts_kernel(place, emb_t, du, keep_b, *pieces):
    height = keep_b.shape[0]
    for m, out in enumerate(pieces):
        rows = piece_at(place[IN_PLANE], m, height)
        out[...] = dot(emb_t[rows, :], du[...]).astype(out.dtype)
    rows = piece_at(place[Z_LOW], 0, height, emb_t.shape[0] - 2 * height)
    keep_b[...] = dot(emb_t[rows, :], du[...])


def other_parts(place, emb_t, du):
    shape = (emb_t.shape[0] // 6, emb_t.shape[0])
    kinds = [F32, F32, BF16, BF16, BF16]
    return pl.pallas_call(
        other_parts_kernel,
        out_shape=tuple(jax.ShapeDtypeStruct(shape, kind) for kind in kinds),
        in_specs=[SMEM] + [VMEM] * 2,
        out_specs=(VMEM,) * 5,
        compiler_params=params(8),
        name="other_parts",
    )(place, emb_t, du)


def rows_back_kernel(place, du, weight, own, other):
    back = dot_t(du[...], weight[...]).astype(BF16)
    mine = pl.program_id(0) == 1 - place[SAME]

    @pl.when(mine)
    def _():
        own[...] = back

    @pl.when(jnp.logical_not(mine))
    def _():
        other[...] = back


def rows_back(place, du, weight):
    rows, columns = du.shape
    out = jax.ShapeDtypeStruct((TILE, columns), BF16)
    return pl.pallas_call(
        rows_back_kernel,
        grid=(rows // TILE,),
        out_shape=(out, out),
        in_specs=[SMEM, row_tiles(columns), whole(weight)],
        out_specs=(whole(out), whole(out)),
        compiler_params=params(8),
        name="rows_back",
    )(place, du, weight)


def summed(refs):
    one, two, three, four = (ref[...].astype(F32) for ref in refs)
    return (one + two) + (three + four)


def small_call(kernel, place, arrays, outs, scratch, mib, name):
    return pl.pallas_call(
        kernel,
        out_shape=tuple(jax.ShapeDtypeStruct(shape, kind) for shape, kind in outs),
        in_specs=[SMEM] + [VMEM] * len(arrays),
        out_specs=(VMEM,) * len(outs),
        scratch_shapes=[pltpu.VMEM(shape, F32) for shape in scratch],
        compiler_params=params(mib),
        name=name,
    )(place, *arrays)


def add_split_kernel(place, *refs):
    total = refs[8]
    total[...] = summed(refs[:4])
    for m, out in enumerate(refs[4:8]):
        out[...] = total[piece_at(place[IN_LINE], m, out.shape[0]), :].astype(out.dtype)


def add_split(place, parts, name):
    rows, columns = parts[0].shape
    outs = [((rows // 4, columns), F32 if m == 0 else BF16) for m in range(4)]
    return small_call(add_split_kernel, place, parts, outs, [(rows, columns)], 4, name)


def add_all_kernel(place, *refs):
    refs[4][...] = summed(refs[:4]).astype(BF16)


def add_all(place, parts, name):
    return small_call(add_all_kernel, place, parts, [(parts[0].shape, BF16)], [], 2, name)[0]


def join_four_kernel(digit, place, *refs):
    out, total = refs[4:]
    for m, piece in enumerate(refs[:4]):
        total[piece_at(place[digit], m, piece.shape[0]), :] = piece[...].astype(F32)
    out[...] = total[...].astype(BF16)


def join_four(place, digit, parts, name):
    shape = (4 * parts[0].shape[0], parts[0].shape[1])
    kernel = functools.partial(join_four_kernel, digit)
    return small_call(kernel, place, parts, [(shape, BF16)], [shape], 7, name)[0]


def add_halve_kernel(bit, place, keep, got, mine, give, total):
    total[...] = keep[...] + got[...].astype(F32)
    for m, out in enumerate((mine, give)):
        out[...] = total[piece_at(place[bit], m, out.shape[0]), :].astype(out.dtype)


def add_halve(place, bit, keep, got, name):
    rows, columns = keep.shape
    outs = [((rows // 2, columns), kind) for kind in (F32, BF16)]
    kernel = functools.partial(add_halve_kernel, bit)
    return small_call(kernel, place, [keep, got], outs, [keep.shape], 3, name)


def add_two_kernel(place, keep, got, out):
    out[...] = (keep[...] + got[...].astype(F32)).astype(BF16)


def add_two(place, keep, got, name):
    return small_call(add_two_kernel, place, [keep, got], [(keep.shape, BF16)], [], 2, name)[0]


def join_two_kernel(bit, place, mine, got, out, total):
    for m, piece in enumerate((mine, got)):
        total[piece_at(place[bit], m, piece.shape[0]), :] = piece[...].astype(F32)
    out[...] = total[...].astype(BF16)


def join_two(place, bit, mine, got, name):
    shape = (2 * mine.shape[0], mine.shape[1])
    kernel = functools.partial(join_two_kernel, bit)
    return small_call(kernel, place, [mine, got], [(shape, BF16)], [shape], 5, name)[0]


def join_all_kernel(place, *refs):
    out = refs[6]
    for m, piece in enumerate(refs[:4]):
        out[piece_at(place[IN_PLANE], m, piece.shape[0]), :] = piece[...]
    height = refs[4].shape[0]
    for m, piece in enumerate(refs[4:6]):
        out[piece_at(place[Z_LOW], m, height, out.shape[0] - 2 * height), :] = piece[...]


def join_all(place, parts_a, parts_b):
    columns = parts_b[0].shape[1]
    arrays = [*parts_a, *parts_b]
    outs = [((columns, columns), BF16)]
    return small_call(join_all_kernel, place, arrays, outs, [], 3, "join_all")[0]


def widen_kernel(own, place, weight, *refs):
    img_out, txt_out, wide, sems = refs[-4:]
    count = sems.shape[0]
    height = weight.shape[0] // count
    for side, out in enumerate((img_out, txt_out)):

        @pl.when((place[SIDE] == side) == own)
        def _():
            copies = []
            for k in range(count):
                part = slice(k * height, (k + 1) * height)
                wide[part, :] = weight[part, :].astype(F32)
                copies.append(
                    pltpu.make_async_copy(wide.at[part, :], out.at[part, :], sems.at[k])
                )
                copies[-1].start()
            for copy in copies:
                copy.wait()


def widen(place, weight, own, outs, name):
    out = jax.ShapeDtypeStruct(weight.shape, F32)
    return pl.pallas_call(
        functools.partial(widen_kernel, own),
        out_shape=(out, out),
        in_specs=[SMEM, VMEM] + [ANY] * len(outs),
        out_specs=(ANY, ANY),
        scratch_shapes=[pltpu.VMEM(weight.shape, F32), pltpu.SemaphoreType.DMA((9,))],
        input_output_aliases={2: 0, 3: 1} if outs else {},
        compiler_params=params(9),
        name=name,
    )(place, weight, *outs)


def body(img_emb, txt_emb, img_proj, txt_proj, log_scale, bias):
    size = lax.axis_size("dp")
    columns = img_emb.shape[1]
    scale = jnp.exp(log_scale)
    here = lax.axis_index("dp").astype(jnp.int32)
    side, chip = here % 2, here // 2
    bits = [(chip // n) % 2 for n in (1, 2, 4, 8)]
    place = jnp.stack([side, chip % 4, (chip // 4) % 4, (chip + side + 1) % 2, *bits])
    place, scale = lax.optimization_barrier((place, scale))

    pair = lambda value: swap(value, size, 2)
    far_as_d = lambda value: shift(value, size, lambda chip, core: -2 if chip % 2 else 2)
    far_as_s = lambda value: shift(value, size, lambda chip, core: 2 if chip % 2 else -2)

    def raw_target(to_pair, to_far):
        pairs = []
        for i in range(size):
            chip, core = i // 2, i % 2
            if core == chip % 2:
                pairs.append((i, 2 * (chip ^ 1) + to_pair))
            else:
                pairs.append((i, 2 * ((chip - 2 if core == 0 else chip + 2) % (size // 2)) + to_far))
        return pairs

    raw_one, raw_two = raw_blocks(place, img_emb, txt_emb)
    got_one = lax.ppermute(raw_one, "dp", raw_target(0, 1))
    got_two = lax.ppermute(raw_two, "dp", raw_target(1, 0))
    img_other, txt_other, _ = lax.optimization_barrier(
        (swap(img_emb, size, 1), swap(txt_emb, size, 1), raw_one)
    )
    met_s, met_d = met_units(
        place,
        (txt_emb, txt_other),
        (img_emb, img_other),
        img_proj,
        txt_proj,
        True,
        58,
        "own_met",
    )
    pair_d, far_s = pair(met_d), far_as_s(met_s)

    img_emb, txt_emb, img_other, txt_other, _ = lax.optimization_barrier(
        (img_emb, txt_emb, img_other, txt_other, met_s)
    )
    unit, inverse, z, weight, emb_t = second_units(
        place, img_emb, txt_emb, img_other, txt_other, img_proj, txt_proj
    )
    grad = call_tiles(own_chip_kernel, scale, bias, z, (met_s, met_d), (), "own_chip", 8)
    got_one, got_two, pair_d, far_s, grad, emb_t = lax.optimization_barrier(
        (got_one, got_two, pair_d, far_s, grad, emb_t)
    )
    relay_far, relay_pair = pair(far_s), far_as_d(pair_d)
    pair_s, far_d = met_units(
        place,
        (got_one, got_two),
        (got_two, got_one),
        img_proj,
        txt_proj,
        False,
        14,
        "raw_met",
    )
    grad = call_tiles(
        first_phase_kernel,
        scale,
        bias,
        z,
        (pair_s, pair_d, far_d, far_s),
        (grad,),
        "first_phase",
        12,
    )

    du, give_b = last_phase(
        place, scale, bias, z, relay_far, relay_pair, grad, unit, inverse, emb_t
    )

    def exchange(sends, masks):
        return [swap(s, size, m) for s, m in zip(sends, masks)]

    plane_masks, line_masks = (2, 4, 6), (8, 16, 24)
    x_bit, y_bit, low_bit, high_bit = (X, 2), (Y, 4), (Z_LOW, 8), (Z_HIGH, 16)

    def halve(keep, got, bit, name):
        keep, give = add_halve(place, bit[0], keep, got, name)
        return keep, swap(give, size, bit[1]), give

    def gather(mine, bit):
        return mine, swap(mine, size, bit[1])

    together = lax.optimization_barrier
    got_b = swap(give_b, size, low_bit[1])
    keep_b, *pieces = other_parts(place, emb_t, du)
    parts_a = [pieces[0], *exchange(pieces[1:], plane_masks)]
    keep_b, got_b, give_b = halve(keep_b, got_b, high_bit, "b_high")
    du, _ = together((du, give_b))
    d_emb, d_emb_send = rows_back(place, du, weight)
    parts_a, got_b, d_emb_send = together((parts_a, got_b, d_emb_send))
    d_emb_other = swap(d_emb_send, size, 1)
    pieces = add_split(place, parts_a, "a_split")
    parts_a = [pieces[0], *exchange(pieces[:0:-1], line_masks[::-1])]
    keep_b, got_b, _ = halve(keep_b, got_b, x_bit, "b_x")
    d_img_emb, d_txt_emb = pick(
        place, SIDE, (d_emb, d_emb_other), (d_emb_other, d_emb), "rows_pick"
    )
    keep_b, got_b, give_b = halve(keep_b, got_b, y_bit, "b_y")
    parts_a, d_img_emb, d_txt_emb, _ = together((parts_a, d_img_emb, d_txt_emb, give_b))

    parts_a, got_b = together((parts_a, got_b))
    shard_a = add_all(place, parts_a, "a_last")
    shard_b = add_two(place, keep_b, got_b, "b_last")
    if size > 32:
        groups = [[i for i in range(size) if i % 32 == k] for k in range(32)]
        shard_a, shard_b = lax.psum((shard_a, shard_b), "dp", axis_index_groups=groups)
    parts_a = [shard_a, *exchange([shard_a] * 3, line_masks)]
    shard_b = join_two(place, y_bit[0], *gather(shard_b, y_bit), "b_join_y")
    got_b = swap(shard_b, size, x_bit[1])
    parts_a, _ = together((parts_a, shard_b))

    parts_a, got_b = together((parts_a, got_b))
    piece_a = join_four(place, IN_LINE, parts_a, "a_join")
    parts_a = [piece_a, *exchange([piece_a] * 3, plane_masks)]
    shard_b = join_two(place, x_bit[0], shard_b, got_b, "b_join_x")
    shard_b = join_two(place, high_bit[0], *gather(shard_b, high_bit), "b_join_high")
    got_b = swap(shard_b, size, low_bit[1])
    parts_a, got_b = together((parts_a, got_b))

    d_weight = join_all(place, parts_a, (shard_b, got_b))
    d_weight_other = swap(d_weight, size, 1)
    outs = widen(place, d_weight, True, (), "widen_own")
    d_img_proj, d_txt_proj = widen(place, d_weight_other, False, outs, "widen_other")
    return (d_img_emb, d_txt_emb, d_img_proj, d_txt_proj)


def solution(mesh):
    return jax.shard_map(
        body,
        mesh=mesh,
        in_specs=(P("dp", None), P("dp", None), P(), P(), P(), P()),
        out_specs=(P("dp", None), P("dp", None), P(), P()),
        check_vma=False,
    )
```

```python
import functools

import jax
import jax.numpy as jnp
from jax import lax
from jax.experimental import pallas as pl
from jax.experimental.pallas import tpu as pltpu
from jax.sharding import PartitionSpec as P

REACH = 3
BF16, F32 = jnp.bfloat16, jnp.float32
TILE = 512
SIDE, IN_PLANE, IN_LINE, SAME, X, Y, Z_LOW, Z_HIGH = range(8)
VMEM = pl.BlockSpec(memory_space=pltpu.VMEM)
SMEM = pl.BlockSpec(memory_space=pltpu.SMEM)
HBM = pl.BlockSpec(memory_space=pltpu.HBM)
ANY = pl.BlockSpec(memory_space=pl.ANY)


def params(mib):
    return pltpu.CompilerParams(vmem_limit_bytes=mib * 1024 * 1024)


def dot_t(left, right):
    return lax.dot_general(left, right, (((1,), (1,)), ((), ())), preferred_element_type=F32)


def dot(left, right):
    return lax.dot_general(left, right, (((1,), (0,)), ((), ())), preferred_element_type=F32)


def shift(value, size, chips):
    pairs = []
    for i in range(size):
        chip, core = i // 2, i % 2
        pairs.append((i, 2 * ((chip + chips(chip, core)) % (size // 2)) + core))
    return lax.ppermute(value, "dp", pairs)


def swap(value, size, mask):
    return lax.ppermute(value, "dp", [(i, i ^ mask) for i in range(size)])


def raw_kernel(place, img_emb, txt_emb, one, two, sems):
    for same, pair in enumerate(((img_emb, txt_emb), (txt_emb, img_emb))):

        @pl.when(place[SAME] == same)
        def _():
            copies = [
                pltpu.make_async_copy(src, dst, sems.at[k])
                for k, (src, dst) in enumerate(zip(pair, (one, two)))
            ]
            for copy in copies:
                copy.start()
            for copy in copies:
                copy.wait()


def raw_blocks(place, img_emb, txt_emb):
    out = jax.ShapeDtypeStruct(img_emb.shape, BF16)
    return pl.pallas_call(
        raw_kernel,
        out_shape=(out, out),
        in_specs=[SMEM] + [HBM] * 2,
        out_specs=(VMEM, VMEM),
        scratch_shapes=[pltpu.SemaphoreType.DMA((2,))],
        compiler_params=params(58),
        name="raw_blocks",
    )(place, img_emb, txt_emb)


def met_kernel(own_chip, place, *refs):
    sides, projs, (z_one, z_two, emb_v, proj_v, sems) = (refs[:2], refs[2:4]), refs[4:6], refs[6:]
    cut = proj_v.shape[0] // 256 * 128 + 128
    parts = [slice(0, cut), slice(cut, proj_v.shape[0])]
    for side, (embs, proj) in enumerate(zip(sides, projs)):

        @pl.when(place[SIDE] == side)
        def _():
            first = 1 - place[SAME] if own_chip else 0
            copies = [pltpu.make_async_copy(embs[0], emb_v.at[first], sems.at[2])]
            for k, part in enumerate(parts):
                copies.append(
                    pltpu.make_async_copy(proj.at[part, :], proj_v.at[part, :], sems.at[k])
                )
            copies.append(pltpu.make_async_copy(embs[1], emb_v.at[1 - first], sems.at[3]))
            for copy in copies:
                copy.start()
            for copy in copies:
                copy.wait()

    for k, z in enumerate((z_one, z_two)):
        raw = dot(emb_v[k], proj_v[...])
        scale = lax.rsqrt(jnp.sum(raw * raw, axis=1, keepdims=True) + 1e-06)
        z[...] = (raw * scale).astype(BF16)


def met_units(place, text_side, image_side, img_proj, txt_proj, own_chip, mib, name):
    out = jax.ShapeDtypeStruct(text_side[0].shape, BF16)
    return pl.pallas_call(
        functools.partial(met_kernel, own_chip),
        out_shape=(out, out),
        in_specs=[SMEM] + [HBM] * 6,
        out_specs=(VMEM, VMEM),
        scratch_shapes=[
            pltpu.VMEM((2, *out.shape), BF16),
            pltpu.VMEM(img_proj.shape, BF16),
            pltpu.SemaphoreType.DMA((4,)),
        ],
        compiler_params=params(mib),
        name=name,
    )(place, *text_side, *image_side, txt_proj, img_proj)


def second_kernel(place, *refs):
    sides, (unit, inverse, z, weight, emb_t, emb_v, sems) = (refs[:3], refs[3:6]), refs[6:]
    rows = emb_v.shape[1]
    for side in range(2):

        @pl.when(place[SIDE] == side)
        def _():
            copies = [
                pltpu.make_async_copy(src, dst, sems.at[at])
                for at, (src, dst) in enumerate(
                    zip(sides[side], (weight, emb_v.at[1 - place[SAME]], emb_v.at[place[SAME]]))
                )
            ]
            for copy in copies:
                copy.start()
            for copy in copies:
                copy.wait()

    for half in range(2):
        here = slice(half * rows, (half + 1) * rows)
        raw = dot(emb_v[half], weight[...])
        scale = lax.rsqrt(jnp.sum(raw * raw, axis=1, keepdims=True) + 1e-06)
        inverse[here, :] = scale
        units = raw * scale
        unit[here, :] = units
        z[here, :] = units.astype(BF16)
        emb_t[:, here] = emb_v[half].T


def second_units(place, img_emb, txt_emb, img_other, txt_other, img_proj, txt_proj):
    rows, columns = img_emb.shape
    return pl.pallas_call(
        second_kernel,
        out_shape=(
            jax.ShapeDtypeStruct((2 * rows, columns), F32),
            jax.ShapeDtypeStruct((2 * rows, 1), F32),
            jax.ShapeDtypeStruct((2 * rows, columns), BF16),
            jax.ShapeDtypeStruct(img_proj.shape, BF16),
            jax.ShapeDtypeStruct((columns, 2 * rows), BF16),
        ),
        in_specs=[SMEM] + [HBM] * 6,
        out_specs=(VMEM,) * 5,
        scratch_shapes=[
            pltpu.VMEM((2, rows, columns), BF16),
            pltpu.SemaphoreType.DMA((3,)),
        ],
        compiler_params=params(18),
        name="second_units",
    )(place, img_proj, img_emb, img_other, txt_proj, txt_emb, txt_other)


def piece_at(digit, m, height, first=0):
    return pl.ds(pl.multiple_of(first + (digit ^ m) * height, 8), height)


def pick_kernel(at, place, *refs):
    sources, outs, sems = (refs[:2], refs[2:4]), refs[4:6], refs[6]
    for flag in range(2):

        @pl.when(place[at] == flag)
        def _():
            copies = [
                pltpu.make_async_copy(pair[flag], out, sems.at[k])
                for k, (pair, out) in enumerate(zip(sources, outs))
            ]
            for copy in copies:
                copy.start()
            for copy in copies:
                copy.wait()


def pick(place, at, first, second, name):
    return pl.pallas_call(
        functools.partial(pick_kernel, at),
        out_shape=tuple(jax.ShapeDtypeStruct(p[0].shape, p[0].dtype) for p in (first, second)),
        in_specs=[SMEM] + [ANY] * 4,
        out_specs=(ANY, ANY),
        scratch_shapes=[pltpu.SemaphoreType.DMA((2,))],
        compiler_params=params(1),
        name=name,
    )(place, *first, *second)


def pair_term(z, block, scale, bias, diagonal):
    half = dot_t(z, block) * (0.5 * scale) + 0.5 * bias
    coef = 0.5 * jnp.tanh(half) + 0.5
    if diagonal is not None:
        row_at = lax.broadcasted_iota(jnp.int32, coef.shape, 0) + diagonal
        col_at = lax.broadcasted_iota(jnp.int32, coef.shape, 1)
        coef = jnp.where(row_at == col_at, coef - 1.0, coef)
    return dot(coef.astype(BF16), block)


def own_chip_kernel(scale, bias, z, met, met_other, grad):
    step = pl.program_id(0)
    per_block = met.shape[0] // TILE
    here = step * TILE
    near = pair_term(z[...], met[...], scale[0], bias[0], here)
    other = pair_term(z[...], met_other[...], scale[0], bias[0], here - per_block * TILE)
    grad[...] = near + other


def first_phase_kernel(scale, bias, z, one, two, far_own, far_other, grad_in, grad):
    step = pl.program_id(0)
    per_block = one.shape[0] // TILE
    total = grad_in[...] + pair_term(z[...], one[...], scale[0], bias[0], None)
    total = total + pair_term(z[...], two[...], scale[0], bias[0], None)

    @pl.when(step < per_block)
    def _():
        grad[...] = total + pair_term(z[...], far_own[...], scale[0], bias[0], None)

    @pl.when(step >= per_block)
    def _():
        grad[...] = total + pair_term(z[...], far_other[...], scale[0], bias[0], None)


def row_tiles(columns):
    return pl.BlockSpec((TILE, columns), lambda i: (i, 0))


def whole(array):
    return pl.BlockSpec(
        array.shape, lambda i: (0,) * len(array.shape), pipeline_mode=pl.Buffered(1)
    )


def call_tiles(kernel, scale, bias, z, blocks, grads, name, mib):
    rows, columns = z.shape
    return pl.pallas_call(
        kernel,
        grid=(rows // TILE,),
        out_shape=jax.ShapeDtypeStruct((rows, columns), F32),
        in_specs=[SMEM, SMEM, row_tiles(columns)]
        + [whole(b) for b in blocks]
        + [row_tiles(columns)] * len(grads),
        out_specs=row_tiles(columns),
        compiler_params=params(mib),
        name=name,
    )(scale, bias, z, *blocks, *grads)


def last_phase_kernel(
    place, scale, bias, z, one, two, grad_in, unit, inverse, emb_t, du, *rest
):
    half, (du_all, emb_v, sem) = rest[0], rest[1:]
    step = pl.program_id(0)
    fetch = pltpu.make_async_copy(emb_t, emb_v, sem)

    @pl.when(step == 0)
    def _():
        fetch.start()

    grad = grad_in[...] + pair_term(z[...], one[...], scale[0], bias[0], None)
    grad = scale[0] * (grad + pair_term(z[...], two[...], scale[0], bias[0], None))
    units = unit[...]
    inner = jnp.sum(units * grad, axis=1, keepdims=True)
    rounded = ((grad - units * inner) * inverse[...]).astype(BF16)
    du[...] = rounded
    du_all[pl.ds(pl.multiple_of(step * TILE, TILE), TILE), :] = rounded

    @pl.when(step == pl.num_programs(0) - 1)
    def _():
        fetch.wait()
        height = half.shape[0]
        first = emb_v.shape[0] - 2 * height
        rows = piece_at(place[Z_LOW], 1, height, first)
        half[...] = dot(emb_v[rows, :], du_all[...]).astype(BF16)


def last_phase(place, scale, bias, z, one, two, grad, unit, inverse, emb_t):
    rows, columns = z.shape
    half = jax.ShapeDtypeStruct((columns // 6, columns), BF16)
    return pl.pallas_call(
        last_phase_kernel,
        grid=(rows // TILE,),
        out_shape=(jax.ShapeDtypeStruct((rows, columns), BF16), half),
        in_specs=[
            SMEM,
            SMEM,
            SMEM,
            row_tiles(columns),
            whole(one),
            whole(two),
            row_tiles(columns),
            row_tiles(columns),
            row_tiles(1),
            HBM,
        ],
        out_specs=(row_tiles(columns), whole(half)),
        scratch_shapes=[
            pltpu.VMEM((rows, columns), BF16),
            pltpu.VMEM(emb_t.shape, BF16),
            pltpu.SemaphoreType.DMA,
        ],
        compiler_params=params(28),
        name="last_phase",
    )(place, scale, bias, z, one, two, grad, unit, inverse, emb_t)


def other_parts_kernel(place, emb_t, du, keep_b, *pieces):
    height = keep_b.shape[0]
    for m, out in enumerate(pieces):
        rows = piece_at(place[IN_PLANE], m, height)
        out[...] = dot(emb_t[rows, :], du[...]).astype(out.dtype)
    rows = piece_at(place[Z_LOW], 0, height, emb_t.shape[0] - 2 * height)
    keep_b[...] = dot(emb_t[rows, :], du[...])


def other_parts(place, emb_t, du):
    shape = (emb_t.shape[0] // 6, emb_t.shape[0])
    kinds = [F32, F32, BF16, BF16, BF16]
    return pl.pallas_call(
        other_parts_kernel,
        out_shape=tuple(jax.ShapeDtypeStruct(shape, kind) for kind in kinds),
        in_specs=[SMEM] + [VMEM] * 2,
        out_specs=(VMEM,) * 5,
        compiler_params=params(8),
        name="other_parts",
    )(place, emb_t, du)


def rows_back_kernel(place, du, weight, own, other):
    back = dot_t(du[...], weight[...]).astype(BF16)
    mine = pl.program_id(0) == 1 - place[SAME]

    @pl.when(mine)
    def _():
        own[...] = back

    @pl.when(jnp.logical_not(mine))
    def _():
        other[...] = back


def rows_back(place, du, weight):
    rows, columns = du.shape
    out = jax.ShapeDtypeStruct((TILE, columns), BF16)
    return pl.pallas_call(
        rows_back_kernel,
        grid=(rows // TILE,),
        out_shape=(out, out),
        in_specs=[SMEM, row_tiles(columns), whole(weight)],
        out_specs=(whole(out), whole(out)),
        compiler_params=params(8),
        name="rows_back",
    )(place, du, weight)


def summed(refs):
    one, two, three, four = (ref[...].astype(F32) for ref in refs)
    return (one + two) + (three + four)


def small_call(kernel, place, arrays, outs, scratch, mib, name):
    return pl.pallas_call(
        kernel,
        out_shape=tuple(jax.ShapeDtypeStruct(shape, kind) for shape, kind in outs),
        in_specs=[SMEM] + [VMEM] * len(arrays),
        out_specs=(VMEM,) * len(outs),
        scratch_shapes=[pltpu.VMEM(shape, F32) for shape in scratch],
        compiler_params=params(mib),
        name=name,
    )(place, *arrays)


def add_split_kernel(place, *refs):
    total = refs[8]
    total[...] = summed(refs[:4])
    for m, out in enumerate(refs[4:8]):
        out[...] = total[piece_at(place[IN_LINE], m, out.shape[0]), :].astype(out.dtype)


def add_split(place, parts, name):
    rows, columns = parts[0].shape
    outs = [((rows // 4, columns), F32 if m == 0 else BF16) for m in range(4)]
    return small_call(add_split_kernel, place, parts, outs, [(rows, columns)], 4, name)


def add_all_kernel(place, *refs):
    refs[4][...] = summed(refs[:4]).astype(BF16)


def add_all(place, parts, name):
    return small_call(add_all_kernel, place, parts, [(parts[0].shape, BF16)], [], 2, name)[0]


def join_four_kernel(digit, place, *refs):
    out, total = refs[4:]
    for m, piece in enumerate(refs[:4]):
        total[piece_at(place[digit], m, piece.shape[0]), :] = piece[...].astype(F32)
    out[...] = total[...].astype(BF16)


def join_four(place, digit, parts, name):
    shape = (4 * parts[0].shape[0], parts[0].shape[1])
    kernel = functools.partial(join_four_kernel, digit)
    return small_call(kernel, place, parts, [(shape, BF16)], [shape], 7, name)[0]


def add_halve_kernel(bit, place, keep, got, mine, give, total):
    total[...] = keep[...] + got[...].astype(F32)
    for m, out in enumerate((mine, give)):
        out[...] = total[piece_at(place[bit], m, out.shape[0]), :].astype(out.dtype)


def add_halve(place, bit, keep, got, name):
    rows, columns = keep.shape
    outs = [((rows // 2, columns), kind) for kind in (F32, BF16)]
    kernel = functools.partial(add_halve_kernel, bit)
    return small_call(kernel, place, [keep, got], outs, [keep.shape], 3, name)


def add_two_kernel(place, keep, got, out):
    out[...] = (keep[...] + got[...].astype(F32)).astype(BF16)


def add_two(place, keep, got, name):
    return small_call(add_two_kernel, place, [keep, got], [(keep.shape, BF16)], [], 2, name)[0]


def join_two_kernel(bit, place, mine, got, out, total):
    for m, piece in enumerate((mine, got)):
        total[piece_at(place[bit], m, piece.shape[0]), :] = piece[...].astype(F32)
    out[...] = total[...].astype(BF16)


def join_two(place, bit, mine, got, name):
    shape = (2 * mine.shape[0], mine.shape[1])
    kernel = functools.partial(join_two_kernel, bit)
    return small_call(kernel, place, [mine, got], [(shape, BF16)], [shape], 5, name)[0]


def join_all_kernel(place, *refs):
    out = refs[6]
    for m, piece in enumerate(refs[:4]):
        out[piece_at(place[IN_PLANE], m, piece.shape[0]), :] = piece[...]
    height = refs[4].shape[0]
    for m, piece in enumerate(refs[4:6]):
        out[piece_at(place[Z_LOW], m, height, out.shape[0] - 2 * height), :] = piece[...]


def join_all(place, parts_a, parts_b):
    columns = parts_b[0].shape[1]
    arrays = [*parts_a, *parts_b]
    outs = [((columns, columns), BF16)]
    return small_call(join_all_kernel, place, arrays, outs, [], 3, "join_all")[0]


def widen_kernel(own, place, weight, *refs):
    img_out, txt_out, wide, sems = refs[-4:]
    count = sems.shape[0]
    height = weight.shape[0] // count
    for side, out in enumerate((img_out, txt_out)):

        @pl.when((place[SIDE] == side) == own)
        def _():
            copies = []
            for k in range(count):
                part = slice(k * height, (k + 1) * height)
                wide[part, :] = weight[part, :].astype(F32)
                copies.append(
                    pltpu.make_async_copy(wide.at[part, :], out.at[part, :], sems.at[k])
                )
                copies[-1].start()
            for copy in copies:
                copy.wait()


def widen(place, weight, own, outs, name):
    out = jax.ShapeDtypeStruct(weight.shape, F32)
    return pl.pallas_call(
        functools.partial(widen_kernel, own),
        out_shape=(out, out),
        in_specs=[SMEM, VMEM] + [ANY] * len(outs),
        out_specs=(ANY, ANY),
        scratch_shapes=[pltpu.VMEM(weight.shape, F32), pltpu.SemaphoreType.DMA((9,))],
        input_output_aliases={2: 0, 3: 1} if outs else {},
        compiler_params=params(9),
        name=name,
    )(place, weight, *outs)


def body(img_emb, txt_emb, img_proj, txt_proj, log_scale, bias):
    size = lax.axis_size("dp")
    columns = img_emb.shape[1]
    scale = jnp.exp(log_scale)
    here = lax.axis_index("dp").astype(jnp.int32)
    side, chip = here % 2, here // 2
    bits = [(chip // n) % 2 for n in (1, 2, 4, 8)]
    place = jnp.stack([side, chip % 4, (chip // 4) % 4, (chip + side + 1) % 2, *bits])
    place, scale = lax.optimization_barrier((place, scale))

    pair = lambda value: swap(value, size, 2)
    far_as_d = lambda value: shift(value, size, lambda chip, core: -2 if chip % 2 else 2)

    def raw_target(to_far, to_pair):
        pairs = []
        for i in range(size):
            chip, core = i // 2, i % 2
            if core == chip % 2:
                pairs.append((i, 2 * ((chip + 2 if core else chip - 2) % (size // 2)) + to_far))
            else:
                pairs.append((i, 2 * (chip ^ 1) + to_pair))
        return pairs

    raw_one, raw_two = raw_blocks(place, img_emb, txt_emb)
    got_one = lax.ppermute(raw_one, "dp", raw_target(0, 1))
    got_two = lax.ppermute(raw_two, "dp", raw_target(1, 0))
    img_other, txt_other, _ = lax.optimization_barrier(
        (swap(img_emb, size, 1), swap(txt_emb, size, 1), raw_one)
    )
    met_s, met_d = met_units(
        place,
        (txt_emb, txt_other),
        (img_emb, img_other),
        img_proj,
        txt_proj,
        True,
        58,
        "own_met",
    )
    pair_s, far_d = pair(met_s), far_as_d(met_d)

    img_emb, txt_emb, img_other, txt_other, _ = lax.optimization_barrier(
        (img_emb, txt_emb, img_other, txt_other, met_s)
    )
    unit, inverse, z, weight, emb_t = second_units(
        place, img_emb, txt_emb, img_other, txt_other, img_proj, txt_proj
    )
    grad = call_tiles(own_chip_kernel, scale, bias, z, (met_s, met_d), (), "own_chip", 8)
    got_one, got_two, _ = lax.optimization_barrier((got_one, got_two, (grad, emb_t)))
    pair_d, far_s = met_units(
        place,
        (got_two, got_one),
        (got_one, got_two),
        img_proj,
        txt_proj,
        False,
        14,
        "raw_met",
    )
    relay_far, relay_pair = pair(far_s), far_as_d(pair_d)
    pair_s, far_d, _ = lax.optimization_barrier((pair_s, far_d, (pair_d, far_s)))
    grad = call_tiles(
        first_phase_kernel,
        scale,
        bias,
        z,
        (pair_s, pair_d, far_d, far_s),
        (grad,),
        "first_phase",
        12,
    )

    du, give_b = last_phase(
        place, scale, bias, z, relay_far, relay_pair, grad, unit, inverse, emb_t
    )

    def exchange(sends, masks):
        return [swap(s, size, m) for s, m in zip(sends, masks)]

    plane_masks, line_masks = (2, 4, 6), (8, 16, 24)
    x_bit, y_bit, low_bit, high_bit = (X, 2), (Y, 4), (Z_LOW, 8), (Z_HIGH, 16)

    def halve(keep, got, bit, name):
        keep, give = add_halve(place, bit[0], keep, got, name)
        return keep, swap(give, size, bit[1]), give

    def gather(mine, bit):
        return mine, swap(mine, size, bit[1])

    together = lax.optimization_barrier
    got_b = swap(give_b, size, low_bit[1])
    keep_b, *pieces = other_parts(place, emb_t, du)
    parts_a = [pieces[0], *exchange(pieces[1:], plane_masks)]
    keep_b, got_b, give_b = halve(keep_b, got_b, high_bit, "b_high")
    du, _ = together((du, give_b))
    d_emb, d_emb_send = rows_back(place, du, weight)
    parts_a, got_b, d_emb_send = together((parts_a, got_b, d_emb_send))
    d_emb_other = swap(d_emb_send, size, 1)
    pieces = add_split(place, parts_a, "a_split")
    parts_a = [pieces[0], *exchange(pieces[:0:-1], line_masks[::-1])]
    keep_b, got_b, _ = halve(keep_b, got_b, x_bit, "b_x")
    d_img_emb, d_txt_emb = pick(
        place, SIDE, (d_emb, d_emb_other), (d_emb_other, d_emb), "rows_pick"
    )
    keep_b, got_b, give_b = halve(keep_b, got_b, y_bit, "b_y")
    parts_a, d_img_emb, d_txt_emb, _ = together((parts_a, d_img_emb, d_txt_emb, give_b))

    parts_a, got_b = together((parts_a, got_b))
    shard_a = add_all(place, parts_a, "a_last")
    shard_b = add_two(place, keep_b, got_b, "b_last")
    if size > 32:
        groups = [[i for i in range(size) if i % 32 == k] for k in range(32)]
        shard_a, shard_b = lax.psum((shard_a, shard_b), "dp", axis_index_groups=groups)
    parts_a = [shard_a, *exchange([shard_a] * 3, line_masks)]
    shard_b = join_two(place, y_bit[0], *gather(shard_b, y_bit), "b_join_y")
    got_b = swap(shard_b, size, x_bit[1])
    parts_a, _ = together((parts_a, shard_b))

    parts_a, got_b = together((parts_a, got_b))
    piece_a = join_four(place, IN_LINE, parts_a, "a_join")
    parts_a = [piece_a, *exchange([piece_a] * 3, plane_masks)]
    shard_b = join_two(place, x_bit[0], shard_b, got_b, "b_join_x")
    shard_b = join_two(place, high_bit[0], *gather(shard_b, high_bit), "b_join_high")
    got_b = swap(shard_b, size, low_bit[1])
    parts_a, got_b = together((parts_a, got_b))

    d_weight = join_all(place, parts_a, (shard_b, got_b))
    d_weight_other = swap(d_weight, size, 1)
    outs = widen(place, d_weight, True, (), "widen_own")
    d_img_proj, d_txt_proj = widen(place, d_weight_other, False, outs, "widen_other")
    return (d_img_emb, d_txt_emb, d_img_proj, d_txt_proj)


def solution(mesh):
    return jax.shard_map(
        body,
        mesh=mesh,
        in_specs=(P("dp", None), P("dp", None), P(), P(), P(), P()),
        out_specs=(P("dp", None), P("dp", None), P(), P()),
        check_vma=False,
    )
```

```python
import functools

import jax
import jax.numpy as jnp
from jax import lax
from jax.experimental import pallas as pl
from jax.experimental.pallas import tpu as pltpu
from jax.sharding import PartitionSpec as P

REACH = 3
BF16, F32 = jnp.bfloat16, jnp.float32
TILE = 512
SIDE, IN_PLANE, IN_LINE, SAME, X, Y, Z_LOW, Z_HIGH = range(8)
VMEM = pl.BlockSpec(memory_space=pltpu.VMEM)
SMEM = pl.BlockSpec(memory_space=pltpu.SMEM)
HBM = pl.BlockSpec(memory_space=pltpu.HBM)
ANY = pl.BlockSpec(memory_space=pl.ANY)


def params(mib):
    return pltpu.CompilerParams(vmem_limit_bytes=mib * 1024 * 1024)


def dot_t(left, right):
    return lax.dot_general(left, right, (((1,), (1,)), ((), ())), preferred_element_type=F32)


def dot(left, right):
    return lax.dot_general(left, right, (((1,), (0,)), ((), ())), preferred_element_type=F32)


def shift(value, size, chips):
    pairs = []
    for i in range(size):
        chip, core = i // 2, i % 2
        pairs.append((i, 2 * ((chip + chips(chip, core)) % (size // 2)) + core))
    return lax.ppermute(value, "dp", pairs)


def swap(value, size, mask):
    return lax.ppermute(value, "dp", [(i, i ^ mask) for i in range(size)])


def met_kernel(own_chip, place, *refs):
    sides, projs, (z_one, z_two, emb_v, proj_v, sems) = (refs[:2], refs[2:4]), refs[4:6], refs[6:]
    cut = proj_v.shape[0] // 256 * 128 + 128
    parts = [slice(0, cut), slice(cut, proj_v.shape[0])]
    for side, (embs, proj) in enumerate(zip(sides, projs)):

        @pl.when(place[SIDE] == side)
        def _():
            first = 1 - place[SAME] if own_chip else 0
            copies = [pltpu.make_async_copy(embs[0], emb_v.at[first], sems.at[2])]
            for k, part in enumerate(parts):
                copies.append(
                    pltpu.make_async_copy(proj.at[part, :], proj_v.at[part, :], sems.at[k])
                )
            copies.append(pltpu.make_async_copy(embs[1], emb_v.at[1 - first], sems.at[3]))
            for copy in copies:
                copy.start()
            for copy in copies:
                copy.wait()

    for k, z in enumerate((z_one, z_two)):
        raw = dot(emb_v[k], proj_v[...])
        scale = lax.rsqrt(jnp.sum(raw * raw, axis=1, keepdims=True) + 1e-06)
        z[...] = (raw * scale).astype(BF16)


def met_units(place, text_side, image_side, img_proj, txt_proj, own_chip, mib, name):
    out = jax.ShapeDtypeStruct(text_side[0].shape, BF16)
    return pl.pallas_call(
        functools.partial(met_kernel, own_chip),
        out_shape=(out, out),
        in_specs=[SMEM] + [HBM] * 6,
        out_specs=(VMEM, VMEM),
        scratch_shapes=[
            pltpu.VMEM((2, *out.shape), BF16),
            pltpu.VMEM(img_proj.shape, BF16),
            pltpu.SemaphoreType.DMA((4,)),
        ],
        compiler_params=params(mib),
        name=name,
    )(place, *text_side, *image_side, txt_proj, img_proj)


def second_kernel(place, *refs):
    sides, (unit, inverse, z, weight, emb_t, emb_v, sems) = (refs[:3], refs[3:6]), refs[6:]
    rows = emb_v.shape[1]
    for side in range(2):

        @pl.when(place[SIDE] == side)
        def _():
            copies = [
                pltpu.make_async_copy(src, dst, sems.at[at])
                for at, (src, dst) in enumerate(
                    zip(sides[side], (weight, emb_v.at[1 - place[SAME]], emb_v.at[place[SAME]]))
                )
            ]
            for copy in copies:
                copy.start()
            for copy in copies:
                copy.wait()

    for half in range(2):
        here = slice(half * rows, (half + 1) * rows)
        raw = dot(emb_v[half], weight[...])
        scale = lax.rsqrt(jnp.sum(raw * raw, axis=1, keepdims=True) + 1e-06)
        inverse[here, :] = scale
        units = raw * scale
        unit[here, :] = units
        z[here, :] = units.astype(BF16)
        emb_t[:, here] = emb_v[half].T


def second_units(place, img_emb, txt_emb, img_other, txt_other, img_proj, txt_proj):
    rows, columns = img_emb.shape
    return pl.pallas_call(
        second_kernel,
        out_shape=(
            jax.ShapeDtypeStruct((2 * rows, columns), F32),
            jax.ShapeDtypeStruct((2 * rows, 1), F32),
            jax.ShapeDtypeStruct((2 * rows, columns), BF16),
            jax.ShapeDtypeStruct(img_proj.shape, BF16),
            jax.ShapeDtypeStruct((columns, 2 * rows), BF16),
        ),
        in_specs=[SMEM] + [HBM] * 6,
        out_specs=(VMEM,) * 5,
        scratch_shapes=[
            pltpu.VMEM((2, rows, columns), BF16),
            pltpu.SemaphoreType.DMA((3,)),
        ],
        compiler_params=params(18),
        name="second_units",
    )(place, img_proj, img_emb, img_other, txt_proj, txt_emb, txt_other)


def piece_at(digit, m, height, first=0):
    return pl.ds(pl.multiple_of(first + (digit ^ m) * height, 8), height)


def pick_kernel(at, place, *refs):
    sources, outs, sems = (refs[:2], refs[2:4]), refs[4:6], refs[6]
    for flag in range(2):

        @pl.when(place[at] == flag)
        def _():
            copies = [
                pltpu.make_async_copy(pair[flag], out, sems.at[k])
                for k, (pair, out) in enumerate(zip(sources, outs))
            ]
            for copy in copies:
                copy.start()
            for copy in copies:
                copy.wait()


def pick(place, at, first, second, name):
    return pl.pallas_call(
        functools.partial(pick_kernel, at),
        out_shape=tuple(jax.ShapeDtypeStruct(p[0].shape, p[0].dtype) for p in (first, second)),
        in_specs=[SMEM] + [ANY] * 4,
        out_specs=(ANY, ANY),
        scratch_shapes=[pltpu.SemaphoreType.DMA((2,))],
        compiler_params=params(1),
        name=name,
    )(place, *first, *second)


def pair_term(z, block, scale, bias, diagonal):
    half = dot_t(z, block) * (0.5 * scale) + 0.5 * bias
    coef = 0.5 * jnp.tanh(half) + 0.5
    if diagonal is not None:
        row_at = lax.broadcasted_iota(jnp.int32, coef.shape, 0) + diagonal
        col_at = lax.broadcasted_iota(jnp.int32, coef.shape, 1)
        coef = jnp.where(row_at == col_at, coef - 1.0, coef)
    return dot(coef.astype(BF16), block)


def own_chip_kernel(scale, bias, z, met, met_other, grad):
    step = pl.program_id(0)
    per_block = met.shape[0] // TILE
    here = step * TILE
    near = pair_term(z[...], met[...], scale[0], bias[0], here)
    other = pair_term(z[...], met_other[...], scale[0], bias[0], here - per_block * TILE)
    grad[...] = near + other


def first_phase_kernel(scale, bias, z, one, two, far_own, far_other, grad_in, grad):
    step = pl.program_id(0)
    per_block = one.shape[0] // TILE
    total = grad_in[...] + pair_term(z[...], one[...], scale[0], bias[0], None)
    total = total + pair_term(z[...], two[...], scale[0], bias[0], None)

    @pl.when(step < per_block)
    def _():
        grad[...] = total + pair_term(z[...], far_own[...], scale[0], bias[0], None)

    @pl.when(step >= per_block)
    def _():
        grad[...] = total + pair_term(z[...], far_other[...], scale[0], bias[0], None)


def row_tiles(columns):
    return pl.BlockSpec((TILE, columns), lambda i: (i, 0))


def whole(array):
    return pl.BlockSpec(
        array.shape, lambda i: (0,) * len(array.shape), pipeline_mode=pl.Buffered(1)
    )


def call_tiles(kernel, scale, bias, z, blocks, grads, name, mib):
    rows, columns = z.shape
    return pl.pallas_call(
        kernel,
        grid=(rows // TILE,),
        out_shape=jax.ShapeDtypeStruct((rows, columns), F32),
        in_specs=[SMEM, SMEM, row_tiles(columns)]
        + [whole(b) for b in blocks]
        + [row_tiles(columns)] * len(grads),
        out_specs=row_tiles(columns),
        compiler_params=params(mib),
        name=name,
    )(scale, bias, z, *blocks, *grads)


def last_phase_kernel(
    place, scale, bias, z, one, two, grad_in, unit, inverse, emb_t, du, *rest
):
    half, (du_all, emb_v, sem) = rest[0], rest[1:]
    step = pl.program_id(0)
    fetch = pltpu.make_async_copy(emb_t, emb_v, sem)

    @pl.when(step == 0)
    def _():
        fetch.start()

    grad = grad_in[...] + pair_term(z[...], one[...], scale[0], bias[0], None)
    grad = scale[0] * (grad + pair_term(z[...], two[...], scale[0], bias[0], None))
    units = unit[...]
    inner = jnp.sum(units * grad, axis=1, keepdims=True)
    rounded = ((grad - units * inner) * inverse[...]).astype(BF16)
    du[...] = rounded
    du_all[pl.ds(pl.multiple_of(step * TILE, TILE), TILE), :] = rounded

    @pl.when(step == pl.num_programs(0) - 1)
    def _():
        fetch.wait()
        height = half.shape[0]
        first = emb_v.shape[0] - 2 * height
        rows = piece_at(place[Z_LOW], 1, height, first)
        half[...] = dot(emb_v[rows, :], du_all[...]).astype(BF16)


def last_phase(place, scale, bias, z, one, two, grad, unit, inverse, emb_t):
    rows, columns = z.shape
    half = jax.ShapeDtypeStruct((columns // 6, columns), BF16)
    return pl.pallas_call(
        last_phase_kernel,
        grid=(rows // TILE,),
        out_shape=(jax.ShapeDtypeStruct((rows, columns), BF16), half),
        in_specs=[
            SMEM,
            SMEM,
            SMEM,
            row_tiles(columns),
            whole(one),
            whole(two),
            row_tiles(columns),
            row_tiles(columns),
            row_tiles(1),
            HBM,
        ],
        out_specs=(row_tiles(columns), whole(half)),
        scratch_shapes=[
            pltpu.VMEM((rows, columns), BF16),
            pltpu.VMEM(emb_t.shape, BF16),
            pltpu.SemaphoreType.DMA,
        ],
        compiler_params=params(28),
        name="last_phase",
    )(place, scale, bias, z, one, two, grad, unit, inverse, emb_t)


def other_parts_kernel(place, emb_t, du, keep_b, *pieces):
    height = keep_b.shape[0]
    for m, out in enumerate(pieces):
        rows = piece_at(place[IN_PLANE], m, height)
        out[...] = dot(emb_t[rows, :], du[...]).astype(out.dtype)
    rows = piece_at(place[Z_LOW], 0, height, emb_t.shape[0] - 2 * height)
    keep_b[...] = dot(emb_t[rows, :], du[...])


def other_parts(place, emb_t, du):
    shape = (emb_t.shape[0] // 6, emb_t.shape[0])
    kinds = [F32, F32, BF16, BF16, BF16]
    return pl.pallas_call(
        other_parts_kernel,
        out_shape=tuple(jax.ShapeDtypeStruct(shape, kind) for kind in kinds),
        in_specs=[SMEM] + [VMEM] * 2,
        out_specs=(VMEM,) * 5,
        compiler_params=params(8),
        name="other_parts",
    )(place, emb_t, du)


def rows_back_kernel(place, du, weight, own, other):
    back = dot_t(du[...], weight[...]).astype(BF16)
    mine = pl.program_id(0) == 1 - place[SAME]

    @pl.when(mine)
    def _():
        own[...] = back

    @pl.when(jnp.logical_not(mine))
    def _():
        other[...] = back


def rows_back(place, du, weight):
    rows, columns = du.shape
    out = jax.ShapeDtypeStruct((TILE, columns), BF16)
    return pl.pallas_call(
        rows_back_kernel,
        grid=(rows // TILE,),
        out_shape=(out, out),
        in_specs=[SMEM, row_tiles(columns), whole(weight)],
        out_specs=(whole(out), whole(out)),
        compiler_params=params(8),
        name="rows_back",
    )(place, du, weight)


def summed(refs):
    one, two, three, four = (ref[...].astype(F32) for ref in refs)
    return (one + two) + (three + four)


def small_call(kernel, place, arrays, outs, scratch, mib, name):
    return pl.pallas_call(
        kernel,
        out_shape=tuple(jax.ShapeDtypeStruct(shape, kind) for shape, kind in outs),
        in_specs=[SMEM] + [VMEM] * len(arrays),
        out_specs=(VMEM,) * len(outs),
        scratch_shapes=[pltpu.VMEM(shape, F32) for shape in scratch],
        compiler_params=params(mib),
        name=name,
    )(place, *arrays)


def add_split_kernel(place, *refs):
    total = refs[8]
    total[...] = summed(refs[:4])
    for m, out in enumerate(refs[4:8]):
        out[...] = total[piece_at(place[IN_LINE], m, out.shape[0]), :].astype(out.dtype)


def add_split(place, parts, name):
    rows, columns = parts[0].shape
    outs = [((rows // 4, columns), F32 if m == 0 else BF16) for m in range(4)]
    return small_call(add_split_kernel, place, parts, outs, [(rows, columns)], 4, name)


def add_all_kernel(place, *refs):
    refs[4][...] = summed(refs[:4]).astype(BF16)


def add_all(place, parts, name):
    return small_call(add_all_kernel, place, parts, [(parts[0].shape, BF16)], [], 2, name)[0]


def join_four_kernel(digit, place, *refs):
    out, total = refs[4:]
    for m, piece in enumerate(refs[:4]):
        total[piece_at(place[digit], m, piece.shape[0]), :] = piece[...].astype(F32)
    out[...] = total[...].astype(BF16)


def join_four(place, digit, parts, name):
    shape = (4 * parts[0].shape[0], parts[0].shape[1])
    kernel = functools.partial(join_four_kernel, digit)
    return small_call(kernel, place, parts, [(shape, BF16)], [shape], 7, name)[0]


def add_halve_kernel(bit, place, keep, got, mine, give, total):
    total[...] = keep[...] + got[...].astype(F32)
    for m, out in enumerate((mine, give)):
        out[...] = total[piece_at(place[bit], m, out.shape[0]), :].astype(out.dtype)


def add_halve(place, bit, keep, got, name):
    rows, columns = keep.shape
    outs = [((rows // 2, columns), kind) for kind in (F32, BF16)]
    kernel = functools.partial(add_halve_kernel, bit)
    return small_call(kernel, place, [keep, got], outs, [keep.shape], 3, name)


def add_two_kernel(place, keep, got, out):
    out[...] = (keep[...] + got[...].astype(F32)).astype(BF16)


def add_two(place, keep, got, name):
    return small_call(add_two_kernel, place, [keep, got], [(keep.shape, BF16)], [], 2, name)[0]


def join_two_kernel(bit, place, mine, got, out, total):
    for m, piece in enumerate((mine, got)):
        total[piece_at(place[bit], m, piece.shape[0]), :] = piece[...].astype(F32)
    out[...] = total[...].astype(BF16)


def join_two(place, bit, mine, got, name):
    shape = (2 * mine.shape[0], mine.shape[1])
    kernel = functools.partial(join_two_kernel, bit)
    return small_call(kernel, place, [mine, got], [(shape, BF16)], [shape], 5, name)[0]


def join_all_kernel(place, *refs):
    out = refs[6]
    for m, piece in enumerate(refs[:4]):
        out[piece_at(place[IN_PLANE], m, piece.shape[0]), :] = piece[...]
    height = refs[4].shape[0]
    for m, piece in enumerate(refs[4:6]):
        out[piece_at(place[Z_LOW], m, height, out.shape[0] - 2 * height), :] = piece[...]


def join_all(place, parts_a, parts_b):
    columns = parts_b[0].shape[1]
    arrays = [*parts_a, *parts_b]
    outs = [((columns, columns), BF16)]
    return small_call(join_all_kernel, place, arrays, outs, [], 3, "join_all")[0]


def widen_kernel(own, place, weight, *refs):
    img_out, txt_out, wide, sems = refs[-4:]
    count = sems.shape[0]
    height = weight.shape[0] // count
    for side, out in enumerate((img_out, txt_out)):

        @pl.when((place[SIDE] == side) == own)
        def _():
            copies = []
            for k in range(count):
                part = slice(k * height, (k + 1) * height)
                wide[part, :] = weight[part, :].astype(F32)
                copies.append(
                    pltpu.make_async_copy(wide.at[part, :], out.at[part, :], sems.at[k])
                )
                copies[-1].start()
            for copy in copies:
                copy.wait()


def widen(place, weight, own, outs, name):
    out = jax.ShapeDtypeStruct(weight.shape, F32)
    return pl.pallas_call(
        functools.partial(widen_kernel, own),
        out_shape=(out, out),
        in_specs=[SMEM, VMEM] + [ANY] * len(outs),
        out_specs=(ANY, ANY),
        scratch_shapes=[pltpu.VMEM(weight.shape, F32), pltpu.SemaphoreType.DMA((9,))],
        input_output_aliases={2: 0, 3: 1} if outs else {},
        compiler_params=params(9),
        name=name,
    )(place, weight, *outs)


def body(img_emb, txt_emb, img_proj, txt_proj, log_scale, bias):
    size = lax.axis_size("dp")
    columns = img_emb.shape[1]
    scale = jnp.exp(log_scale)
    here = lax.axis_index("dp").astype(jnp.int32)
    side, chip = here % 2, here // 2
    bits = [(chip // n) % 2 for n in (1, 2, 4, 8)]
    place = jnp.stack([side, chip % 4, (chip // 4) % 4, (chip + side + 1) % 2, *bits])
    place, scale = lax.optimization_barrier((place, scale))

    pair = lambda value: swap(value, size, 2)
    far_as_d = lambda value: shift(value, size, lambda chip, core: -2 if chip % 2 else 2)

    def raw_target(to_far, to_pair):
        pairs = []
        for i in range(size):
            chip, core = i // 2, i % 2
            if core == chip % 2:
                pairs.append((i, 2 * ((chip + 2 if core else chip - 2) % (size // 2)) + to_far))
            else:
                pairs.append((i, 2 * (chip ^ 1) + to_pair))
        return pairs

    same = place[SAME] == 1
    raw_one = jnp.where(same, txt_emb, img_emb)
    raw_two = jnp.where(same, img_emb, txt_emb)
    got_one = lax.ppermute(raw_one, "dp", raw_target(0, 1))
    got_two = lax.ppermute(raw_two, "dp", raw_target(1, 0))
    img_other, txt_other, _ = lax.optimization_barrier(
        (swap(img_emb, size, 1), swap(txt_emb, size, 1), raw_one)
    )
    met_s, met_d = met_units(
        place,
        (txt_emb, txt_other),
        (img_emb, img_other),
        img_proj,
        txt_proj,
        True,
        58,
        "own_met",
    )
    img_emb, txt_emb, img_other, txt_other, _ = lax.optimization_barrier(
        (img_emb, txt_emb, img_other, txt_other, met_s)
    )
    unit, inverse, z, weight, emb_t = second_units(
        place, img_emb, txt_emb, img_other, txt_other, img_proj, txt_proj
    )
    got_one, got_two, sent_s, sent_d, _ = lax.optimization_barrier(
        (got_one, got_two, met_s, met_d, emb_t)
    )
    pair_s, far_d = pair(sent_s), far_as_d(sent_d)
    pair_d, far_s = met_units(
        place,
        (got_two, got_one),
        (got_one, got_two),
        img_proj,
        txt_proj,
        False,
        14,
        "raw_met",
    )
    relay_far, relay_pair = pair(far_s), far_as_d(pair_d)
    z, _ = lax.optimization_barrier((z, (pair_d, far_s)))
    grad = call_tiles(own_chip_kernel, scale, bias, z, (met_s, met_d), (), "own_chip", 8)
    pair_s, far_d, _ = lax.optimization_barrier((pair_s, far_d, grad))
    grad = call_tiles(
        first_phase_kernel,
        scale,
        bias,
        z,
        (pair_s, pair_d, far_d, far_s),
        (grad,),
        "first_phase",
        12,
    )

    du, give_b = last_phase(
        place, scale, bias, z, relay_far, relay_pair, grad, unit, inverse, emb_t
    )

    def exchange(sends, masks):
        return [swap(s, size, m) for s, m in zip(sends, masks)]

    plane_masks, line_masks = (2, 4, 6), (8, 16, 24)
    x_bit, y_bit, low_bit, high_bit = (X, 2), (Y, 4), (Z_LOW, 8), (Z_HIGH, 16)

    def halve(keep, got, bit, name):
        keep, give = add_halve(place, bit[0], keep, got, name)
        return keep, swap(give, size, bit[1]), give

    def gather(mine, bit):
        return mine, swap(mine, size, bit[1])

    together = lax.optimization_barrier
    got_b = swap(give_b, size, low_bit[1])
    keep_b, *pieces = other_parts(place, emb_t, du)
    parts_a = [pieces[0], *exchange(pieces[1:], plane_masks)]
    keep_b, got_b, give_b = halve(keep_b, got_b, high_bit, "b_high")
    du, _ = together((du, give_b))
    d_emb, d_emb_send = rows_back(place, du, weight)
    parts_a, got_b, d_emb_send = together((parts_a, got_b, d_emb_send))
    d_emb_other = swap(d_emb_send, size, 1)
    pieces = add_split(place, parts_a, "a_split")
    parts_a = [pieces[0], *exchange(pieces[:0:-1], line_masks[::-1])]
    keep_b, got_b, _ = halve(keep_b, got_b, x_bit, "b_x")
    d_img_emb, d_txt_emb = pick(
        place, SIDE, (d_emb, d_emb_other), (d_emb_other, d_emb), "rows_pick"
    )
    keep_b, got_b, give_b = halve(keep_b, got_b, y_bit, "b_y")
    parts_a, d_img_emb, d_txt_emb, _ = together((parts_a, d_img_emb, d_txt_emb, give_b))

    parts_a, got_b = together((parts_a, got_b))
    shard_a = add_all(place, parts_a, "a_last")
    shard_b = add_two(place, keep_b, got_b, "b_last")
    if size > 32:
        groups = [[i for i in range(size) if i % 32 == k] for k in range(32)]
        shard_a, shard_b = lax.psum((shard_a, shard_b), "dp", axis_index_groups=groups)
    parts_a = [shard_a, *exchange([shard_a] * 3, line_masks)]
    shard_b = join_two(place, y_bit[0], *gather(shard_b, y_bit), "b_join_y")
    got_b = swap(shard_b, size, x_bit[1])
    parts_a, _ = together((parts_a, shard_b))

    parts_a, got_b = together((parts_a, got_b))
    piece_a = join_four(place, IN_LINE, parts_a, "a_join")
    parts_a = [piece_a, *exchange([piece_a] * 3, plane_masks)]
    shard_b = join_two(place, x_bit[0], shard_b, got_b, "b_join_x")
    shard_b = join_two(place, high_bit[0], *gather(shard_b, high_bit), "b_join_high")
    got_b = swap(shard_b, size, low_bit[1])
    parts_a, got_b = together((parts_a, got_b))

    d_weight = join_all(place, parts_a, (shard_b, got_b))
    d_weight_other = swap(d_weight, size, 1)
    outs = widen(place, d_weight, True, (), "widen_own")
    d_img_proj, d_txt_proj = widen(place, d_weight_other, False, outs, "widen_other")
    return (d_img_emb, d_txt_emb, d_img_proj, d_txt_proj)


def solution(mesh):
    return jax.shard_map(
        body,
        mesh=mesh,
        in_specs=(P("dp", None), P("dp", None), P(), P(), P(), P()),
        out_specs=(P("dp", None), P("dp", None), P(), P()),
        check_vma=False,
    )
```

```python
import functools

import jax
import jax.numpy as jnp
from jax import lax
from jax.experimental import pallas as pl
from jax.experimental.pallas import tpu as pltpu
from jax.sharding import PartitionSpec as P

REACH = 3
BF16, F32 = jnp.bfloat16, jnp.float32
TILE = 512
SIDE, IN_PLANE, IN_LINE, SAME, X, Y, Z_LOW, Z_HIGH = range(8)
VMEM = pl.BlockSpec(memory_space=pltpu.VMEM)
SMEM = pl.BlockSpec(memory_space=pltpu.SMEM)
HBM = pl.BlockSpec(memory_space=pltpu.HBM)
ANY = pl.BlockSpec(memory_space=pl.ANY)


def params(mib):
    return pltpu.CompilerParams(vmem_limit_bytes=mib * 1024 * 1024)


def dot_t(left, right):
    return lax.dot_general(left, right, (((1,), (1,)), ((), ())), preferred_element_type=F32)


def dot(left, right):
    return lax.dot_general(left, right, (((1,), (0,)), ((), ())), preferred_element_type=F32)


def shift(value, size, chips):
    pairs = []
    for i in range(size):
        chip, core = i // 2, i % 2
        pairs.append((i, 2 * ((chip + chips(chip, core)) % (size // 2)) + core))
    return lax.ppermute(value, "dp", pairs)


def swap(value, size, mask):
    return lax.ppermute(value, "dp", [(i, i ^ mask) for i in range(size)])


def met_kernel(own_chip, place, *refs):
    sides, projs, (z_one, z_two, emb_v, proj_v, sems) = (refs[:2], refs[2:4]), refs[4:6], refs[6:]
    cut = proj_v.shape[0] // 256 * 128 + 128
    parts = [slice(0, cut), slice(cut, proj_v.shape[0])]
    for side, (embs, proj) in enumerate(zip(sides, projs)):

        @pl.when(place[SIDE] == side)
        def _():
            first = 1 - place[SAME] if own_chip else 0
            copies = [pltpu.make_async_copy(embs[0], emb_v.at[first], sems.at[2])]
            for k, part in enumerate(parts):
                copies.append(
                    pltpu.make_async_copy(proj.at[part, :], proj_v.at[part, :], sems.at[k])
                )
            copies.append(pltpu.make_async_copy(embs[1], emb_v.at[1 - first], sems.at[3]))
            for copy in copies:
                copy.start()
            for copy in copies:
                copy.wait()

    for k, z in enumerate((z_one, z_two)):
        raw = dot(emb_v[k], proj_v[...])
        scale = lax.rsqrt(jnp.sum(raw * raw, axis=1, keepdims=True) + 1e-06)
        z[...] = (raw * scale).astype(BF16)


def met_units(place, text_side, image_side, img_proj, txt_proj, own_chip, mib, name):
    out = jax.ShapeDtypeStruct(text_side[0].shape, BF16)
    return pl.pallas_call(
        functools.partial(met_kernel, own_chip),
        out_shape=(out, out),
        in_specs=[SMEM] + [HBM] * 6,
        out_specs=(VMEM, VMEM),
        scratch_shapes=[
            pltpu.VMEM((2, *out.shape), BF16),
            pltpu.VMEM(img_proj.shape, BF16),
            pltpu.SemaphoreType.DMA((4,)),
        ],
        compiler_params=params(mib),
        name=name,
    )(place, *text_side, *image_side, txt_proj, img_proj)


def second_kernel(place, *refs):
    sides, (unit, inverse, z, weight, emb_t, emb_v, sems) = (refs[:3], refs[3:6]), refs[6:]
    rows = emb_v.shape[1]
    for side in range(2):

        @pl.when(place[SIDE] == side)
        def _():
            copies = [
                pltpu.make_async_copy(src, dst, sems.at[at])
                for at, (src, dst) in enumerate(
                    zip(sides[side], (weight, emb_v.at[1 - place[SAME]], emb_v.at[place[SAME]]))
                )
            ]
            for copy in copies:
                copy.start()
            for copy in copies:
                copy.wait()

    for half in range(2):
        here = slice(half * rows, (half + 1) * rows)
        raw = dot(emb_v[half], weight[...])
        scale = lax.rsqrt(jnp.sum(raw * raw, axis=1, keepdims=True) + 1e-06)
        inverse[here, :] = scale
        units = raw * scale
        unit[here, :] = units
        z[here, :] = units.astype(BF16)
        emb_t[:, here] = emb_v[half].T


def second_units(place, img_emb, txt_emb, img_other, txt_other, img_proj, txt_proj):
    rows, columns = img_emb.shape
    return pl.pallas_call(
        second_kernel,
        out_shape=(
            jax.ShapeDtypeStruct((2 * rows, columns), F32),
            jax.ShapeDtypeStruct((2 * rows, 1), F32),
            jax.ShapeDtypeStruct((2 * rows, columns), BF16),
            jax.ShapeDtypeStruct(img_proj.shape, BF16),
            jax.ShapeDtypeStruct((columns, 2 * rows), BF16),
        ),
        in_specs=[SMEM] + [HBM] * 6,
        out_specs=(VMEM,) * 5,
        scratch_shapes=[
            pltpu.VMEM((2, rows, columns), BF16),
            pltpu.SemaphoreType.DMA((3,)),
        ],
        compiler_params=params(18),
        name="second_units",
    )(place, img_proj, img_emb, img_other, txt_proj, txt_emb, txt_other)


def piece_at(digit, m, height, first=0):
    return pl.ds(pl.multiple_of(first + (digit ^ m) * height, 8), height)


def pick_kernel(at, place, *refs):
    sources, outs, sems = (refs[:2], refs[2:4]), refs[4:6], refs[6]
    for flag in range(2):

        @pl.when(place[at] == flag)
        def _():
            copies = [
                pltpu.make_async_copy(pair[flag], out, sems.at[k])
                for k, (pair, out) in enumerate(zip(sources, outs))
            ]
            for copy in copies:
                copy.start()
            for copy in copies:
                copy.wait()


def pick(place, at, first, second, name):
    return pl.pallas_call(
        functools.partial(pick_kernel, at),
        out_shape=tuple(jax.ShapeDtypeStruct(p[0].shape, p[0].dtype) for p in (first, second)),
        in_specs=[SMEM] + [ANY] * 4,
        out_specs=(ANY, ANY),
        scratch_shapes=[pltpu.SemaphoreType.DMA((2,))],
        compiler_params=params(1),
        name=name,
    )(place, *first, *second)


def pair_term(z, block, scale, bias, diagonal):
    half = dot_t(z, block) * (0.5 * scale) + 0.5 * bias
    coef = 0.5 * jnp.tanh(half) + 0.5
    if diagonal is not None:
        row_at = lax.broadcasted_iota(jnp.int32, coef.shape, 0) + diagonal
        col_at = lax.broadcasted_iota(jnp.int32, coef.shape, 1)
        coef = jnp.where(row_at == col_at, coef - 1.0, coef)
    return dot(coef.astype(BF16), block)


def own_chip_kernel(scale, bias, z, met, met_other, grad):
    step = pl.program_id(0)
    per_block = met.shape[0] // TILE
    here = step * TILE
    near = pair_term(z[...], met[...], scale[0], bias[0], here)
    other = pair_term(z[...], met_other[...], scale[0], bias[0], here - per_block * TILE)
    grad[...] = near + other


def first_phase_kernel(scale, bias, z, one, two, far_own, far_other, grad_in, grad):
    step = pl.program_id(0)
    per_block = one.shape[0] // TILE
    total = grad_in[...] + pair_term(z[...], one[...], scale[0], bias[0], None)
    total = total + pair_term(z[...], two[...], scale[0], bias[0], None)

    @pl.when(step < per_block)
    def _():
        grad[...] = total + pair_term(z[...], far_own[...], scale[0], bias[0], None)

    @pl.when(step >= per_block)
    def _():
        grad[...] = total + pair_term(z[...], far_other[...], scale[0], bias[0], None)


def relayed_kernel(scale, bias, z, block, grad_in, grad):
    grad[...] = grad_in[...] + pair_term(z[...], block[...], scale[0], bias[0], None)


def row_tiles(columns):
    return pl.BlockSpec((TILE, columns), lambda i: (i, 0))


def whole(array):
    return pl.BlockSpec(
        array.shape, lambda i: (0,) * len(array.shape), pipeline_mode=pl.Buffered(1)
    )


def call_tiles(kernel, scale, bias, z, blocks, grads, name, mib):
    rows, columns = z.shape
    return pl.pallas_call(
        kernel,
        grid=(rows // TILE,),
        out_shape=jax.ShapeDtypeStruct((rows, columns), F32),
        in_specs=[SMEM, SMEM, row_tiles(columns)]
        + [whole(b) for b in blocks]
        + [row_tiles(columns)] * len(grads),
        out_specs=row_tiles(columns),
        compiler_params=params(mib),
        name=name,
    )(scale, bias, z, *blocks, *grads)


def last_phase_kernel(
    place, scale, bias, z, block, grad_in, unit, inverse, emb_t, du, *rest
):
    half, (du_all, emb_v, sem) = rest[0], rest[1:]
    step = pl.program_id(0)
    fetch = pltpu.make_async_copy(emb_t, emb_v, sem)

    @pl.when(step == 0)
    def _():
        fetch.start()

    grad = grad_in[...] + pair_term(z[...], block[...], scale[0], bias[0], None)
    grad = scale[0] * grad
    units = unit[...]
    inner = jnp.sum(units * grad, axis=1, keepdims=True)
    rounded = ((grad - units * inner) * inverse[...]).astype(BF16)
    du[...] = rounded
    du_all[pl.ds(pl.multiple_of(step * TILE, TILE), TILE), :] = rounded

    @pl.when(step == pl.num_programs(0) - 1)
    def _():
        fetch.wait()
        height = half.shape[0]
        first = emb_v.shape[0] - 2 * height
        rows = piece_at(place[Z_LOW], 1, height, first)
        half[...] = dot(emb_v[rows, :], du_all[...]).astype(BF16)


def last_phase(place, scale, bias, z, block, grad, unit, inverse, emb_t):
    rows, columns = z.shape
    half = jax.ShapeDtypeStruct((columns // 6, columns), BF16)
    return pl.pallas_call(
        last_phase_kernel,
        grid=(rows // TILE,),
        out_shape=(jax.ShapeDtypeStruct((rows, columns), BF16), half),
        in_specs=[
            SMEM,
            SMEM,
            SMEM,
            row_tiles(columns),
            whole(block),
            row_tiles(columns),
            row_tiles(columns),
            row_tiles(1),
            HBM,
        ],
        out_specs=(row_tiles(columns), whole(half)),
        scratch_shapes=[
            pltpu.VMEM((rows, columns), BF16),
            pltpu.VMEM(emb_t.shape, BF16),
            pltpu.SemaphoreType.DMA,
        ],
        compiler_params=params(28),
        name="last_phase",
    )(place, scale, bias, z, block, grad, unit, inverse, emb_t)


def sent_parts_kernel(place, emb_t, du, *pieces):
    for m, out in enumerate(pieces):
        rows = piece_at(place[IN_PLANE], m + 1, out.shape[0])
        out[...] = dot(emb_t[rows, :], du[...]).astype(out.dtype)


def kept_parts_kernel(place, emb_t, du, keep_a, keep_b):
    height = keep_b.shape[0]
    at_b = emb_t.shape[0] - 2 * height
    for out, rows in (
        (keep_a, piece_at(place[IN_PLANE], 0, height)),
        (keep_b, piece_at(place[Z_LOW], 0, height, at_b)),
    ):
        out[...] = dot(emb_t[rows, :], du[...])


def parts(kernel, place, emb_t, du, kinds, name):
    shape = (emb_t.shape[0] // 6, emb_t.shape[0])
    return pl.pallas_call(
        kernel,
        out_shape=tuple(jax.ShapeDtypeStruct(shape, kind) for kind in kinds),
        in_specs=[SMEM] + [VMEM] * 2,
        out_specs=(VMEM,) * len(kinds),
        compiler_params=params(6),
        name=name,
    )(place, emb_t, du)


def rows_back_kernel(place, du, weight, own, other):
    back = dot_t(du[...], weight[...]).astype(BF16)
    mine = pl.program_id(0) == 1 - place[SAME]

    @pl.when(mine)
    def _():
        own[...] = back

    @pl.when(jnp.logical_not(mine))
    def _():
        other[...] = back


def rows_back(place, du, weight):
    rows, columns = du.shape
    out = jax.ShapeDtypeStruct((TILE, columns), BF16)
    return pl.pallas_call(
        rows_back_kernel,
        grid=(rows // TILE,),
        out_shape=(out, out),
        in_specs=[SMEM, row_tiles(columns), whole(weight)],
        out_specs=(whole(out), whole(out)),
        compiler_params=params(8),
        name="rows_back",
    )(place, du, weight)


def summed(refs):
    one, two, three, four = (ref[...].astype(F32) for ref in refs)
    return (one + two) + (three + four)


def small_call(kernel, place, arrays, outs, scratch, mib, name):
    return pl.pallas_call(
        kernel,
        out_shape=tuple(jax.ShapeDtypeStruct(shape, kind) for shape, kind in outs),
        in_specs=[SMEM] + [VMEM] * len(arrays),
        out_specs=(VMEM,) * len(outs),
        scratch_shapes=[pltpu.VMEM(shape, F32) for shape in scratch],
        compiler_params=params(mib),
        name=name,
    )(place, *arrays)


def add_split_kernel(place, *refs):
    total = refs[8]
    total[...] = summed(refs[:4])
    for m, out in enumerate(refs[4:8]):
        out[...] = total[piece_at(place[IN_LINE], m, out.shape[0]), :].astype(out.dtype)


def add_split(place, parts, name):
    rows, columns = parts[0].shape
    outs = [((rows // 4, columns), F32 if m == 0 else BF16) for m in range(4)]
    return small_call(add_split_kernel, place, parts, outs, [(rows, columns)], 4, name)


def add_all_kernel(place, *refs):
    refs[4][...] = summed(refs[:4]).astype(BF16)


def add_all(place, parts, name):
    return small_call(add_all_kernel, place, parts, [(parts[0].shape, BF16)], [], 2, name)[0]


def join_four_kernel(digit, place, *refs):
    out, total = refs[4:]
    for m, piece in enumerate(refs[:4]):
        total[piece_at(place[digit], m, piece.shape[0]), :] = piece[...].astype(F32)
    out[...] = total[...].astype(BF16)


def join_four(place, digit, parts, name):
    shape = (4 * parts[0].shape[0], parts[0].shape[1])
    kernel = functools.partial(join_four_kernel, digit)
    return small_call(kernel, place, parts, [(shape, BF16)], [shape], 7, name)[0]


def add_halve_kernel(bit, place, keep, got, mine, give, total):
    total[...] = keep[...] + got[...].astype(F32)
    for m, out in enumerate((mine, give)):
        out[...] = total[piece_at(place[bit], m, out.shape[0]), :].astype(out.dtype)


def add_halve(place, bit, keep, got, name):
    rows, columns = keep.shape
    outs = [((rows // 2, columns), kind) for kind in (F32, BF16)]
    kernel = functools.partial(add_halve_kernel, bit)
    return small_call(kernel, place, [keep, got], outs, [keep.shape], 3, name)


def add_two_kernel(place, keep, got, out):
    out[...] = (keep[...] + got[...].astype(F32)).astype(BF16)


def add_two(place, keep, got, name):
    return small_call(add_two_kernel, place, [keep, got], [(keep.shape, BF16)], [], 2, name)[0]


def join_two_kernel(bit, place, mine, got, out, total):
    for m, piece in enumerate((mine, got)):
        total[piece_at(place[bit], m, piece.shape[0]), :] = piece[...].astype(F32)
    out[...] = total[...].astype(BF16)


def join_two(place, bit, mine, got, name):
    shape = (2 * mine.shape[0], mine.shape[1])
    kernel = functools.partial(join_two_kernel, bit)
    return small_call(kernel, place, [mine, got], [(shape, BF16)], [shape], 5, name)[0]


def join_all_kernel(place, *refs):
    out = refs[6]
    for m, piece in enumerate(refs[:4]):
        out[piece_at(place[IN_PLANE], m, piece.shape[0]), :] = piece[...]
    height = refs[4].shape[0]
    for m, piece in enumerate(refs[4:6]):
        out[piece_at(place[Z_LOW], m, height, out.shape[0] - 2 * height), :] = piece[...]


def join_all(place, parts_a, parts_b):
    columns = parts_b[0].shape[1]
    arrays = [*parts_a, *parts_b]
    outs = [((columns, columns), BF16)]
    return small_call(join_all_kernel, place, arrays, outs, [], 3, "join_all")[0]


def widen_kernel(own, place, weight, *refs):
    img_out, txt_out, wide, sems = refs[-4:]
    count = sems.shape[0]
    height = weight.shape[0] // count
    for side, out in enumerate((img_out, txt_out)):

        @pl.when((place[SIDE] == side) == own)
        def _():
            copies = []
            for k in range(count):
                part = slice(k * height, (k + 1) * height)
                wide[part, :] = weight[part, :].astype(F32)
                copies.append(
                    pltpu.make_async_copy(wide.at[part, :], out.at[part, :], sems.at[k])
                )
                copies[-1].start()
            for copy in copies:
                copy.wait()


def widen(place, weight, own, outs, name):
    out = jax.ShapeDtypeStruct(weight.shape, F32)
    return pl.pallas_call(
        functools.partial(widen_kernel, own),
        out_shape=(out, out),
        in_specs=[SMEM, VMEM] + [ANY] * len(outs),
        out_specs=(ANY, ANY),
        scratch_shapes=[pltpu.VMEM(weight.shape, F32), pltpu.SemaphoreType.DMA((9,))],
        input_output_aliases={2: 0, 3: 1} if outs else {},
        compiler_params=params(9),
        name=name,
    )(place, weight, *outs)


def body(img_emb, txt_emb, img_proj, txt_proj, log_scale, bias):
    size = lax.axis_size("dp")
    columns = img_emb.shape[1]
    scale = jnp.exp(log_scale)
    here = lax.axis_index("dp").astype(jnp.int32)
    side, chip = here % 2, here // 2
    bits = [(chip // n) % 2 for n in (1, 2, 4, 8)]
    place = jnp.stack([side, chip % 4, (chip // 4) % 4, (chip + side + 1) % 2, *bits])
    place, scale = lax.optimization_barrier((place, scale))

    pair = lambda value: swap(value, size, 2)
    far_as_d = lambda value: shift(value, size, lambda chip, core: -2 if chip % 2 else 2)

    def raw_target(to_far, to_pair):
        pairs = []
        for i in range(size):
            chip, core = i // 2, i % 2
            if core == chip % 2:
                pairs.append((i, 2 * ((chip + 2 if core else chip - 2) % (size // 2)) + to_far))
            else:
                pairs.append((i, 2 * (chip ^ 1) + to_pair))
        return pairs

    same = place[SAME] == 1
    raw_one = jnp.where(same, txt_emb, img_emb)
    raw_two = jnp.where(same, img_emb, txt_emb)
    got_one = lax.ppermute(raw_one, "dp", raw_target(0, 1))
    got_two = lax.ppermute(raw_two, "dp", raw_target(1, 0))
    img_other, txt_other, _ = lax.optimization_barrier(
        (swap(img_emb, size, 1), swap(txt_emb, size, 1), raw_one)
    )
    met_s, met_d = met_units(
        place,
        (txt_emb, txt_other),
        (img_emb, img_other),
        img_proj,
        txt_proj,
        True,
        58,
        "own_met",
    )
    img_emb, txt_emb, img_other, txt_other, _ = lax.optimization_barrier(
        (img_emb, txt_emb, img_other, txt_other, met_s)
    )
    unit, inverse, z, weight, emb_t = second_units(
        place, img_emb, txt_emb, img_other, txt_other, img_proj, txt_proj
    )
    got_one, got_two, sent_s, sent_d, _ = lax.optimization_barrier(
        (got_one, got_two, met_s, met_d, emb_t)
    )
    pair_s, far_d = pair(sent_s), far_as_d(sent_d)
    pair_d, far_s = met_units(
        place,
        (got_two, got_one),
        (got_one, got_two),
        img_proj,
        txt_proj,
        False,
        14,
        "raw_met",
    )
    relay_far, relay_pair = pair(far_s), far_as_d(pair_d)
    z, _ = lax.optimization_barrier((z, (pair_d, far_s)))
    grad = call_tiles(own_chip_kernel, scale, bias, z, (met_s, met_d), (), "own_chip", 8)
    pair_s, far_d, _ = lax.optimization_barrier((pair_s, far_d, grad))
    grad = call_tiles(
        first_phase_kernel,
        scale,
        bias,
        z,
        (pair_s, pair_d, far_d, far_s),
        (grad,),
        "first_phase",
        12,
    )

    grad = call_tiles(relayed_kernel, scale, bias, z, (relay_far,), (grad,), "relayed", 10)
    du, give_b = last_phase(
        place, scale, bias, z, relay_pair, grad, unit, inverse, emb_t
    )

    def exchange(sends, masks):
        return [swap(s, size, m) for s, m in zip(sends, masks)]

    plane_masks, line_masks = (2, 4, 6), (8, 16, 24)
    x_bit, y_bit, low_bit, high_bit = (X, 2), (Y, 4), (Z_LOW, 8), (Z_HIGH, 16)

    def halve(keep, got, bit, name):
        keep, give = add_halve(place, bit[0], keep, got, name)
        return keep, swap(give, size, bit[1]), give

    def gather(mine, bit):
        return mine, swap(mine, size, bit[1])

    together = lax.optimization_barrier
    got_b = swap(give_b, size, low_bit[1])
    sends = parts(sent_parts_kernel, place, emb_t, du, (BF16,) * 3, "sent_parts")
    got_a = exchange(sends, plane_masks)
    du, got_b = together((du, got_b))
    keep_a, keep_b = parts(kept_parts_kernel, place, emb_t, du, (F32, F32), "kept_parts")
    parts_a = [keep_a, *got_a]
    keep_b, got_b, give_b = halve(keep_b, got_b, high_bit, "b_high")
    du, _ = together((du, give_b))
    d_emb, d_emb_send = rows_back(place, du, weight)
    parts_a, got_b, d_emb_send = together((parts_a, got_b, d_emb_send))
    d_emb_other = swap(d_emb_send, size, 1)
    pieces = add_split(place, parts_a, "a_split")
    parts_a = [pieces[0], *exchange(pieces[:0:-1], line_masks[::-1])]
    got_b, _ = together((got_b, pieces))
    keep_b, got_b, _ = halve(keep_b, got_b, x_bit, "b_x")
    d_img_emb, d_txt_emb = pick(
        place, SIDE, (d_emb, d_emb_other), (d_emb_other, d_emb), "rows_pick"
    )
    keep_b, got_b, give_b = halve(keep_b, got_b, y_bit, "b_y")
    parts_a, d_img_emb, d_txt_emb, _ = together((parts_a, d_img_emb, d_txt_emb, give_b))

    parts_a, got_b = together((parts_a, got_b))
    shard_a = add_all(place, parts_a, "a_last")
    got_b, _ = together((got_b, shard_a))
    shard_b = add_two(place, keep_b, got_b, "b_last")
    if size > 32:
        groups = [[i for i in range(size) if i % 32 == k] for k in range(32)]
        shard_a, shard_b = lax.psum((shard_a, shard_b), "dp", axis_index_groups=groups)
    parts_a = [shard_a, *exchange([shard_a] * 3, line_masks)]
    shard_b = join_two(place, y_bit[0], *gather(shard_b, y_bit), "b_join_y")
    got_b = swap(shard_b, size, x_bit[1])
    parts_a, _ = together((parts_a, shard_b))

    parts_a, got_b = together((parts_a, got_b))
    piece_a = join_four(place, IN_LINE, parts_a, "a_join")
    parts_a = [piece_a, *exchange([piece_a] * 3, plane_masks)]
    got_b, _ = together((got_b, piece_a))
    shard_b = join_two(place, x_bit[0], shard_b, got_b, "b_join_x")
    shard_b = join_two(place, high_bit[0], *gather(shard_b, high_bit), "b_join_high")
    got_b = swap(shard_b, size, low_bit[1])
    parts_a, got_b = together((parts_a, got_b))

    d_weight = join_all(place, parts_a, (shard_b, got_b))
    d_weight_other = swap(d_weight, size, 1)
    outs = widen(place, d_weight, True, (), "widen_own")
    d_img_proj, d_txt_proj = widen(place, d_weight_other, False, outs, "widen_other")
    return (d_img_emb, d_txt_emb, d_img_proj, d_txt_proj)


def solution(mesh):
    return jax.shard_map(
        body,
        mesh=mesh,
        in_specs=(P("dp", None), P("dp", None), P(), P(), P(), P()),
        out_specs=(P("dp", None), P("dp", None), P(), P()),
        check_vma=False,
    )
```

```python
import functools

import jax
import jax.numpy as jnp
from jax import lax
from jax.experimental import pallas as pl
from jax.experimental.pallas import tpu as pltpu
from jax.sharding import PartitionSpec as P

REACH = 3
BF16, F32 = jnp.bfloat16, jnp.float32
TILE = 512
SIDE, IN_PLANE, IN_LINE, SAME, X, Y, Z_LOW, Z_HIGH = range(8)
VMEM = pl.BlockSpec(memory_space=pltpu.VMEM)
SMEM = pl.BlockSpec(memory_space=pltpu.SMEM)
HBM = pl.BlockSpec(memory_space=pltpu.HBM)
ANY = pl.BlockSpec(memory_space=pl.ANY)


def params(mib):
    return pltpu.CompilerParams(vmem_limit_bytes=mib * 1024 * 1024)


def dot_t(left, right):
    return lax.dot_general(left, right, (((1,), (1,)), ((), ())), preferred_element_type=F32)


def dot(left, right):
    return lax.dot_general(left, right, (((1,), (0,)), ((), ())), preferred_element_type=F32)


def shift(value, size, chips):
    pairs = []
    for i in range(size):
        chip, core = i // 2, i % 2
        pairs.append((i, 2 * ((chip + chips(chip, core)) % (size // 2)) + core))
    return lax.ppermute(value, "dp", pairs)


def swap(value, size, mask):
    return lax.ppermute(value, "dp", [(i, i ^ mask) for i in range(size)])


def met_kernel(own_chip, place, *refs):
    sides, projs, (z_one, z_two, emb_v, proj_v, sems) = (refs[:2], refs[2:4]), refs[4:6], refs[6:]
    cut = proj_v.shape[0] // 256 * 128 + 128
    parts = [slice(0, cut), slice(cut, proj_v.shape[0])]
    for side, (embs, proj) in enumerate(zip(sides, projs)):

        @pl.when(place[SIDE] == side)
        def _():
            first = 1 - place[SAME] if own_chip else 0
            copies = [pltpu.make_async_copy(embs[0], emb_v.at[first], sems.at[2])]
            for k, part in enumerate(parts):
                copies.append(
                    pltpu.make_async_copy(proj.at[part, :], proj_v.at[part, :], sems.at[k])
                )
            copies.append(pltpu.make_async_copy(embs[1], emb_v.at[1 - first], sems.at[3]))
            for copy in copies:
                copy.start()
            for copy in copies:
                copy.wait()

    for k, z in enumerate((z_one, z_two)):
        raw = dot(emb_v[k], proj_v[...])
        scale = lax.rsqrt(jnp.sum(raw * raw, axis=1, keepdims=True) + 1e-06)
        z[...] = (raw * scale).astype(BF16)


def met_units(place, text_side, image_side, img_proj, txt_proj, own_chip, mib, name):
    out = jax.ShapeDtypeStruct(text_side[0].shape, BF16)
    return pl.pallas_call(
        functools.partial(met_kernel, own_chip),
        out_shape=(out, out),
        in_specs=[SMEM] + [HBM] * 6,
        out_specs=(VMEM, VMEM),
        scratch_shapes=[
            pltpu.VMEM((2, *out.shape), BF16),
            pltpu.VMEM(img_proj.shape, BF16),
            pltpu.SemaphoreType.DMA((4,)),
        ],
        compiler_params=params(mib),
        name=name,
    )(place, *text_side, *image_side, txt_proj, img_proj)


def second_kernel(place, *refs):
    sides, (unit, inverse, z, weight, emb_t, emb_v, sems) = (refs[:3], refs[3:6]), refs[6:]
    rows = emb_v.shape[1]
    for side in range(2):

        @pl.when(place[SIDE] == side)
        def _():
            copies = [
                pltpu.make_async_copy(src, dst, sems.at[at])
                for at, (src, dst) in enumerate(
                    zip(sides[side], (weight, emb_v.at[1 - place[SAME]], emb_v.at[place[SAME]]))
                )
            ]
            for copy in copies:
                copy.start()
            for copy in copies:
                copy.wait()

    for half in range(2):
        here = slice(half * rows, (half + 1) * rows)
        raw = dot(emb_v[half], weight[...])
        scale = lax.rsqrt(jnp.sum(raw * raw, axis=1, keepdims=True) + 1e-06)
        inverse[here, :] = scale
        units = raw * scale
        unit[here, :] = units
        z[here, :] = units.astype(BF16)
        emb_t[:, here] = emb_v[half].T


def second_units(place, img_emb, txt_emb, img_other, txt_other, img_proj, txt_proj):
    rows, columns = img_emb.shape
    return pl.pallas_call(
        second_kernel,
        out_shape=(
            jax.ShapeDtypeStruct((2 * rows, columns), F32),
            jax.ShapeDtypeStruct((2 * rows, 1), F32),
            jax.ShapeDtypeStruct((2 * rows, columns), BF16),
            jax.ShapeDtypeStruct(img_proj.shape, BF16),
            jax.ShapeDtypeStruct((columns, 2 * rows), BF16),
        ),
        in_specs=[SMEM] + [HBM] * 6,
        out_specs=(VMEM,) * 5,
        scratch_shapes=[
            pltpu.VMEM((2, rows, columns), BF16),
            pltpu.SemaphoreType.DMA((3,)),
        ],
        compiler_params=params(18),
        name="second_units",
    )(place, img_proj, img_emb, img_other, txt_proj, txt_emb, txt_other)


def piece_at(digit, m, height, first=0):
    return pl.ds(pl.multiple_of(first + (digit ^ m) * height, 8), height)


def pick_kernel(at, place, *refs):
    sources, outs, sems = (refs[:2], refs[2:4]), refs[4:6], refs[6]
    for flag in range(2):

        @pl.when(place[at] == flag)
        def _():
            copies = [
                pltpu.make_async_copy(pair[flag], out, sems.at[k])
                for k, (pair, out) in enumerate(zip(sources, outs))
            ]
            for copy in copies:
                copy.start()
            for copy in copies:
                copy.wait()


def pick(place, at, first, second, name):
    return pl.pallas_call(
        functools.partial(pick_kernel, at),
        out_shape=tuple(jax.ShapeDtypeStruct(p[0].shape, p[0].dtype) for p in (first, second)),
        in_specs=[SMEM] + [ANY] * 4,
        out_specs=(ANY, ANY),
        scratch_shapes=[pltpu.SemaphoreType.DMA((2,))],
        compiler_params=params(1),
        name=name,
    )(place, *first, *second)


def pair_term(z, block, scale, bias, diagonal):
    half = dot_t(z, block) * (0.5 * scale) + 0.5 * bias
    coef = 0.5 * jnp.tanh(half) + 0.5
    if diagonal is not None:
        row_at = lax.broadcasted_iota(jnp.int32, coef.shape, 0) + diagonal
        col_at = lax.broadcasted_iota(jnp.int32, coef.shape, 1)
        coef = jnp.where(row_at == col_at, coef - 1.0, coef)
    return dot(coef.astype(BF16), block)


def own_chip_kernel(scale, bias, z, met, met_other, grad):
    step = pl.program_id(0)
    per_block = met.shape[0] // TILE
    here = step * TILE
    near = pair_term(z[...], met[...], scale[0], bias[0], here)
    other = pair_term(z[...], met_other[...], scale[0], bias[0], here - per_block * TILE)
    grad[...] = near + other


def first_phase_kernel(scale, bias, z, one, two, far_own, far_other, grad_in, grad):
    step = pl.program_id(0)
    per_block = one.shape[0] // TILE
    total = grad_in[...] + pair_term(z[...], one[...], scale[0], bias[0], None)
    total = total + pair_term(z[...], two[...], scale[0], bias[0], None)

    @pl.when(step < per_block)
    def _():
        grad[...] = total + pair_term(z[...], far_own[...], scale[0], bias[0], None)

    @pl.when(step >= per_block)
    def _():
        grad[...] = total + pair_term(z[...], far_other[...], scale[0], bias[0], None)


def relayed_kernel(scale, bias, z, block, grad_in, grad):
    grad[...] = grad_in[...] + pair_term(z[...], block[...], scale[0], bias[0], None)


def row_tiles(columns):
    return pl.BlockSpec((TILE, columns), lambda i: (i, 0))


def whole(array):
    return pl.BlockSpec(
        array.shape, lambda i: (0,) * len(array.shape), pipeline_mode=pl.Buffered(1)
    )


def call_tiles(kernel, scale, bias, z, blocks, grads, name, mib):
    rows, columns = z.shape
    return pl.pallas_call(
        kernel,
        grid=(rows // TILE,),
        out_shape=jax.ShapeDtypeStruct((rows, columns), F32),
        in_specs=[SMEM, SMEM, row_tiles(columns)]
        + [whole(b) for b in blocks]
        + [row_tiles(columns)] * len(grads),
        out_specs=row_tiles(columns),
        compiler_params=params(mib),
        name=name,
    )(scale, bias, z, *blocks, *grads)


def last_phase_kernel(
    place, scale, bias, z, block, grad_in, unit, inverse, emb_t, du, *rest
):
    half, (du_all, emb_v, sem) = rest[0], rest[1:]
    step = pl.program_id(0)
    fetch = pltpu.make_async_copy(emb_t, emb_v, sem)

    @pl.when(step == 0)
    def _():
        fetch.start()

    grad = grad_in[...] + pair_term(z[...], block[...], scale[0], bias[0], None)
    grad = scale[0] * grad
    units = unit[...]
    inner = jnp.sum(units * grad, axis=1, keepdims=True)
    rounded = ((grad - units * inner) * inverse[...]).astype(BF16)
    du[...] = rounded
    du_all[pl.ds(pl.multiple_of(step * TILE, TILE), TILE), :] = rounded

    @pl.when(step == pl.num_programs(0) - 1)
    def _():
        fetch.wait()
        height = half.shape[0]
        first = emb_v.shape[0] - 2 * height
        rows = piece_at(place[Z_LOW], 1, height, first)
        half[...] = dot(emb_v[rows, :], du_all[...]).astype(BF16)


def last_phase(place, scale, bias, z, block, grad, unit, inverse, emb_t):
    rows, columns = z.shape
    half = jax.ShapeDtypeStruct((columns // 6, columns), BF16)
    return pl.pallas_call(
        last_phase_kernel,
        grid=(rows // TILE,),
        out_shape=(jax.ShapeDtypeStruct((rows, columns), BF16), half),
        in_specs=[
            SMEM,
            SMEM,
            SMEM,
            row_tiles(columns),
            whole(block),
            row_tiles(columns),
            row_tiles(columns),
            row_tiles(1),
            HBM,
        ],
        out_specs=(row_tiles(columns), whole(half)),
        scratch_shapes=[
            pltpu.VMEM((rows, columns), BF16),
            pltpu.VMEM(emb_t.shape, BF16),
            pltpu.SemaphoreType.DMA,
        ],
        compiler_params=params(28),
        name="last_phase",
    )(place, scale, bias, z, block, grad, unit, inverse, emb_t)


def sent_parts_kernel(place, emb_t, du, *pieces):
    for m, out in enumerate(pieces):
        rows = piece_at(place[IN_PLANE], m + 1, out.shape[0])
        out[...] = dot(emb_t[rows, :], du[...]).astype(out.dtype)


def kept_parts_kernel(place, emb_t, du, keep_a, keep_b):
    height = keep_b.shape[0]
    at_b = emb_t.shape[0] - 2 * height
    for out, rows in (
        (keep_a, piece_at(place[IN_PLANE], 0, height)),
        (keep_b, piece_at(place[Z_LOW], 0, height, at_b)),
    ):
        out[...] = dot(emb_t[rows, :], du[...])


def parts(kernel, place, emb_t, du, kinds, name):
    shape = (emb_t.shape[0] // 6, emb_t.shape[0])
    return pl.pallas_call(
        kernel,
        out_shape=tuple(jax.ShapeDtypeStruct(shape, kind) for kind in kinds),
        in_specs=[SMEM] + [VMEM] * 2,
        out_specs=(VMEM,) * len(kinds),
        compiler_params=params(6),
        name=name,
    )(place, emb_t, du)


def rows_back_kernel(place, du, weight, own, other):
    back = dot_t(du[...], weight[...]).astype(BF16)
    mine = pl.program_id(0) == 1 - place[SAME]

    @pl.when(mine)
    def _():
        own[...] = back

    @pl.when(jnp.logical_not(mine))
    def _():
        other[...] = back


def rows_back(place, du, weight):
    rows, columns = du.shape
    out = jax.ShapeDtypeStruct((TILE, columns), BF16)
    return pl.pallas_call(
        rows_back_kernel,
        grid=(rows // TILE,),
        out_shape=(out, out),
        in_specs=[SMEM, row_tiles(columns), whole(weight)],
        out_specs=(whole(out), whole(out)),
        compiler_params=params(8),
        name="rows_back",
    )(place, du, weight)


def summed(refs):
    one, two, three, four = (ref[...].astype(F32) for ref in refs)
    return (one + two) + (three + four)


def small_call(kernel, place, arrays, outs, scratch, mib, name):
    return pl.pallas_call(
        kernel,
        out_shape=tuple(jax.ShapeDtypeStruct(shape, kind) for shape, kind in outs),
        in_specs=[SMEM] + [VMEM] * len(arrays),
        out_specs=(VMEM,) * len(outs),
        scratch_shapes=[pltpu.VMEM(shape, F32) for shape in scratch],
        compiler_params=params(mib),
        name=name,
    )(place, *arrays)


def add_split_kernel(place, *refs):
    total = refs[8]
    total[...] = summed(refs[:4])
    for m, out in enumerate(refs[4:8]):
        out[...] = total[piece_at(place[IN_LINE], m, out.shape[0]), :].astype(out.dtype)


def add_split(place, parts, name):
    rows, columns = parts[0].shape
    outs = [((rows // 4, columns), F32 if m == 0 else BF16) for m in range(4)]
    return small_call(add_split_kernel, place, parts, outs, [(rows, columns)], 4, name)


def add_all_kernel(place, *refs):
    refs[4][...] = summed(refs[:4]).astype(BF16)


def add_all(place, parts, name):
    return small_call(add_all_kernel, place, parts, [(parts[0].shape, BF16)], [], 2, name)[0]


def join_four_kernel(digit, place, *refs):
    out, total = refs[4:]
    for m, piece in enumerate(refs[:4]):
        total[piece_at(place[digit], m, piece.shape[0]), :] = piece[...].astype(F32)
    out[...] = total[...].astype(BF16)


def join_four(place, digit, parts, name):
    shape = (4 * parts[0].shape[0], parts[0].shape[1])
    kernel = functools.partial(join_four_kernel, digit)
    return small_call(kernel, place, parts, [(shape, BF16)], [shape], 7, name)[0]


def add_halve_kernel(bit, place, keep, got, mine, give, total):
    total[...] = keep[...] + got[...].astype(F32)
    for m, out in enumerate((mine, give)):
        out[...] = total[piece_at(place[bit], m, out.shape[0]), :].astype(out.dtype)


def add_halve(place, bit, keep, got, name):
    rows, columns = keep.shape
    outs = [((rows // 2, columns), kind) for kind in (F32, BF16)]
    kernel = functools.partial(add_halve_kernel, bit)
    return small_call(kernel, place, [keep, got], outs, [keep.shape], 3, name)


def add_two_kernel(place, keep, got, out):
    out[...] = (keep[...] + got[...].astype(F32)).astype(BF16)


def add_two(place, keep, got, name):
    return small_call(add_two_kernel, place, [keep, got], [(keep.shape, BF16)], [], 2, name)[0]


def join_two_kernel(bit, place, mine, got, out, total):
    for m, piece in enumerate((mine, got)):
        total[piece_at(place[bit], m, piece.shape[0]), :] = piece[...].astype(F32)
    out[...] = total[...].astype(BF16)


def join_two(place, bit, mine, got, name):
    shape = (2 * mine.shape[0], mine.shape[1])
    kernel = functools.partial(join_two_kernel, bit)
    return small_call(kernel, place, [mine, got], [(shape, BF16)], [shape], 5, name)[0]


def join_all_kernel(place, *refs):
    out = refs[6]
    for m, piece in enumerate(refs[:4]):
        out[piece_at(place[IN_PLANE], m, piece.shape[0]), :] = piece[...]
    height = refs[4].shape[0]
    for m, piece in enumerate(refs[4:6]):
        out[piece_at(place[Z_LOW], m, height, out.shape[0] - 2 * height), :] = piece[...]


def join_all(place, parts_a, parts_b):
    columns = parts_b[0].shape[1]
    arrays = [*parts_a, *parts_b]
    outs = [((columns, columns), BF16)]
    return small_call(join_all_kernel, place, arrays, outs, [], 3, "join_all")[0]


def widen_kernel(own, place, weight, *refs):
    img_out, txt_out, wide, sems = refs[-4:]
    count = sems.shape[0]
    height = weight.shape[0] // count
    for side, out in enumerate((img_out, txt_out)):

        @pl.when((place[SIDE] == side) == own)
        def _():
            copies = []
            for k in range(count):
                part = slice(k * height, (k + 1) * height)
                wide[part, :] = weight[part, :].astype(F32)
                copies.append(
                    pltpu.make_async_copy(wide.at[part, :], out.at[part, :], sems.at[k])
                )
                copies[-1].start()
            for copy in copies:
                copy.wait()


def widen(place, weight, own, outs, name):
    out = jax.ShapeDtypeStruct(weight.shape, F32)
    return pl.pallas_call(
        functools.partial(widen_kernel, own),
        out_shape=(out, out),
        in_specs=[SMEM, VMEM] + [ANY] * len(outs),
        out_specs=(ANY, ANY),
        scratch_shapes=[pltpu.VMEM(weight.shape, F32), pltpu.SemaphoreType.DMA((9,))],
        input_output_aliases={2: 0, 3: 1} if outs else {},
        compiler_params=params(9),
        name=name,
    )(place, weight, *outs)


def body(img_emb, txt_emb, img_proj, txt_proj, log_scale, bias):
    size = lax.axis_size("dp")
    columns = img_emb.shape[1]
    scale = jnp.exp(log_scale)
    here = lax.axis_index("dp").astype(jnp.int32)
    side, chip = here % 2, here // 2
    bits = [(chip // n) % 2 for n in (1, 2, 4, 8)]
    place = jnp.stack([side, chip % 4, (chip // 4) % 4, (chip + side + 1) % 2, *bits])
    place, scale = lax.optimization_barrier((place, scale))

    pair = lambda value: swap(value, size, 2)
    far_as_d = lambda value: shift(value, size, lambda chip, core: -2 if chip % 2 else 2)

    def raw_target(to_far, to_pair):
        pairs = []
        for i in range(size):
            chip, core = i // 2, i % 2
            if core == chip % 2:
                pairs.append((i, 2 * ((chip + 2 if core else chip - 2) % (size // 2)) + to_far))
            else:
                pairs.append((i, 2 * (chip ^ 1) + to_pair))
        return pairs

    same = (chip + side) % 2 == 0
    raw_one = jnp.where(same, txt_emb, img_emb)
    raw_two = jnp.where(same, img_emb, txt_emb)
    got_one = lax.ppermute(raw_one, "dp", raw_target(0, 1))
    got_two = lax.ppermute(raw_two, "dp", raw_target(1, 0))
    img_other, txt_other, _ = lax.optimization_barrier(
        (swap(img_emb, size, 1), swap(txt_emb, size, 1), raw_one)
    )
    met_s, met_d = met_units(
        place,
        (txt_emb, txt_other),
        (img_emb, img_other),
        img_proj,
        txt_proj,
        True,
        58,
        "own_met",
    )
    img_emb, txt_emb, img_other, txt_other, _ = lax.optimization_barrier(
        (img_emb, txt_emb, img_other, txt_other, met_s)
    )
    unit, inverse, z, weight, emb_t = second_units(
        place, img_emb, txt_emb, img_other, txt_other, img_proj, txt_proj
    )
    got_one, got_two, sent_s, sent_d, _ = lax.optimization_barrier(
        (got_one, got_two, met_s, met_d, emb_t)
    )
    pair_s, far_d = pair(sent_s), far_as_d(sent_d)
    pair_d, far_s = met_units(
        place,
        (got_two, got_one),
        (got_one, got_two),
        img_proj,
        txt_proj,
        False,
        14,
        "raw_met",
    )
    relay_far, relay_pair = pair(far_s), far_as_d(pair_d)
    z, _ = lax.optimization_barrier((z, (pair_d, far_s)))
    grad = call_tiles(own_chip_kernel, scale, bias, z, (met_s, met_d), (), "own_chip", 8)
    pair_s, far_d, _ = lax.optimization_barrier((pair_s, far_d, grad))
    grad = call_tiles(
        first_phase_kernel,
        scale,
        bias,
        z,
        (pair_s, pair_d, far_d, far_s),
        (grad,),
        "first_phase",
        12,
    )

    grad = call_tiles(relayed_kernel, scale, bias, z, (relay_far,), (grad,), "relayed", 10)
    du, give_b = last_phase(
        place, scale, bias, z, relay_pair, grad, unit, inverse, emb_t
    )

    def exchange(sends, masks):
        return [swap(s, size, m) for s, m in zip(sends, masks)]

    plane_masks, line_masks = (2, 4, 6), (8, 16, 24)
    x_bit, y_bit, low_bit, high_bit = (X, 2), (Y, 4), (Z_LOW, 8), (Z_HIGH, 16)

    def halve(keep, got, bit, name):
        keep, give = add_halve(place, bit[0], keep, got, name)
        return keep, swap(give, size, bit[1]), give

    def gather(mine, bit):
        return mine, swap(mine, size, bit[1])

    together = lax.optimization_barrier
    got_b = swap(give_b, size, low_bit[1])
    sends = parts(sent_parts_kernel, place, emb_t, du, (BF16,) * 3, "sent_parts")
    got_a = exchange(sends, plane_masks)
    keep_a, keep_b = parts(kept_parts_kernel, place, emb_t, du, (F32, F32), "kept_parts")
    parts_a = [keep_a, *got_a]
    keep_b, got_b, give_b = halve(keep_b, got_b, high_bit, "b_high")
    du, _ = together((du, give_b))
    d_emb, d_emb_send = rows_back(place, du, weight)
    parts_a, got_b, d_emb_send = together((parts_a, got_b, d_emb_send))
    d_emb_other = swap(d_emb_send, size, 1)

    pieces = add_split(place, parts_a, "a_split")
    parts_a = [pieces[0], *exchange(pieces[:0:-1], line_masks[::-1])]
    got_b, _ = together((got_b, pieces))
    keep_b, got_b, _ = halve(keep_b, got_b, x_bit, "b_x")
    d_img_emb, d_txt_emb = pick(
        place, SIDE, (d_emb, d_emb_other), (d_emb_other, d_emb), "rows_pick"
    )
    keep_b, got_b, _ = halve(keep_b, got_b, y_bit, "b_y")
    shard_b = add_two(place, keep_b, got_b, "b_last")
    parts_a, d_img_emb, d_txt_emb, _ = together((parts_a, d_img_emb, d_txt_emb, shard_b))

    shard_a = add_all(place, parts_a, "a_last")
    if size > 32:
        groups = [[i for i in range(size) if i % 32 == k] for k in range(32)]
        shard_a, shard_b = lax.psum((shard_a, shard_b), "dp", axis_index_groups=groups)
    parts_a = [shard_a, *exchange([shard_a] * 3, line_masks)]
    shard_b, _ = together((shard_b, shard_a))
    shard_b = join_two(place, y_bit[0], *gather(shard_b, y_bit), "b_join_y")
    got_b = swap(shard_b, size, x_bit[1])
    parts_a, _ = together((parts_a, shard_b))

    parts_a, got_b = together((parts_a, got_b))
    piece_a = join_four(place, IN_LINE, parts_a, "a_join")
    got_b, _ = together((got_b, piece_a))
    shard_b = join_two(place, x_bit[0], shard_b, got_b, "b_join_x")
    got_b = swap(shard_b, size, high_bit[1])
    parts_a = [piece_a, *exchange([piece_a] * 3, plane_masks)]
    shard_b = join_two(place, high_bit[0], shard_b, got_b, "b_join_high")
    got_b = swap(shard_b, size, low_bit[1])
    parts_a, got_b = together((parts_a, got_b))

    d_weight = join_all(place, parts_a, (shard_b, got_b))
    d_weight_other = swap(d_weight, size, 1)
    outs = widen(place, d_weight, True, (), "widen_own")
    d_img_proj, d_txt_proj = widen(place, d_weight_other, False, outs, "widen_other")
    return (d_img_emb, d_txt_emb, d_img_proj, d_txt_proj)


def solution(mesh):
    return jax.shard_map(
        body,
        mesh=mesh,
        in_specs=(P("dp", None), P("dp", None), P(), P(), P(), P()),
        out_specs=(P("dp", None), P("dp", None), P(), P()),
        check_vma=False,
    )
```

```python
import functools

import jax
import jax.numpy as jnp
from jax import lax
from jax.experimental import pallas as pl
from jax.experimental.pallas import tpu as pltpu
from jax.sharding import PartitionSpec as P

REACH = 3
BF16, F32 = jnp.bfloat16, jnp.float32
TILE = 512
SIDE, IN_PLANE, IN_LINE, SAME, X, Y, Z_LOW, Z_HIGH = range(8)
VMEM = pl.BlockSpec(memory_space=pltpu.VMEM)
SMEM = pl.BlockSpec(memory_space=pltpu.SMEM)
HBM = pl.BlockSpec(memory_space=pltpu.HBM)
ANY = pl.BlockSpec(memory_space=pl.ANY)


def params(mib):
    return pltpu.CompilerParams(vmem_limit_bytes=mib * 1024 * 1024)


def dot_t(left, right):
    return lax.dot_general(left, right, (((1,), (1,)), ((), ())), preferred_element_type=F32)


def dot(left, right):
    return lax.dot_general(left, right, (((1,), (0,)), ((), ())), preferred_element_type=F32)


def shift(value, size, chips):
    pairs = []
    for i in range(size):
        chip, core = i // 2, i % 2
        pairs.append((i, 2 * ((chip + chips(chip, core)) % (size // 2)) + core))
    return lax.ppermute(value, "dp", pairs)


def swap(value, size, mask):
    return lax.ppermute(value, "dp", [(i, i ^ mask) for i in range(size)])


def met_kernel(own_chip, place, *refs):
    sides, projs, (z_one, z_two, emb_v, proj_v, sems) = (refs[:2], refs[2:4]), refs[4:6], refs[6:]
    cut = proj_v.shape[0] // 256 * 128 + 128
    parts = [slice(0, cut), slice(cut, proj_v.shape[0])]
    for side, (embs, proj) in enumerate(zip(sides, projs)):

        @pl.when(place[SIDE] == side)
        def _():
            first = 1 - place[SAME] if own_chip else 0
            copies = [pltpu.make_async_copy(embs[0], emb_v.at[first], sems.at[2])]
            for k, part in enumerate(parts):
                copies.append(
                    pltpu.make_async_copy(proj.at[part, :], proj_v.at[part, :], sems.at[k])
                )
            copies.append(pltpu.make_async_copy(embs[1], emb_v.at[1 - first], sems.at[3]))
            for copy in copies:
                copy.start()
            for copy in copies:
                copy.wait()

    for k, z in enumerate((z_one, z_two)):
        raw = dot(emb_v[k], proj_v[...])
        scale = lax.rsqrt(jnp.sum(raw * raw, axis=1, keepdims=True) + 1e-06)
        z[...] = (raw * scale).astype(BF16)


def met_units(place, text_side, image_side, img_proj, txt_proj, own_chip, mib, name):
    out = jax.ShapeDtypeStruct(text_side[0].shape, BF16)
    return pl.pallas_call(
        functools.partial(met_kernel, own_chip),
        out_shape=(out, out),
        in_specs=[SMEM] + [HBM] * 6,
        out_specs=(VMEM, VMEM),
        scratch_shapes=[
            pltpu.VMEM((2, *out.shape), BF16),
            pltpu.VMEM(img_proj.shape, BF16),
            pltpu.SemaphoreType.DMA((4,)),
        ],
        compiler_params=params(mib),
        name=name,
    )(place, *text_side, *image_side, txt_proj, img_proj)


def second_kernel(place, *refs):
    sides, (unit, inverse, z, weight, emb_t, emb_v, sems) = (refs[:3], refs[3:6]), refs[6:]
    rows = emb_v.shape[1]
    for side in range(2):

        @pl.when(place[SIDE] == side)
        def _():
            copies = [
                pltpu.make_async_copy(src, dst, sems.at[at])
                for at, (src, dst) in enumerate(
                    zip(sides[side], (weight, emb_v.at[1 - place[SAME]], emb_v.at[place[SAME]]))
                )
            ]
            for copy in copies:
                copy.start()
            for copy in copies:
                copy.wait()

    for half in range(2):
        here = slice(half * rows, (half + 1) * rows)
        raw = dot(emb_v[half], weight[...])
        scale = lax.rsqrt(jnp.sum(raw * raw, axis=1, keepdims=True) + 1e-06)
        inverse[here, :] = scale
        units = raw * scale
        unit[here, :] = units
        z[here, :] = units.astype(BF16)
        emb_t[:, here] = emb_v[half].T


def second_units(place, img_emb, txt_emb, img_other, txt_other, img_proj, txt_proj):
    rows, columns = img_emb.shape
    return pl.pallas_call(
        second_kernel,
        out_shape=(
            jax.ShapeDtypeStruct((2 * rows, columns), F32),
            jax.ShapeDtypeStruct((2 * rows, 1), F32),
            jax.ShapeDtypeStruct((2 * rows, columns), BF16),
            jax.ShapeDtypeStruct(img_proj.shape, BF16),
            jax.ShapeDtypeStruct((columns, 2 * rows), BF16),
        ),
        in_specs=[SMEM] + [HBM] * 6,
        out_specs=(VMEM,) * 5,
        scratch_shapes=[
            pltpu.VMEM((2, rows, columns), BF16),
            pltpu.SemaphoreType.DMA((3,)),
        ],
        compiler_params=params(18),
        name="second_units",
    )(place, img_proj, img_emb, img_other, txt_proj, txt_emb, txt_other)


def piece_at(digit, m, height, first=0):
    return pl.ds(pl.multiple_of(first + (digit ^ m) * height, 8), height)


def pick_kernel(at, place, *refs):
    sources, outs, sems = (refs[:2], refs[2:4]), refs[4:6], refs[6]
    for flag in range(2):

        @pl.when(place[at] == flag)
        def _():
            copies = [
                pltpu.make_async_copy(pair[flag], out, sems.at[k])
                for k, (pair, out) in enumerate(zip(sources, outs))
            ]
            for copy in copies:
                copy.start()
            for copy in copies:
                copy.wait()


def pick(place, at, first, second, name):
    return pl.pallas_call(
        functools.partial(pick_kernel, at),
        out_shape=tuple(jax.ShapeDtypeStruct(p[0].shape, p[0].dtype) for p in (first, second)),
        in_specs=[SMEM] + [ANY] * 4,
        out_specs=(ANY, ANY),
        scratch_shapes=[pltpu.SemaphoreType.DMA((2,))],
        compiler_params=params(1),
        name=name,
    )(place, *first, *second)


def pair_term(z, block, scale, bias, diagonal):
    half = dot_t(z, block) * (0.5 * scale) + 0.5 * bias
    coef = 0.5 * jnp.tanh(half) + 0.5
    if diagonal is not None:
        row_at = lax.broadcasted_iota(jnp.int32, coef.shape, 0) + diagonal
        col_at = lax.broadcasted_iota(jnp.int32, coef.shape, 1)
        coef = jnp.where(row_at == col_at, coef - 1.0, coef)
    return dot(coef.astype(BF16), block)


def own_chip_kernel(scale, bias, z, met, met_other, grad):
    step = pl.program_id(0)
    per_block = met.shape[0] // TILE
    here = step * TILE
    near = pair_term(z[...], met[...], scale[0], bias[0], here)
    other = pair_term(z[...], met_other[...], scale[0], bias[0], here - per_block * TILE)
    grad[...] = near + other


def first_phase_kernel(scale, bias, z, one, two, far_own, far_other, grad_in, grad):
    step = pl.program_id(0)
    per_block = one.shape[0] // TILE
    total = grad_in[...] + pair_term(z[...], one[...], scale[0], bias[0], None)
    total = total + pair_term(z[...], two[...], scale[0], bias[0], None)

    @pl.when(step < per_block)
    def _():
        grad[...] = total + pair_term(z[...], far_own[...], scale[0], bias[0], None)

    @pl.when(step >= per_block)
    def _():
        grad[...] = total + pair_term(z[...], far_other[...], scale[0], bias[0], None)


def relayed_kernel(scale, bias, z, block, grad_in, grad):
    grad[...] = grad_in[...] + pair_term(z[...], block[...], scale[0], bias[0], None)


def row_tiles(columns):
    return pl.BlockSpec((TILE, columns), lambda i: (i, 0))


def whole(array):
    return pl.BlockSpec(
        array.shape, lambda i: (0,) * len(array.shape), pipeline_mode=pl.Buffered(1)
    )


def call_tiles(kernel, scale, bias, z, blocks, grads, name, mib):
    rows, columns = z.shape
    return pl.pallas_call(
        kernel,
        grid=(rows // TILE,),
        out_shape=jax.ShapeDtypeStruct((rows, columns), F32),
        in_specs=[SMEM, SMEM, row_tiles(columns)]
        + [whole(b) for b in blocks]
        + [row_tiles(columns)] * len(grads),
        out_specs=row_tiles(columns),
        compiler_params=params(mib),
        name=name,
    )(scale, bias, z, *blocks, *grads)


def last_phase_kernel(
    place, scale, bias, z, block, grad_in, unit, inverse, emb_t, du, *rest
):
    half, (du_all, emb_v, sem) = rest[0], rest[1:]
    step = pl.program_id(0)
    fetch = pltpu.make_async_copy(emb_t, emb_v, sem)

    @pl.when(step == 0)
    def _():
        fetch.start()

    grad = grad_in[...] + pair_term(z[...], block[...], scale[0], bias[0], None)
    grad = scale[0] * grad
    units = unit[...]
    inner = jnp.sum(units * grad, axis=1, keepdims=True)
    rounded = ((grad - units * inner) * inverse[...]).astype(BF16)
    du[...] = rounded
    du_all[pl.ds(pl.multiple_of(step * TILE, TILE), TILE), :] = rounded

    @pl.when(step == pl.num_programs(0) - 1)
    def _():
        fetch.wait()
        height = half.shape[0]
        first = emb_v.shape[0] - 2 * height
        rows = piece_at(place[Z_LOW], 1, height, first)
        half[...] = dot(emb_v[rows, :], du_all[...]).astype(BF16)


def last_phase(place, scale, bias, z, block, grad, unit, inverse, emb_t):
    rows, columns = z.shape
    half = jax.ShapeDtypeStruct((columns // 6, columns), BF16)
    return pl.pallas_call(
        last_phase_kernel,
        grid=(rows // TILE,),
        out_shape=(jax.ShapeDtypeStruct((rows, columns), BF16), half),
        in_specs=[
            SMEM,
            SMEM,
            SMEM,
            row_tiles(columns),
            whole(block),
            row_tiles(columns),
            row_tiles(columns),
            row_tiles(1),
            HBM,
        ],
        out_specs=(row_tiles(columns), whole(half)),
        scratch_shapes=[
            pltpu.VMEM((rows, columns), BF16),
            pltpu.VMEM(emb_t.shape, BF16),
            pltpu.SemaphoreType.DMA,
        ],
        compiler_params=params(28),
        name="last_phase",
    )(place, scale, bias, z, block, grad, unit, inverse, emb_t)


def sent_parts_kernel(place, emb_t, du, *pieces):
    for m, out in enumerate(pieces):
        rows = piece_at(place[IN_PLANE], m + 1, out.shape[0])
        out[...] = dot(emb_t[rows, :], du[...]).astype(out.dtype)


def kept_parts_kernel(place, emb_t, du, keep_a, keep_b):
    height = keep_b.shape[0]
    at_b = emb_t.shape[0] - 2 * height
    for out, rows in (
        (keep_a, piece_at(place[IN_PLANE], 0, height)),
        (keep_b, piece_at(place[Z_LOW], 0, height, at_b)),
    ):
        out[...] = dot(emb_t[rows, :], du[...])


def parts(kernel, place, emb_t, du, kinds, name):
    shape = (emb_t.shape[0] // 6, emb_t.shape[0])
    return pl.pallas_call(
        kernel,
        out_shape=tuple(jax.ShapeDtypeStruct(shape, kind) for kind in kinds),
        in_specs=[SMEM] + [VMEM] * 2,
        out_specs=(VMEM,) * len(kinds),
        compiler_params=params(6),
        name=name,
    )(place, emb_t, du)


def rows_back_kernel(place, du, weight, own, other):
    back = dot_t(du[...], weight[...]).astype(BF16)
    mine = pl.program_id(0) == 1 - place[SAME]

    @pl.when(mine)
    def _():
        own[...] = back

    @pl.when(jnp.logical_not(mine))
    def _():
        other[...] = back


def rows_back(place, du, weight):
    rows, columns = du.shape
    out = jax.ShapeDtypeStruct((TILE, columns), BF16)
    return pl.pallas_call(
        rows_back_kernel,
        grid=(rows // TILE,),
        out_shape=(out, out),
        in_specs=[SMEM, row_tiles(columns), whole(weight)],
        out_specs=(whole(out), whole(out)),
        compiler_params=params(8),
        name="rows_back",
    )(place, du, weight)


def summed(refs):
    one, two, three, four = (ref[...].astype(F32) for ref in refs)
    return (one + two) + (three + four)


def small_call(kernel, place, arrays, outs, scratch, mib, name):
    return pl.pallas_call(
        kernel,
        out_shape=tuple(jax.ShapeDtypeStruct(shape, kind) for shape, kind in outs),
        in_specs=[SMEM] + [VMEM] * len(arrays),
        out_specs=(VMEM,) * len(outs),
        scratch_shapes=[pltpu.VMEM(shape, F32) for shape in scratch],
        compiler_params=params(mib),
        name=name,
    )(place, *arrays)


def add_split_kernel(place, *refs):
    total = refs[8]
    total[...] = summed(refs[:4])
    for m, out in enumerate(refs[4:8]):
        out[...] = total[piece_at(place[IN_LINE], m, out.shape[0]), :].astype(out.dtype)


def add_split(place, parts, name):
    rows, columns = parts[0].shape
    outs = [((rows // 4, columns), F32 if m == 0 else BF16) for m in range(4)]
    return small_call(add_split_kernel, place, parts, outs, [(rows, columns)], 4, name)


def add_all_kernel(place, *refs):
    refs[4][...] = summed(refs[:4]).astype(BF16)


def add_all(place, parts, name):
    return small_call(add_all_kernel, place, parts, [(parts[0].shape, BF16)], [], 2, name)[0]


def join_four_kernel(digit, place, *refs):
    out, total = refs[4:]
    for m, piece in enumerate(refs[:4]):
        total[piece_at(place[digit], m, piece.shape[0]), :] = piece[...].astype(F32)
    out[...] = total[...].astype(BF16)


def join_four(place, digit, parts, name):
    shape = (4 * parts[0].shape[0], parts[0].shape[1])
    kernel = functools.partial(join_four_kernel, digit)
    return small_call(kernel, place, parts, [(shape, BF16)], [shape], 7, name)[0]


def add_halve_kernel(bit, place, keep, got, mine, give, total):
    total[...] = keep[...] + got[...].astype(F32)
    for m, out in enumerate((mine, give)):
        out[...] = total[piece_at(place[bit], m, out.shape[0]), :].astype(out.dtype)


def add_halve(place, bit, keep, got, name):
    rows, columns = keep.shape
    outs = [((rows // 2, columns), kind) for kind in (F32, BF16)]
    kernel = functools.partial(add_halve_kernel, bit)
    return small_call(kernel, place, [keep, got], outs, [keep.shape], 3, name)


def add_two_kernel(place, keep, got, out):
    out[...] = (keep[...] + got[...].astype(F32)).astype(BF16)


def add_two(place, keep, got, name):
    return small_call(add_two_kernel, place, [keep, got], [(keep.shape, BF16)], [], 2, name)[0]


def join_plane_kernel(place, mine, got_y, got_x, got_xy, out, total):
    height = mine.shape[0]
    for m, (one, two) in enumerate(((mine, got_y), (got_x, got_xy))):
        first = (place[X] ^ m) * 2 * height
        for n, piece in enumerate((one, two)):
            total[piece_at(place[Y], n, height, first), :] = piece[...].astype(F32)
    out[...] = total[...].astype(BF16)


def join_plane(place, pieces, name):
    shape = (4 * pieces[0].shape[0], pieces[0].shape[1])
    return small_call(join_plane_kernel, place, pieces, [(shape, BF16)], [shape], 3, name)[0]


def join_two_kernel(bit, place, mine, got, out, total):
    for m, piece in enumerate((mine, got)):
        total[piece_at(place[bit], m, piece.shape[0]), :] = piece[...].astype(F32)
    out[...] = total[...].astype(BF16)


def join_two(place, bit, mine, got, name):
    shape = (2 * mine.shape[0], mine.shape[1])
    kernel = functools.partial(join_two_kernel, bit)
    return small_call(kernel, place, [mine, got], [(shape, BF16)], [shape], 5, name)[0]


def join_all_kernel(place, *refs):
    out = refs[6]
    for m, piece in enumerate(refs[:4]):
        out[piece_at(place[IN_PLANE], m, piece.shape[0]), :] = piece[...]
    height = refs[4].shape[0]
    for m, piece in enumerate(refs[4:6]):
        out[piece_at(place[Z_LOW], m, height, out.shape[0] - 2 * height), :] = piece[...]


def join_all(place, parts_a, parts_b):
    columns = parts_b[0].shape[1]
    arrays = [*parts_a, *parts_b]
    outs = [((columns, columns), BF16)]
    return small_call(join_all_kernel, place, arrays, outs, [], 3, "join_all")[0]


def widen_kernel(own, place, weight, *refs):
    img_out, txt_out, wide, sems = refs[-4:]
    count = sems.shape[0]
    height = weight.shape[0] // count
    for side, out in enumerate((img_out, txt_out)):

        @pl.when((place[SIDE] == side) == own)
        def _():
            copies = []
            for k in range(count):
                part = slice(k * height, (k + 1) * height)
                wide[part, :] = weight[part, :].astype(F32)
                copies.append(
                    pltpu.make_async_copy(wide.at[part, :], out.at[part, :], sems.at[k])
                )
                copies[-1].start()
            for copy in copies:
                copy.wait()


def widen(place, weight, own, outs, name):
    out = jax.ShapeDtypeStruct(weight.shape, F32)
    return pl.pallas_call(
        functools.partial(widen_kernel, own),
        out_shape=(out, out),
        in_specs=[SMEM, VMEM] + [ANY] * len(outs),
        out_specs=(ANY, ANY),
        scratch_shapes=[pltpu.VMEM(weight.shape, F32), pltpu.SemaphoreType.DMA((9,))],
        input_output_aliases={2: 0, 3: 1} if outs else {},
        compiler_params=params(9),
        name=name,
    )(place, weight, *outs)


def body(img_emb, txt_emb, img_proj, txt_proj, log_scale, bias):
    size = lax.axis_size("dp")
    columns = img_emb.shape[1]
    scale = jnp.exp(log_scale)
    here = lax.axis_index("dp").astype(jnp.int32)
    side, chip = here % 2, here // 2
    bits = [(chip // n) % 2 for n in (1, 2, 4, 8)]
    place = jnp.stack([side, chip % 4, (chip // 4) % 4, (chip + side + 1) % 2, *bits])
    place, scale = lax.optimization_barrier((place, scale))

    pair = lambda value: swap(value, size, 2)
    far_as_d = lambda value: shift(value, size, lambda chip, core: -2 if chip % 2 else 2)

    def raw_target(to_far, to_pair):
        pairs = []
        for i in range(size):
            chip, core = i // 2, i % 2
            if core == chip % 2:
                pairs.append((i, 2 * ((chip + 2 if core else chip - 2) % (size // 2)) + to_far))
            else:
                pairs.append((i, 2 * (chip ^ 1) + to_pair))
        return pairs

    same = (chip + side) % 2 == 0
    raw_one = jnp.where(same, txt_emb, img_emb)
    raw_two = jnp.where(same, img_emb, txt_emb)
    got_one = lax.ppermute(raw_one, "dp", raw_target(0, 1))
    got_two = lax.ppermute(raw_two, "dp", raw_target(1, 0))
    img_other, txt_other, _ = lax.optimization_barrier(
        (swap(img_emb, size, 1), swap(txt_emb, size, 1), raw_one)
    )
    met_s, met_d = met_units(
        place,
        (txt_emb, txt_other),
        (img_emb, img_other),
        img_proj,
        txt_proj,
        True,
        58,
        "own_met",
    )
    img_emb, txt_emb, img_other, txt_other, _ = lax.optimization_barrier(
        (img_emb, txt_emb, img_other, txt_other, met_s)
    )
    unit, inverse, z, weight, emb_t = second_units(
        place, img_emb, txt_emb, img_other, txt_other, img_proj, txt_proj
    )
    got_one, got_two, sent_s, sent_d, _ = lax.optimization_barrier(
        (got_one, got_two, met_s, met_d, emb_t)
    )
    pair_s, far_d = pair(sent_s), far_as_d(sent_d)
    pair_d, far_s = met_units(
        place,
        (got_two, got_one),
        (got_one, got_two),
        img_proj,
        txt_proj,
        False,
        14,
        "raw_met",
    )
    relay_far, relay_pair = pair(far_s), far_as_d(pair_d)
    z, _ = lax.optimization_barrier((z, (pair_d, far_s)))
    grad = call_tiles(own_chip_kernel, scale, bias, z, (met_s, met_d), (), "own_chip", 8)
    pair_s, far_d, _ = lax.optimization_barrier((pair_s, far_d, grad))
    grad = call_tiles(
        first_phase_kernel,
        scale,
        bias,
        z,
        (pair_s, pair_d, far_d, far_s),
        (grad,),
        "first_phase",
        12,
    )

    grad = call_tiles(relayed_kernel, scale, bias, z, (relay_far,), (grad,), "relayed", 10)
    du, give_b = last_phase(
        place, scale, bias, z, relay_pair, grad, unit, inverse, emb_t
    )

    def exchange(sends, masks):
        return [swap(s, size, m) for s, m in zip(sends, masks)]

    plane_masks, line_masks = (2, 4, 6), (8, 16, 24)
    x_bit, y_bit, low_bit, high_bit = (X, 2), (Y, 4), (Z_LOW, 8), (Z_HIGH, 16)

    def halve(keep, got, bit, name):
        keep, give = add_halve(place, bit[0], keep, got, name)
        return keep, swap(give, size, bit[1]), give

    def gather(mine, bit):
        return mine, swap(mine, size, bit[1])

    together = lax.optimization_barrier
    got_b = swap(give_b, size, low_bit[1])
    sends = parts(sent_parts_kernel, place, emb_t, du, (BF16,) * 3, "sent_parts")
    got_a = exchange(sends, plane_masks)
    keep_a, keep_b = parts(kept_parts_kernel, place, emb_t, du, (F32, F32), "kept_parts")
    parts_a = [keep_a, *got_a]
    keep_b, got_b, give_b = halve(keep_b, got_b, high_bit, "b_high")
    du, _ = together((du, give_b))
    d_emb, d_emb_send = rows_back(place, du, weight)
    parts_a, got_b, d_emb_send = together((parts_a, got_b, d_emb_send))
    d_emb_other = swap(d_emb_send, size, 1)

    pieces = add_split(place, parts_a, "a_split")
    parts_a = [pieces[0], *exchange(pieces[:0:-1], line_masks[::-1])]
    got_b, _ = together((got_b, pieces))
    keep_b, got_b, _ = halve(keep_b, got_b, x_bit, "b_x")
    d_img_emb, d_txt_emb = pick(
        place, SIDE, (d_emb, d_emb_other), (d_emb_other, d_emb), "rows_pick"
    )
    keep_b, got_b, _ = halve(keep_b, got_b, y_bit, "b_y")
    shard_b = add_two(place, keep_b, got_b, "b_last")
    parts_a, d_img_emb, d_txt_emb, _ = together((parts_a, d_img_emb, d_txt_emb, shard_b))

    shard_a = add_all(place, parts_a, "a_last")
    if size > 32:
        groups = [[i for i in range(size) if i % 32 == k] for k in range(32)]
        shard_a, shard_b = lax.psum((shard_a, shard_b), "dp", axis_index_groups=groups)
    parts_a = [shard_a, *exchange([shard_a] * 3, line_masks)]
    shard_b, _ = together((shard_b, shard_a))
    got_y, got_x = swap(shard_b, size, y_bit[1]), swap(shard_b, size, x_bit[1])
    got_xy = swap(got_y, size, x_bit[1])
    shard_b = join_plane(place, (shard_b, got_y, got_x, got_xy), "b_join_plane")
    parts_a, _ = together((parts_a, shard_b))

    piece_a = join_four(place, IN_LINE, parts_a, "a_join")
    shard_b, _ = together((shard_b, parts_a[1]))
    got_b = swap(shard_b, size, high_bit[1])
    parts_a = [piece_a, *exchange([piece_a] * 3, plane_masks)]
    shard_b = join_two(place, high_bit[0], shard_b, got_b, "b_join_high")
    got_b = swap(shard_b, size, low_bit[1])
    parts_a, got_b = together((parts_a, got_b))

    d_weight = join_all(place, parts_a, (shard_b, got_b))
    d_weight_other = swap(d_weight, size, 1)
    outs = widen(place, d_weight, True, (), "widen_own")
    d_img_proj, d_txt_proj = widen(place, d_weight_other, False, outs, "widen_other")
    return (d_img_emb, d_txt_emb, d_img_proj, d_txt_proj)


def solution(mesh):
    return jax.shard_map(
        body,
        mesh=mesh,
        in_specs=(P("dp", None), P("dp", None), P(), P(), P(), P()),
        out_specs=(P("dp", None), P("dp", None), P(), P()),
        check_vma=False,
    )
```

```python
import functools

import jax
import jax.numpy as jnp
from jax import lax
from jax.experimental import pallas as pl
from jax.experimental.pallas import tpu as pltpu
from jax.sharding import PartitionSpec as P

REACH = 3
BF16, F32 = jnp.bfloat16, jnp.float32
TILE = 512
SIDE, IN_PLANE, IN_LINE, SAME, X, Y, Z_LOW, Z_HIGH = range(8)
VMEM = pl.BlockSpec(memory_space=pltpu.VMEM)
SMEM = pl.BlockSpec(memory_space=pltpu.SMEM)
HBM = pl.BlockSpec(memory_space=pltpu.HBM)
ANY = pl.BlockSpec(memory_space=pl.ANY)


def params(mib):
    return pltpu.CompilerParams(vmem_limit_bytes=mib * 1024 * 1024)


def dot_t(left, right):
    return lax.dot_general(left, right, (((1,), (1,)), ((), ())), preferred_element_type=F32)


def dot(left, right):
    return lax.dot_general(left, right, (((1,), (0,)), ((), ())), preferred_element_type=F32)


def shift(value, size, chips):
    pairs = []
    for i in range(size):
        chip, core = i // 2, i % 2
        pairs.append((i, 2 * ((chip + chips(chip, core)) % (size // 2)) + core))
    return lax.ppermute(value, "dp", pairs)


def swap(value, size, mask):
    return lax.ppermute(value, "dp", [(i, i ^ mask) for i in range(size)])


def met_kernel(own_chip, place, *refs):
    sides, projs, (z_one, z_two, emb_v, proj_v, sems) = (refs[:2], refs[2:4]), refs[4:6], refs[6:]
    cut = proj_v.shape[0] // 256 * 128 + 128
    parts = [slice(0, cut), slice(cut, proj_v.shape[0])]
    for side, (embs, proj) in enumerate(zip(sides, projs)):

        @pl.when(place[SIDE] == side)
        def _():
            first = 1 - place[SAME] if own_chip else 0
            copies = [pltpu.make_async_copy(embs[0], emb_v.at[first], sems.at[2])]
            for k, part in enumerate(parts):
                copies.append(
                    pltpu.make_async_copy(proj.at[part, :], proj_v.at[part, :], sems.at[k])
                )
            copies.append(pltpu.make_async_copy(embs[1], emb_v.at[1 - first], sems.at[3]))
            for copy in copies:
                copy.start()
            for copy in copies:
                copy.wait()

    for k, z in enumerate((z_one, z_two)):
        raw = dot(emb_v[k], proj_v[...])
        scale = lax.rsqrt(jnp.sum(raw * raw, axis=1, keepdims=True) + 1e-06)
        z[...] = (raw * scale).astype(BF16)


def met_units(place, text_side, image_side, img_proj, txt_proj, own_chip, mib, name):
    out = jax.ShapeDtypeStruct(text_side[0].shape, BF16)
    return pl.pallas_call(
        functools.partial(met_kernel, own_chip),
        out_shape=(out, out),
        in_specs=[SMEM] + [HBM] * 6,
        out_specs=(VMEM, VMEM),
        scratch_shapes=[
            pltpu.VMEM((2, *out.shape), BF16),
            pltpu.VMEM(img_proj.shape, BF16),
            pltpu.SemaphoreType.DMA((4,)),
        ],
        compiler_params=params(mib),
        name=name,
    )(place, *text_side, *image_side, txt_proj, img_proj)


def second_kernel(place, *refs):
    sides, (unit, inverse, z, weight, emb_t, emb_v, sems) = (refs[:3], refs[3:6]), refs[6:]
    rows = emb_v.shape[1]
    for side in range(2):

        @pl.when(place[SIDE] == side)
        def _():
            copies = [
                pltpu.make_async_copy(src, dst, sems.at[at])
                for at, (src, dst) in enumerate(
                    zip(sides[side], (weight, emb_v.at[1 - place[SAME]], emb_v.at[place[SAME]]))
                )
            ]
            for copy in copies:
                copy.start()
            for copy in copies:
                copy.wait()

    for half in range(2):
        here = slice(half * rows, (half + 1) * rows)
        raw = dot(emb_v[half], weight[...])
        scale = lax.rsqrt(jnp.sum(raw * raw, axis=1, keepdims=True) + 1e-06)
        inverse[here, :] = scale
        units = raw * scale
        unit[here, :] = units
        z[here, :] = units.astype(BF16)
        emb_t[:, here] = emb_v[half].T


def second_units(place, img_emb, txt_emb, img_other, txt_other, img_proj, txt_proj):
    rows, columns = img_emb.shape
    return pl.pallas_call(
        second_kernel,
        out_shape=(
            jax.ShapeDtypeStruct((2 * rows, columns), F32),
            jax.ShapeDtypeStruct((2 * rows, 1), F32),
            jax.ShapeDtypeStruct((2 * rows, columns), BF16),
            jax.ShapeDtypeStruct(img_proj.shape, BF16),
            jax.ShapeDtypeStruct((columns, 2 * rows), BF16),
        ),
        in_specs=[SMEM] + [HBM] * 6,
        out_specs=(VMEM,) * 5,
        scratch_shapes=[
            pltpu.VMEM((2, rows, columns), BF16),
            pltpu.SemaphoreType.DMA((3,)),
        ],
        compiler_params=params(18),
        name="second_units",
    )(place, img_proj, img_emb, img_other, txt_proj, txt_emb, txt_other)


def piece_at(digit, m, height, first=0):
    return pl.ds(pl.multiple_of(first + (digit ^ m) * height, 8), height)


def pick_kernel(at, place, *refs):
    sources, outs, sems = (refs[:2], refs[2:4]), refs[4:6], refs[6]
    for flag in range(2):

        @pl.when(place[at] == flag)
        def _():
            copies = [
                pltpu.make_async_copy(pair[flag], out, sems.at[k])
                for k, (pair, out) in enumerate(zip(sources, outs))
            ]
            for copy in copies:
                copy.start()
            for copy in copies:
                copy.wait()


def pick(place, at, first, second, name):
    return pl.pallas_call(
        functools.partial(pick_kernel, at),
        out_shape=tuple(jax.ShapeDtypeStruct(p[0].shape, p[0].dtype) for p in (first, second)),
        in_specs=[SMEM] + [ANY] * 4,
        out_specs=(ANY, ANY),
        scratch_shapes=[pltpu.SemaphoreType.DMA((2,))],
        compiler_params=params(1),
        name=name,
    )(place, *first, *second)


def pair_term(z, block, scale, bias, diagonal):
    half = dot_t(z, block) * (0.5 * scale) + 0.5 * bias
    coef = 0.5 * jnp.tanh(half) + 0.5
    if diagonal is not None:
        row_at = lax.broadcasted_iota(jnp.int32, coef.shape, 0) + diagonal
        col_at = lax.broadcasted_iota(jnp.int32, coef.shape, 1)
        coef = jnp.where(row_at == col_at, coef - 1.0, coef)
    return dot(coef.astype(BF16), block)


def own_chip_kernel(scale, bias, z, met, met_other, grad):
    step = pl.program_id(0)
    per_block = met.shape[0] // TILE
    here = step * TILE
    near = pair_term(z[...], met[...], scale[0], bias[0], here)
    other = pair_term(z[...], met_other[...], scale[0], bias[0], here - per_block * TILE)
    grad[...] = near + other


def first_phase_kernel(scale, bias, z, one, two, far_own, far_other, grad_in, grad):
    step = pl.program_id(0)
    per_block = one.shape[0] // TILE
    total = grad_in[...] + pair_term(z[...], one[...], scale[0], bias[0], None)
    total = total + pair_term(z[...], two[...], scale[0], bias[0], None)

    @pl.when(step < per_block)
    def _():
        grad[...] = total + pair_term(z[...], far_own[...], scale[0], bias[0], None)

    @pl.when(step >= per_block)
    def _():
        grad[...] = total + pair_term(z[...], far_other[...], scale[0], bias[0], None)


def relayed_kernel(scale, bias, z, block, grad_in, grad):
    grad[...] = grad_in[...] + pair_term(z[...], block[...], scale[0], bias[0], None)


def row_tiles(columns):
    return pl.BlockSpec((TILE, columns), lambda i: (i, 0))


def whole(array):
    return pl.BlockSpec(
        array.shape, lambda i: (0,) * len(array.shape), pipeline_mode=pl.Buffered(1)
    )


def call_tiles(kernel, scale, bias, z, blocks, grads, name, mib):
    rows, columns = z.shape
    return pl.pallas_call(
        kernel,
        grid=(rows // TILE,),
        out_shape=jax.ShapeDtypeStruct((rows, columns), F32),
        in_specs=[SMEM, SMEM, row_tiles(columns)]
        + [whole(b) for b in blocks]
        + [row_tiles(columns)] * len(grads),
        out_specs=row_tiles(columns),
        compiler_params=params(mib),
        name=name,
    )(scale, bias, z, *blocks, *grads)


def last_phase_kernel(
    place, scale, bias, z, block, grad_in, unit, inverse, emb_t, du, *rest
):
    half, (du_all, emb_v, sem) = rest[0], rest[1:]
    step = pl.program_id(0)
    fetch = pltpu.make_async_copy(emb_t, emb_v, sem)

    @pl.when(step == 0)
    def _():
        fetch.start()

    grad = grad_in[...] + pair_term(z[...], block[...], scale[0], bias[0], None)
    grad = scale[0] * grad
    units = unit[...]
    inner = jnp.sum(units * grad, axis=1, keepdims=True)
    rounded = ((grad - units * inner) * inverse[...]).astype(BF16)
    du[...] = rounded
    du_all[pl.ds(pl.multiple_of(step * TILE, TILE), TILE), :] = rounded

    @pl.when(step == pl.num_programs(0) - 1)
    def _():
        fetch.wait()
        height = half.shape[0]
        first = emb_v.shape[0] - 2 * height
        rows = piece_at(place[Z_LOW], 1, height, first)
        half[...] = dot(emb_v[rows, :], du_all[...]).astype(BF16)


def last_phase(place, scale, bias, z, block, grad, unit, inverse, emb_t):
    rows, columns = z.shape
    half = jax.ShapeDtypeStruct((columns // 6, columns), BF16)
    return pl.pallas_call(
        last_phase_kernel,
        grid=(rows // TILE,),
        out_shape=(jax.ShapeDtypeStruct((rows, columns), BF16), half),
        in_specs=[
            SMEM,
            SMEM,
            SMEM,
            row_tiles(columns),
            whole(block),
            row_tiles(columns),
            row_tiles(columns),
            row_tiles(1),
            HBM,
        ],
        out_specs=(row_tiles(columns), whole(half)),
        scratch_shapes=[
            pltpu.VMEM((rows, columns), BF16),
            pltpu.VMEM(emb_t.shape, BF16),
            pltpu.SemaphoreType.DMA,
        ],
        compiler_params=params(28),
        name="last_phase",
    )(place, scale, bias, z, block, grad, unit, inverse, emb_t)


def sent_parts_kernel(place, emb_t, du, *pieces):
    for m, out in enumerate(pieces):
        rows = piece_at(place[IN_PLANE], m + 1, out.shape[0])
        out[...] = dot(emb_t[rows, :], du[...]).astype(out.dtype)


def kept_parts_kernel(place, emb_t, du, keep_a, keep_b):
    height = keep_b.shape[0]
    at_b = emb_t.shape[0] - 2 * height
    for out, rows in (
        (keep_a, piece_at(place[IN_PLANE], 0, height)),
        (keep_b, piece_at(place[Z_LOW], 0, height, at_b)),
    ):
        out[...] = dot(emb_t[rows, :], du[...])


def parts(kernel, place, emb_t, du, kinds, name):
    shape = (emb_t.shape[0] // 6, emb_t.shape[0])
    return pl.pallas_call(
        kernel,
        out_shape=tuple(jax.ShapeDtypeStruct(shape, kind) for kind in kinds),
        in_specs=[SMEM] + [VMEM] * 2,
        out_specs=(VMEM,) * len(kinds),
        compiler_params=params(6),
        name=name,
    )(place, emb_t, du)


def rows_back_kernel(place, du, weight, own, other):
    back = dot_t(du[...], weight[...]).astype(BF16)
    mine = pl.program_id(0) == 1 - place[SAME]

    @pl.when(mine)
    def _():
        own[...] = back

    @pl.when(jnp.logical_not(mine))
    def _():
        other[...] = back


def rows_back(place, du, weight):
    rows, columns = du.shape
    out = jax.ShapeDtypeStruct((TILE, columns), BF16)
    return pl.pallas_call(
        rows_back_kernel,
        grid=(rows // TILE,),
        out_shape=(out, out),
        in_specs=[SMEM, row_tiles(columns), whole(weight)],
        out_specs=(whole(out), whole(out)),
        compiler_params=params(8),
        name="rows_back",
    )(place, du, weight)


def summed(refs):
    one, two, three, four = (ref[...].astype(F32) for ref in refs)
    return (one + two) + (three + four)


def small_call(kernel, place, arrays, outs, scratch, mib, name):
    return pl.pallas_call(
        kernel,
        out_shape=tuple(jax.ShapeDtypeStruct(shape, kind) for shape, kind in outs),
        in_specs=[SMEM] + [VMEM] * len(arrays),
        out_specs=(VMEM,) * len(outs),
        scratch_shapes=[pltpu.VMEM(shape, F32) for shape in scratch],
        compiler_params=params(mib),
        name=name,
    )(place, *arrays)


def cut(place, bit, total, mine, give, first=0):
    for m, out in enumerate((mine, give)):
        out[...] = total[piece_at(place[bit], m, out.shape[0], first), :].astype(out.dtype)


def middle_one_kernel(place, *refs):
    parts, (keep, got), outs, (total, total_b) = refs[:4], refs[4:6], refs[6:12], refs[12:]
    total[...] = summed(parts)
    total_b[...] = keep[...] + got[...].astype(F32)
    cut(place, Z_LOW, total, outs[0], outs[1])
    cut(place, Z_HIGH, total, outs[2], outs[3], total.shape[0] // 2)
    cut(place, X, total_b, outs[4], outs[5])


def middle_one(place, parts, keep, got, name):
    rows, columns = parts[0].shape
    shape = (rows // 4, columns)
    outs = [(shape, F32), (shape, BF16)] * 3
    scratch = [(rows, columns), keep.shape]
    return small_call(middle_one_kernel, place, [*parts, keep, got], outs, scratch, 5, name)


def middle_two_kernel(place, *refs):
    (keep_low, got_low, keep_high, got_high, keep, got), outs, total = refs[:6], refs[6:10], refs[10]
    outs[0][...] = (keep_low[...] + got_low[...].astype(F32)).astype(BF16)
    outs[1][...] = (keep_high[...] + got_high[...].astype(F32)).astype(BF16)
    total[...] = keep[...] + got[...].astype(F32)
    cut(place, Y, total, outs[2], outs[3])


def middle_two(place, arrays, name):
    shape = arrays[0].shape
    half = (shape[0] // 2, shape[1])
    outs = [(shape, BF16), (shape, BF16), (half, F32), (half, BF16)]
    return small_call(middle_two_kernel, place, arrays, outs, [shape], 3, name)


def middle_three_kernel(place, *refs):
    for k in range(3):
        refs[6 + k][...] = (refs[2 * k][...].astype(F32) + refs[2 * k + 1][...].astype(F32)).astype(BF16)


def middle_three(place, arrays, name):
    outs = [(array.shape, BF16) for array in arrays[::2]]
    return small_call(middle_three_kernel, place, arrays, outs, [], 2, name)


def middle_four_kernel(place, *refs):
    (low, got_low, high, got_high), quarters = refs[:4], refs[4:8]
    out, out_b, total, total_b = refs[8:]
    height = low.shape[0]
    for m, piece in enumerate((low, got_low)):
        total[piece_at(place[Z_LOW], m, height), :] = piece[...].astype(F32)
    for m, piece in enumerate((high, got_high)):
        total[piece_at(place[Z_HIGH], m, height, 2 * height), :] = piece[...].astype(F32)
    out[...] = total[...].astype(BF16)
    height = quarters[0].shape[0]
    for k, piece in enumerate(quarters):
        first = (place[X] ^ (k // 2)) * 2 * height
        total_b[piece_at(place[Y], k % 2, height, first), :] = piece[...].astype(F32)
    out_b[...] = total_b[...].astype(BF16)


def middle_four(place, arrays, quarters, name):
    shapes = [(4 * a[0].shape[0], a[0].shape[1]) for a in (arrays, quarters)]
    outs = [(shape, BF16) for shape in shapes]
    return small_call(middle_four_kernel, place, [*arrays, *quarters], outs, shapes, 5, name)


def add_halve_kernel(bit, place, keep, got, mine, give, total):
    total[...] = keep[...] + got[...].astype(F32)
    for m, out in enumerate((mine, give)):
        out[...] = total[piece_at(place[bit], m, out.shape[0]), :].astype(out.dtype)


def add_halve(place, bit, keep, got, name):
    rows, columns = keep.shape
    outs = [((rows // 2, columns), kind) for kind in (F32, BF16)]
    kernel = functools.partial(add_halve_kernel, bit)
    return small_call(kernel, place, [keep, got], outs, [keep.shape], 3, name)


def join_two_kernel(bit, place, mine, got, out, total):
    for m, piece in enumerate((mine, got)):
        total[piece_at(place[bit], m, piece.shape[0]), :] = piece[...].astype(F32)
    out[...] = total[...].astype(BF16)


def join_two(place, bit, mine, got, name):
    shape = (2 * mine.shape[0], mine.shape[1])
    kernel = functools.partial(join_two_kernel, bit)
    return small_call(kernel, place, [mine, got], [(shape, BF16)], [shape], 5, name)[0]


def join_all_kernel(place, *refs):
    out = refs[6]
    for m, piece in enumerate(refs[:4]):
        out[piece_at(place[IN_PLANE], m, piece.shape[0]), :] = piece[...]
    height = refs[4].shape[0]
    for m, piece in enumerate(refs[4:6]):
        out[piece_at(place[Z_LOW], m, height, out.shape[0] - 2 * height), :] = piece[...]


def join_all(place, parts_a, parts_b):
    columns = parts_b[0].shape[1]
    arrays = [*parts_a, *parts_b]
    outs = [((columns, columns), BF16)]
    return small_call(join_all_kernel, place, arrays, outs, [], 3, "join_all")[0]


def widen_kernel(own, place, weight, *refs):
    img_out, txt_out, wide, sems = refs[-4:]
    count = sems.shape[0]
    height = weight.shape[0] // count
    for side, out in enumerate((img_out, txt_out)):

        @pl.when((place[SIDE] == side) == own)
        def _():
            copies = []
            for k in range(count):
                part = slice(k * height, (k + 1) * height)
                wide[part, :] = weight[part, :].astype(F32)
                copies.append(
                    pltpu.make_async_copy(wide.at[part, :], out.at[part, :], sems.at[k])
                )
                copies[-1].start()
            for copy in copies:
                copy.wait()


def widen(place, weight, own, outs, name):
    out = jax.ShapeDtypeStruct(weight.shape, F32)
    return pl.pallas_call(
        functools.partial(widen_kernel, own),
        out_shape=(out, out),
        in_specs=[SMEM, VMEM] + [ANY] * len(outs),
        out_specs=(ANY, ANY),
        scratch_shapes=[pltpu.VMEM(weight.shape, F32), pltpu.SemaphoreType.DMA((9,))],
        input_output_aliases={2: 0, 3: 1} if outs else {},
        compiler_params=params(9),
        name=name,
    )(place, weight, *outs)


def body(img_emb, txt_emb, img_proj, txt_proj, log_scale, bias):
    size = lax.axis_size("dp")
    columns = img_emb.shape[1]
    scale = jnp.exp(log_scale)
    here = lax.axis_index("dp").astype(jnp.int32)
    side, chip = here % 2, here // 2
    bits = [(chip // n) % 2 for n in (1, 2, 4, 8)]
    place = jnp.stack([side, chip % 4, (chip // 4) % 4, (chip + side + 1) % 2, *bits])
    place, scale = lax.optimization_barrier((place, scale))

    pair = lambda value: swap(value, size, 2)
    far_as_d = lambda value: shift(value, size, lambda chip, core: -2 if chip % 2 else 2)

    def raw_target(to_far, to_pair):
        pairs = []
        for i in range(size):
            chip, core = i // 2, i % 2
            if core == chip % 2:
                pairs.append((i, 2 * ((chip + 2 if core else chip - 2) % (size // 2)) + to_far))
            else:
                pairs.append((i, 2 * (chip ^ 1) + to_pair))
        return pairs

    same = (chip + side) % 2 == 0
    raw_one = jnp.where(same, txt_emb, img_emb)
    raw_two = jnp.where(same, img_emb, txt_emb)
    got_one = lax.ppermute(raw_one, "dp", raw_target(0, 1))
    got_two = lax.ppermute(raw_two, "dp", raw_target(1, 0))
    img_other, txt_other, _ = lax.optimization_barrier(
        (swap(img_emb, size, 1), swap(txt_emb, size, 1), raw_one)
    )
    met_s, met_d = met_units(
        place,
        (txt_emb, txt_other),
        (img_emb, img_other),
        img_proj,
        txt_proj,
        True,
        58,
        "own_met",
    )
    img_emb, txt_emb, img_other, txt_other, _ = lax.optimization_barrier(
        (img_emb, txt_emb, img_other, txt_other, met_s)
    )
    unit, inverse, z, weight, emb_t = second_units(
        place, img_emb, txt_emb, img_other, txt_other, img_proj, txt_proj
    )
    got_one, got_two, sent_s, sent_d, _ = lax.optimization_barrier(
        (got_one, got_two, met_s, met_d, emb_t)
    )
    pair_s, far_d = pair(sent_s), far_as_d(sent_d)
    pair_d, far_s = met_units(
        place,
        (got_two, got_one),
        (got_one, got_two),
        img_proj,
        txt_proj,
        False,
        14,
        "raw_met",
    )
    relay_far, relay_pair = pair(far_s), far_as_d(pair_d)
    z, _ = lax.optimization_barrier((z, (pair_d, far_s)))
    grad = call_tiles(own_chip_kernel, scale, bias, z, (met_s, met_d), (), "own_chip", 8)
    pair_s, far_d, _ = lax.optimization_barrier((pair_s, far_d, grad))
    grad = call_tiles(
        first_phase_kernel,
        scale,
        bias,
        z,
        (pair_s, pair_d, far_d, far_s),
        (grad,),
        "first_phase",
        12,
    )

    grad = call_tiles(relayed_kernel, scale, bias, z, (relay_far,), (grad,), "relayed", 10)
    du, give_b = last_phase(
        place, scale, bias, z, relay_pair, grad, unit, inverse, emb_t
    )

    def exchange(sends, masks):
        return [swap(s, size, m) for s, m in zip(sends, masks)]

    plane_masks, line_masks = (2, 4, 6), (8, 16, 24)
    x_bit, y_bit, low_bit, high_bit = (X, 2), (Y, 4), (Z_LOW, 8), (Z_HIGH, 16)

    def halve(keep, got, bit, name):
        keep, give = add_halve(place, bit[0], keep, got, name)
        return keep, swap(give, size, bit[1]), give

    def gather(mine, bit):
        return mine, swap(mine, size, bit[1])

    together = lax.optimization_barrier
    got_b = swap(give_b, size, low_bit[1])
    sends = parts(sent_parts_kernel, place, emb_t, du, (BF16,) * 3, "sent_parts")
    got_a = exchange(sends, plane_masks)
    keep_a, keep_b = parts(kept_parts_kernel, place, emb_t, du, (F32, F32), "kept_parts")
    parts_a = [keep_a, *got_a]
    keep_b, got_b, give_b = halve(keep_b, got_b, high_bit, "b_high")
    du, _ = together((du, give_b))
    d_emb, d_emb_send = rows_back(place, du, weight)
    parts_a, got_b, d_emb_send = together((parts_a, got_b, d_emb_send))
    d_emb_other = swap(d_emb_send, size, 1)

    near, far = low_bit[1], high_bit[1]
    keep_low, give_low, keep_high, give_high, keep_b, give_b = middle_one(
        place, parts_a, keep_b, got_b, "middle_one"
    )
    got_high, got_low = swap(give_high, size, far), swap(give_low, size, near)
    got_b = swap(give_b, size, x_bit[1])
    got_low, got_high, got_b = together((got_low, got_high, got_b))
    low, high, keep_b, give_b = middle_two(
        place, (keep_low, got_low, keep_high, got_high, keep_b, got_b), "middle_two"
    )
    got_low, got_high = swap(low, size, far), swap(high, size, near)
    got_b = swap(give_b, size, y_bit[1])
    d_img_emb, d_txt_emb = pick(
        place, SIDE, (d_emb, d_emb_other), (d_emb_other, d_emb), "rows_pick"
    )
    got_low, got_high, got_b, d_img_emb, d_txt_emb = together(
        (got_low, got_high, got_b, d_img_emb, d_txt_emb)
    )
    low, high, shard_b = middle_three(
        place, (low, got_low, high, got_high, keep_b, got_b), "middle_three"
    )
    if size > 32:
        groups = [[i for i in range(size) if i % 32 == k] for k in range(32)]
        low, high, shard_b = lax.psum((low, high, shard_b), "dp", axis_index_groups=groups)
    got_high, got_low = swap(high, size, far), swap(low, size, near)
    got_y, got_x = swap(shard_b, size, y_bit[1]), swap(shard_b, size, x_bit[1])
    got_xy = swap(got_y, size, x_bit[1])
    piece_a, shard_b = middle_four(
        place,
        (low, got_low, high, got_high),
        (shard_b, got_y, got_x, got_xy),
        "middle_four",
    )
    got_b = swap(shard_b, size, high_bit[1])
    parts_a = [piece_a, *exchange([piece_a] * 3, plane_masks)]
    shard_b = join_two(place, high_bit[0], shard_b, got_b, "b_join_high")
    got_b = swap(shard_b, size, low_bit[1])
    parts_a, got_b = together((parts_a, got_b))

    d_weight = join_all(place, parts_a, (shard_b, got_b))
    d_weight_other = swap(d_weight, size, 1)
    outs = widen(place, d_weight, True, (), "widen_own")
    d_img_proj, d_txt_proj = widen(place, d_weight_other, False, outs, "widen_other")
    return (d_img_emb, d_txt_emb, d_img_proj, d_txt_proj)


def solution(mesh):
    return jax.shard_map(
        body,
        mesh=mesh,
        in_specs=(P("dp", None), P("dp", None), P(), P(), P(), P()),
        out_specs=(P("dp", None), P("dp", None), P(), P()),
        check_vma=False,
    )
```

```python
import functools

import jax
import jax.numpy as jnp
from jax import lax
from jax.experimental import pallas as pl
from jax.experimental.pallas import tpu as pltpu
from jax.sharding import PartitionSpec as P

REACH = 3
BF16, F32 = jnp.bfloat16, jnp.float32
TILE = 512
SIDE, IN_PLANE, IN_LINE, SAME, X, Y, Z_LOW, Z_HIGH = range(8)
VMEM = pl.BlockSpec(memory_space=pltpu.VMEM)
SMEM = pl.BlockSpec(memory_space=pltpu.SMEM)
HBM = pl.BlockSpec(memory_space=pltpu.HBM)
ANY = pl.BlockSpec(memory_space=pl.ANY)


def params(mib):
    return pltpu.CompilerParams(vmem_limit_bytes=mib * 1024 * 1024)


def dot_t(left, right):
    return lax.dot_general(left, right, (((1,), (1,)), ((), ())), preferred_element_type=F32)


def dot(left, right):
    return lax.dot_general(left, right, (((1,), (0,)), ((), ())), preferred_element_type=F32)


def shift(value, size, chips):
    pairs = []
    for i in range(size):
        chip, core = i // 2, i % 2
        pairs.append((i, 2 * ((chip + chips(chip, core)) % (size // 2)) + core))
    return lax.ppermute(value, "dp", pairs)


def swap(value, size, mask):
    return lax.ppermute(value, "dp", [(i, i ^ mask) for i in range(size)])


def met_kernel(own_chip, place, *refs):
    sides, projs, (z_one, z_two, emb_v, proj_v, sems) = (refs[:2], refs[2:4]), refs[4:6], refs[6:]
    cut = proj_v.shape[0] // 256 * 128 + 128
    parts = [slice(0, cut), slice(cut, proj_v.shape[0])]
    for side, (embs, proj) in enumerate(zip(sides, projs)):

        @pl.when(place[SIDE] == side)
        def _():
            first = 1 - place[SAME] if own_chip else 0
            copies = [pltpu.make_async_copy(embs[0], emb_v.at[first], sems.at[2])]
            for k, part in enumerate(parts):
                copies.append(
                    pltpu.make_async_copy(proj.at[part, :], proj_v.at[part, :], sems.at[k])
                )
            copies.append(pltpu.make_async_copy(embs[1], emb_v.at[1 - first], sems.at[3]))
            for copy in copies:
                copy.start()
            for copy in copies:
                copy.wait()

    for k, z in enumerate((z_one, z_two)):
        raw = dot(emb_v[k], proj_v[...])
        scale = lax.rsqrt(jnp.sum(raw * raw, axis=1, keepdims=True) + 1e-06)
        z[...] = (raw * scale).astype(BF16)


def met_units(place, text_side, image_side, img_proj, txt_proj, own_chip, mib, name):
    out = jax.ShapeDtypeStruct(text_side[0].shape, BF16)
    return pl.pallas_call(
        functools.partial(met_kernel, own_chip),
        out_shape=(out, out),
        in_specs=[SMEM] + [HBM] * 6,
        out_specs=(VMEM, VMEM),
        scratch_shapes=[
            pltpu.VMEM((2, *out.shape), BF16),
            pltpu.VMEM(img_proj.shape, BF16),
            pltpu.SemaphoreType.DMA((4,)),
        ],
        compiler_params=params(mib),
        name=name,
    )(place, *text_side, *image_side, txt_proj, img_proj)


def second_kernel(place, *refs):
    sides, (unit, inverse, z, weight, emb_t, emb_v, sems) = (refs[:3], refs[3:6]), refs[6:]
    rows = emb_v.shape[1]
    for side in range(2):

        @pl.when(place[SIDE] == side)
        def _():
            copies = [
                pltpu.make_async_copy(src, dst, sems.at[at])
                for at, (src, dst) in enumerate(
                    zip(sides[side], (weight, emb_v.at[1 - place[SAME]], emb_v.at[place[SAME]]))
                )
            ]
            for copy in copies:
                copy.start()
            for copy in copies:
                copy.wait()

    for half in range(2):
        here = slice(half * rows, (half + 1) * rows)
        raw = dot(emb_v[half], weight[...])
        scale = lax.rsqrt(jnp.sum(raw * raw, axis=1, keepdims=True) + 1e-06)
        inverse[here, :] = scale
        units = raw * scale
        unit[here, :] = units
        z[here, :] = units.astype(BF16)
        emb_t[:, here] = emb_v[half].T


def second_units(place, img_emb, txt_emb, img_other, txt_other, img_proj, txt_proj):
    rows, columns = img_emb.shape
    return pl.pallas_call(
        second_kernel,
        out_shape=(
            jax.ShapeDtypeStruct((2 * rows, columns), F32),
            jax.ShapeDtypeStruct((2 * rows, 1), F32),
            jax.ShapeDtypeStruct((2 * rows, columns), BF16),
            jax.ShapeDtypeStruct(img_proj.shape, BF16),
            jax.ShapeDtypeStruct((columns, 2 * rows), BF16),
        ),
        in_specs=[SMEM] + [HBM] * 6,
        out_specs=(VMEM,) * 5,
        scratch_shapes=[
            pltpu.VMEM((2, rows, columns), BF16),
            pltpu.SemaphoreType.DMA((3,)),
        ],
        compiler_params=params(18),
        name="second_units",
    )(place, img_proj, img_emb, img_other, txt_proj, txt_emb, txt_other)


def piece_at(digit, m, height, first=0):
    return pl.ds(pl.multiple_of(first + (digit ^ m) * height, 8), height)


def pick_kernel(at, place, *refs):
    sources, outs, sems = (refs[:2], refs[2:4]), refs[4:6], refs[6]
    for flag in range(2):

        @pl.when(place[at] == flag)
        def _():
            copies = [
                pltpu.make_async_copy(pair[flag], out, sems.at[k])
                for k, (pair, out) in enumerate(zip(sources, outs))
            ]
            for copy in copies:
                copy.start()
            for copy in copies:
                copy.wait()


def pick(place, at, first, second, name):
    return pl.pallas_call(
        functools.partial(pick_kernel, at),
        out_shape=tuple(jax.ShapeDtypeStruct(p[0].shape, p[0].dtype) for p in (first, second)),
        in_specs=[SMEM] + [ANY] * 4,
        out_specs=(ANY, ANY),
        scratch_shapes=[pltpu.SemaphoreType.DMA((2,))],
        compiler_params=params(1),
        name=name,
    )(place, *first, *second)


def pair_term(z, block, scale, bias, diagonal):
    half = dot_t(z, block) * (0.5 * scale) + 0.5 * bias
    coef = 0.5 * jnp.tanh(half) + 0.5
    if diagonal is not None:
        row_at = lax.broadcasted_iota(jnp.int32, coef.shape, 0) + diagonal
        col_at = lax.broadcasted_iota(jnp.int32, coef.shape, 1)
        coef = jnp.where(row_at == col_at, coef - 1.0, coef)
    return dot(coef.astype(BF16), block)


def own_chip_kernel(scale, bias, z, met, met_other, grad):
    step = pl.program_id(0)
    per_block = met.shape[0] // TILE
    here = step * TILE
    near = pair_term(z[...], met[...], scale[0], bias[0], here)
    other = pair_term(z[...], met_other[...], scale[0], bias[0], here - per_block * TILE)
    grad[...] = near + other


def first_phase_kernel(scale, bias, z, one, two, far_own, far_other, grad_in, grad):
    step = pl.program_id(0)
    per_block = one.shape[0] // TILE
    total = grad_in[...] + pair_term(z[...], one[...], scale[0], bias[0], None)
    total = total + pair_term(z[...], two[...], scale[0], bias[0], None)

    @pl.when(step < per_block)
    def _():
        grad[...] = total + pair_term(z[...], far_own[...], scale[0], bias[0], None)

    @pl.when(step >= per_block)
    def _():
        grad[...] = total + pair_term(z[...], far_other[...], scale[0], bias[0], None)


def relayed_kernel(scale, bias, z, block, grad_in, grad):
    grad[...] = grad_in[...] + pair_term(z[...], block[...], scale[0], bias[0], None)


def row_tiles(columns):
    return pl.BlockSpec((TILE, columns), lambda i: (i, 0))


def whole(array):
    return pl.BlockSpec(
        array.shape, lambda i: (0,) * len(array.shape), pipeline_mode=pl.Buffered(1)
    )


def call_tiles(kernel, scale, bias, z, blocks, grads, name, mib):
    rows, columns = z.shape
    return pl.pallas_call(
        kernel,
        grid=(rows // TILE,),
        out_shape=jax.ShapeDtypeStruct((rows, columns), F32),
        in_specs=[SMEM, SMEM, row_tiles(columns)]
        + [whole(b) for b in blocks]
        + [row_tiles(columns)] * len(grads),
        out_specs=row_tiles(columns),
        compiler_params=params(mib),
        name=name,
    )(scale, bias, z, *blocks, *grads)


def last_phase_kernel(
    place, scale, bias, z, block, grad_in, unit, inverse, emb_t, du, *rest
):
    half, (du_all, emb_v, sem) = rest[0], rest[1:]
    step = pl.program_id(0)
    fetch = pltpu.make_async_copy(emb_t, emb_v, sem)

    @pl.when(step == 0)
    def _():
        fetch.start()

    grad = grad_in[...] + pair_term(z[...], block[...], scale[0], bias[0], None)
    grad = scale[0] * grad
    units = unit[...]
    inner = jnp.sum(units * grad, axis=1, keepdims=True)
    rounded = ((grad - units * inner) * inverse[...]).astype(BF16)
    du[...] = rounded
    du_all[pl.ds(pl.multiple_of(step * TILE, TILE), TILE), :] = rounded

    @pl.when(step == pl.num_programs(0) - 1)
    def _():
        fetch.wait()
        height = half.shape[0]
        first = emb_v.shape[0] - 2 * height
        rows = piece_at(place[Z_LOW], 1, height, first)
        half[...] = dot(emb_v[rows, :], du_all[...]).astype(BF16)


def last_phase(place, scale, bias, z, block, grad, unit, inverse, emb_t):
    rows, columns = z.shape
    half = jax.ShapeDtypeStruct((columns // 6, columns), BF16)
    return pl.pallas_call(
        last_phase_kernel,
        grid=(rows // TILE,),
        out_shape=(jax.ShapeDtypeStruct((rows, columns), BF16), half),
        in_specs=[
            SMEM,
            SMEM,
            SMEM,
            row_tiles(columns),
            whole(block),
            row_tiles(columns),
            row_tiles(columns),
            row_tiles(1),
            HBM,
        ],
        out_specs=(row_tiles(columns), whole(half)),
        scratch_shapes=[
            pltpu.VMEM((rows, columns), BF16),
            pltpu.VMEM(emb_t.shape, BF16),
            pltpu.SemaphoreType.DMA,
        ],
        compiler_params=params(28),
        name="last_phase",
    )(place, scale, bias, z, block, grad, unit, inverse, emb_t)


def sent_parts_kernel(place, emb_t, du, *pieces):
    for m, out in enumerate(pieces):
        rows = piece_at(place[IN_PLANE], m + 1, out.shape[0])
        out[...] = dot(emb_t[rows, :], du[...]).astype(out.dtype)


def kept_parts_kernel(place, emb_t, du, keep_a, keep_b):
    height = keep_b.shape[0]
    at_b = emb_t.shape[0] - 2 * height
    for out, rows in (
        (keep_a, piece_at(place[IN_PLANE], 0, height)),
        (keep_b, piece_at(place[Z_LOW], 0, height, at_b)),
    ):
        out[...] = dot(emb_t[rows, :], du[...])


def parts(kernel, place, emb_t, du, kinds, name):
    shape = (emb_t.shape[0] // 6, emb_t.shape[0])
    return pl.pallas_call(
        kernel,
        out_shape=tuple(jax.ShapeDtypeStruct(shape, kind) for kind in kinds),
        in_specs=[SMEM] + [VMEM] * 2,
        out_specs=(VMEM,) * len(kinds),
        compiler_params=params(6),
        name=name,
    )(place, emb_t, du)


def rows_back_kernel(place, du, weight, own, other):
    back = dot_t(du[...], weight[...]).astype(BF16)
    mine = pl.program_id(0) == 1 - place[SAME]

    @pl.when(mine)
    def _():
        own[...] = back

    @pl.when(jnp.logical_not(mine))
    def _():
        other[...] = back


def rows_back(place, du, weight):
    rows, columns = du.shape
    out = jax.ShapeDtypeStruct((TILE, columns), BF16)
    return pl.pallas_call(
        rows_back_kernel,
        grid=(rows // TILE,),
        out_shape=(out, out),
        in_specs=[SMEM, row_tiles(columns), whole(weight)],
        out_specs=(whole(out), whole(out)),
        compiler_params=params(8),
        name="rows_back",
    )(place, du, weight)


def summed(refs):
    one, two, three, four = (ref[...].astype(F32) for ref in refs)
    return (one + two) + (three + four)


def small_call(kernel, place, arrays, outs, scratch, mib, name):
    return pl.pallas_call(
        kernel,
        out_shape=tuple(jax.ShapeDtypeStruct(shape, kind) for shape, kind in outs),
        in_specs=[SMEM] + [VMEM] * len(arrays),
        out_specs=(VMEM,) * len(outs),
        scratch_shapes=[pltpu.VMEM(shape, F32) for shape in scratch],
        compiler_params=params(mib),
        name=name,
    )(place, *arrays)


def cut(place, bit, total, mine, give, first=0):
    for m, out in enumerate((mine, give)):
        out[...] = total[piece_at(place[bit], m, out.shape[0], first), :].astype(out.dtype)


def middle_one_kernel(place, *refs):
    parts, (keep, got), outs, (total, total_b) = refs[:4], refs[4:6], refs[6:12], refs[12:]
    total[...] = summed(parts)
    total_b[...] = keep[...] + got[...].astype(F32)
    cut(place, Z_LOW, total, outs[0], outs[1])
    cut(place, Z_HIGH, total, outs[2], outs[3], total.shape[0] // 2)
    cut(place, X, total_b, outs[4], outs[5])


def middle_one(place, parts, keep, got, name):
    rows, columns = parts[0].shape
    shape = (rows // 4, columns)
    outs = [(shape, F32), (shape, BF16)] * 3
    scratch = [(rows, columns), keep.shape]
    return small_call(middle_one_kernel, place, [*parts, keep, got], outs, scratch, 5, name)


def middle_two_kernel(place, *refs):
    for k in range(3):
        refs[6 + k][...] = (refs[2 * k][...] + refs[2 * k + 1][...].astype(F32)).astype(BF16)


def middle_two(place, arrays, name):
    outs = [(array.shape, BF16) for array in arrays[::2]]
    return small_call(middle_two_kernel, place, arrays, outs, [], 3, name)


def middle_three_kernel(place, *refs):
    for k in range(3):
        refs[6 + k][...] = (refs[2 * k][...].astype(F32) + refs[2 * k + 1][...].astype(F32)).astype(BF16)


def middle_three(place, arrays, name):
    outs = [(array.shape, BF16) for array in arrays[::2]]
    return small_call(middle_three_kernel, place, arrays, outs, [], 2, name)


def middle_four_kernel(place, *refs):
    (low, got_low, high, got_high), (mine, got) = refs[:4], refs[4:6]
    out, out_b, total, total_b = refs[6:]
    height = low.shape[0]
    for m, piece in enumerate((low, got_low)):
        total[piece_at(place[Z_LOW], m, height), :] = piece[...].astype(F32)
    for m, piece in enumerate((high, got_high)):
        total[piece_at(place[Z_HIGH], m, height, 2 * height), :] = piece[...].astype(F32)
    out[...] = total[...].astype(BF16)
    for m, piece in enumerate((mine, got)):
        total_b[piece_at(place[X], m, mine.shape[0]), :] = piece[...].astype(F32)
    out_b[...] = total_b[...].astype(BF16)


def middle_four(place, arrays, pair, name):
    shapes = [(len(a) * a[0].shape[0], a[0].shape[1]) for a in (arrays, pair)]
    outs = [(shape, BF16) for shape in shapes]
    return small_call(middle_four_kernel, place, [*arrays, *pair], outs, shapes, 5, name)


def add_halve_kernel(bit, place, keep, got, mine, give, total):
    total[...] = keep[...] + got[...].astype(F32)
    for m, out in enumerate((mine, give)):
        out[...] = total[piece_at(place[bit], m, out.shape[0]), :].astype(out.dtype)


def add_halve(place, bit, keep, got, name):
    rows, columns = keep.shape
    outs = [((rows // 2, columns), kind) for kind in (F32, BF16)]
    kernel = functools.partial(add_halve_kernel, bit)
    return small_call(kernel, place, [keep, got], outs, [keep.shape], 3, name)


def join_two_kernel(bit, place, mine, got, out, total):
    for m, piece in enumerate((mine, got)):
        total[piece_at(place[bit], m, piece.shape[0]), :] = piece[...].astype(F32)
    out[...] = total[...].astype(BF16)


def join_two(place, bit, mine, got, name):
    shape = (2 * mine.shape[0], mine.shape[1])
    kernel = functools.partial(join_two_kernel, bit)
    return small_call(kernel, place, [mine, got], [(shape, BF16)], [shape], 5, name)[0]


def join_all_kernel(place, *refs):
    out = refs[6]
    for m, piece in enumerate(refs[:4]):
        out[piece_at(place[IN_PLANE], m, piece.shape[0]), :] = piece[...]
    height = refs[4].shape[0]
    for m, piece in enumerate(refs[4:6]):
        out[piece_at(place[Z_LOW], m, height, out.shape[0] - 2 * height), :] = piece[...]


def join_all(place, parts_a, parts_b):
    columns = parts_b[0].shape[1]
    arrays = [*parts_a, *parts_b]
    outs = [((columns, columns), BF16)]
    return small_call(join_all_kernel, place, arrays, outs, [], 3, "join_all")[0]


def widen_kernel(own, place, weight, *refs):
    img_out, txt_out, wide, sems = refs[-4:]
    count = sems.shape[0]
    height = weight.shape[0] // count
    for side, out in enumerate((img_out, txt_out)):

        @pl.when((place[SIDE] == side) == own)
        def _():
            copies = []
            for k in range(count):
                part = slice(k * height, (k + 1) * height)
                wide[part, :] = weight[part, :].astype(F32)
                copies.append(
                    pltpu.make_async_copy(wide.at[part, :], out.at[part, :], sems.at[k])
                )
                copies[-1].start()
            for copy in copies:
                copy.wait()


def widen(place, weight, own, outs, name):
    out = jax.ShapeDtypeStruct(weight.shape, F32)
    return pl.pallas_call(
        functools.partial(widen_kernel, own),
        out_shape=(out, out),
        in_specs=[SMEM, VMEM] + [ANY] * len(outs),
        out_specs=(ANY, ANY),
        scratch_shapes=[pltpu.VMEM(weight.shape, F32), pltpu.SemaphoreType.DMA((9,))],
        input_output_aliases={2: 0, 3: 1} if outs else {},
        compiler_params=params(9),
        name=name,
    )(place, weight, *outs)


def body(img_emb, txt_emb, img_proj, txt_proj, log_scale, bias):
    size = lax.axis_size("dp")
    columns = img_emb.shape[1]
    scale = jnp.exp(log_scale)
    here = lax.axis_index("dp").astype(jnp.int32)
    side, chip = here % 2, here // 2
    bits = [(chip // n) % 2 for n in (1, 2, 4, 8)]
    place = jnp.stack([side, chip % 4, (chip // 4) % 4, (chip + side + 1) % 2, *bits])
    place, scale = lax.optimization_barrier((place, scale))

    pair = lambda value: swap(value, size, 2)
    far_as_d = lambda value: shift(value, size, lambda chip, core: -2 if chip % 2 else 2)

    def raw_target(to_far, to_pair):
        pairs = []
        for i in range(size):
            chip, core = i // 2, i % 2
            if core == chip % 2:
                pairs.append((i, 2 * ((chip + 2 if core else chip - 2) % (size // 2)) + to_far))
            else:
                pairs.append((i, 2 * (chip ^ 1) + to_pair))
        return pairs

    same = (chip + side) % 2 == 0
    raw_one = jnp.where(same, txt_emb, img_emb)
    raw_two = jnp.where(same, img_emb, txt_emb)
    got_one = lax.ppermute(raw_one, "dp", raw_target(0, 1))
    got_two = lax.ppermute(raw_two, "dp", raw_target(1, 0))
    img_other, txt_other, _ = lax.optimization_barrier(
        (swap(img_emb, size, 1), swap(txt_emb, size, 1), raw_one)
    )
    met_s, met_d = met_units(
        place,
        (txt_emb, txt_other),
        (img_emb, img_other),
        img_proj,
        txt_proj,
        True,
        58,
        "own_met",
    )
    img_emb, txt_emb, img_other, txt_other, _ = lax.optimization_barrier(
        (img_emb, txt_emb, img_other, txt_other, met_s)
    )
    unit, inverse, z, weight, emb_t = second_units(
        place, img_emb, txt_emb, img_other, txt_other, img_proj, txt_proj
    )
    got_one, got_two, sent_s, sent_d, _ = lax.optimization_barrier(
        (got_one, got_two, met_s, met_d, emb_t)
    )
    pair_s, far_d = pair(sent_s), far_as_d(sent_d)
    pair_d, far_s = met_units(
        place,
        (got_two, got_one),
        (got_one, got_two),
        img_proj,
        txt_proj,
        False,
        14,
        "raw_met",
    )
    relay_far, relay_pair = pair(far_s), far_as_d(pair_d)
    z, _ = lax.optimization_barrier((z, (pair_d, far_s)))
    grad = call_tiles(own_chip_kernel, scale, bias, z, (met_s, met_d), (), "own_chip", 8)
    pair_s, far_d, _ = lax.optimization_barrier((pair_s, far_d, grad))
    grad = call_tiles(
        first_phase_kernel,
        scale,
        bias,
        z,
        (pair_s, pair_d, far_d, far_s),
        (grad,),
        "first_phase",
        12,
    )

    grad = call_tiles(relayed_kernel, scale, bias, z, (relay_far,), (grad,), "relayed", 10)
    du, give_b = last_phase(
        place, scale, bias, z, relay_pair, grad, unit, inverse, emb_t
    )

    def exchange(sends, masks):
        return [swap(s, size, m) for s, m in zip(sends, masks)]

    plane_masks, line_masks = (2, 4, 6), (8, 16, 24)
    x_bit, y_bit, low_bit, high_bit = (X, 2), (Y, 4), (Z_LOW, 8), (Z_HIGH, 16)

    def halve(keep, got, bit, name):
        keep, give = add_halve(place, bit[0], keep, got, name)
        return keep, swap(give, size, bit[1]), give

    def gather(mine, bit):
        return mine, swap(mine, size, bit[1])

    together = lax.optimization_barrier
    got_b = swap(give_b, size, low_bit[1])
    sends = parts(sent_parts_kernel, place, emb_t, du, (BF16,) * 3, "sent_parts")
    got_a = exchange(sends, plane_masks)
    keep_a, keep_b = parts(kept_parts_kernel, place, emb_t, du, (F32, F32), "kept_parts")
    parts_a = [keep_a, *got_a]
    keep_b, got_b, give_b = halve(keep_b, got_b, high_bit, "b_high")
    du, _ = together((du, give_b))
    d_emb, d_emb_send = rows_back(place, du, weight)
    parts_a, got_b, d_emb_send = together((parts_a, got_b, d_emb_send))
    d_emb_other = swap(d_emb_send, size, 1)

    near, far = low_bit[1], high_bit[1]
    keep_low, give_low, keep_high, give_high, keep_b, give_b = middle_one(
        place, parts_a, keep_b, got_b, "middle_one"
    )
    got_high, got_low = swap(give_high, size, far), swap(give_low, size, near)
    got_b = swap(give_b, size, x_bit[1])
    got_low, got_high, got_b = together((got_low, got_high, got_b))
    low, high, shard_b = middle_two(
        place, (keep_low, got_low, keep_high, got_high, keep_b, got_b), "middle_two"
    )
    got_low, got_high = swap(low, size, far), swap(high, size, near)
    got_b = swap(shard_b, size, y_bit[1])
    d_img_emb, d_txt_emb = pick(
        place, SIDE, (d_emb, d_emb_other), (d_emb_other, d_emb), "rows_pick"
    )
    got_low, got_high, got_b, d_img_emb, d_txt_emb = together(
        (got_low, got_high, got_b, d_img_emb, d_txt_emb)
    )
    low, high, shard_b = middle_three(
        place, (low, got_low, high, got_high, shard_b, got_b), "middle_three"
    )
    if size > 32:
        groups = [[i for i in range(size) if i % 32 == k] for k in range(32)]
        low, high, shard_b = lax.psum((low, high, shard_b), "dp", axis_index_groups=groups)
    got_high, got_low = swap(high, size, far), swap(low, size, near)
    got_b = swap(shard_b, size, x_bit[1])
    piece_a, shard_b = middle_four(
        place, (low, got_low, high, got_high), (shard_b, got_b), "middle_four"
    )
    got_b = swap(shard_b, size, high_bit[1])
    parts_a = [piece_a, *exchange([piece_a] * 3, plane_masks)]
    shard_b = join_two(place, high_bit[0], shard_b, got_b, "b_join_high")
    got_b = swap(shard_b, size, low_bit[1])
    parts_a, got_b = together((parts_a, got_b))

    d_weight = join_all(place, parts_a, (shard_b, got_b))
    d_weight_other = swap(d_weight, size, 1)
    outs = widen(place, d_weight, True, (), "widen_own")
    d_img_proj, d_txt_proj = widen(place, d_weight_other, False, outs, "widen_other")
    return (d_img_emb, d_txt_emb, d_img_proj, d_txt_proj)


def solution(mesh):
    return jax.shard_map(
        body,
        mesh=mesh,
        in_specs=(P("dp", None), P("dp", None), P(), P(), P(), P()),
        out_specs=(P("dp", None), P("dp", None), P(), P()),
        check_vma=False,
    )
```

```python
import functools

import jax
import jax.numpy as jnp
from jax import lax
from jax.experimental import pallas as pl
from jax.experimental.pallas import tpu as pltpu
from jax.sharding import PartitionSpec as P

REACH = 3
BF16, F32 = jnp.bfloat16, jnp.float32
TILE = 512
SIDE, IN_PLANE, IN_LINE, SAME, X, Y, Z_LOW, Z_HIGH = range(8)
VMEM = pl.BlockSpec(memory_space=pltpu.VMEM)
SMEM = pl.BlockSpec(memory_space=pltpu.SMEM)
HBM = pl.BlockSpec(memory_space=pltpu.HBM)
ANY = pl.BlockSpec(memory_space=pl.ANY)


def params(mib):
    return pltpu.CompilerParams(vmem_limit_bytes=mib * 1024 * 1024)


def dot_t(left, right):
    return lax.dot_general(left, right, (((1,), (1,)), ((), ())), preferred_element_type=F32)


def dot(left, right):
    return lax.dot_general(left, right, (((1,), (0,)), ((), ())), preferred_element_type=F32)


def shift(value, size, chips):
    pairs = []
    for i in range(size):
        chip, core = i // 2, i % 2
        pairs.append((i, 2 * ((chip + chips(chip, core)) % (size // 2)) + core))
    return lax.ppermute(value, "dp", pairs)


def swap(value, size, mask):
    return lax.ppermute(value, "dp", [(i, i ^ mask) for i in range(size)])


def met_kernel(own_chip, place, *refs):
    sides, projs, (z_one, z_two, emb_v, proj_v, sems) = (refs[:2], refs[2:4]), refs[4:6], refs[6:]
    cut = proj_v.shape[0] // 256 * 128 + 128
    parts = [slice(0, cut), slice(cut, proj_v.shape[0])]
    for side, (embs, proj) in enumerate(zip(sides, projs)):

        @pl.when(place[SIDE] == side)
        def _():
            first = 1 - place[SAME] if own_chip else 0
            copies = [pltpu.make_async_copy(embs[0], emb_v.at[first], sems.at[2])]
            for k, part in enumerate(parts):
                copies.append(
                    pltpu.make_async_copy(proj.at[part, :], proj_v.at[part, :], sems.at[k])
                )
            copies.append(pltpu.make_async_copy(embs[1], emb_v.at[1 - first], sems.at[3]))
            for copy in copies:
                copy.start()
            for copy in copies:
                copy.wait()

    for k, z in enumerate((z_one, z_two)):
        raw = dot(emb_v[k], proj_v[...])
        scale = lax.rsqrt(jnp.sum(raw * raw, axis=1, keepdims=True) + 1e-06)
        z[...] = (raw * scale).astype(BF16)


def met_units(place, text_side, image_side, img_proj, txt_proj, own_chip, mib, name):
    out = jax.ShapeDtypeStruct(text_side[0].shape, BF16)
    return pl.pallas_call(
        functools.partial(met_kernel, own_chip),
        out_shape=(out, out),
        in_specs=[SMEM] + [HBM] * 6,
        out_specs=(VMEM, VMEM),
        scratch_shapes=[
            pltpu.VMEM((2, *out.shape), BF16),
            pltpu.VMEM(img_proj.shape, BF16),
            pltpu.SemaphoreType.DMA((4,)),
        ],
        compiler_params=params(mib),
        name=name,
    )(place, *text_side, *image_side, txt_proj, img_proj)


def second_kernel(place, *refs):
    sides, (unit, inverse, z, weight, emb_t, emb_v, sems) = (refs[:3], refs[3:6]), refs[6:]
    rows = emb_v.shape[1]
    for side in range(2):

        @pl.when(place[SIDE] == side)
        def _():
            copies = [
                pltpu.make_async_copy(src, dst, sems.at[at])
                for at, (src, dst) in enumerate(
                    zip(sides[side], (weight, emb_v.at[1 - place[SAME]], emb_v.at[place[SAME]]))
                )
            ]
            for copy in copies:
                copy.start()
            for copy in copies:
                copy.wait()

    for half in range(2):
        here = slice(half * rows, (half + 1) * rows)
        raw = dot(emb_v[half], weight[...])
        scale = lax.rsqrt(jnp.sum(raw * raw, axis=1, keepdims=True) + 1e-06)
        inverse[here, :] = scale
        units = raw * scale
        unit[here, :] = units
        z[here, :] = units.astype(BF16)
        emb_t[:, here] = emb_v[half].T


def second_units(place, img_emb, txt_emb, img_other, txt_other, img_proj, txt_proj):
    rows, columns = img_emb.shape
    return pl.pallas_call(
        second_kernel,
        out_shape=(
            jax.ShapeDtypeStruct((2 * rows, columns), F32),
            jax.ShapeDtypeStruct((2 * rows, 1), F32),
            jax.ShapeDtypeStruct((2 * rows, columns), BF16),
            jax.ShapeDtypeStruct(img_proj.shape, BF16),
            jax.ShapeDtypeStruct((columns, 2 * rows), BF16),
        ),
        in_specs=[SMEM] + [HBM] * 6,
        out_specs=(VMEM,) * 5,
        scratch_shapes=[
            pltpu.VMEM((2, rows, columns), BF16),
            pltpu.SemaphoreType.DMA((3,)),
        ],
        compiler_params=params(18),
        name="second_units",
    )(place, img_proj, img_emb, img_other, txt_proj, txt_emb, txt_other)


def piece_at(digit, m, height, first=0):
    return pl.ds(pl.multiple_of(first + (digit ^ m) * height, 8), height)


def pick_kernel(at, place, *refs):
    sources, outs, sems = (refs[:2], refs[2:4]), refs[4:6], refs[6]
    for flag in range(2):

        @pl.when(place[at] == flag)
        def _():
            copies = [
                pltpu.make_async_copy(pair[flag], out, sems.at[k])
                for k, (pair, out) in enumerate(zip(sources, outs))
            ]
            for copy in copies:
                copy.start()
            for copy in copies:
                copy.wait()


def pick(place, at, first, second, name):
    return pl.pallas_call(
        functools.partial(pick_kernel, at),
        out_shape=tuple(jax.ShapeDtypeStruct(p[0].shape, p[0].dtype) for p in (first, second)),
        in_specs=[SMEM] + [ANY] * 4,
        out_specs=(ANY, ANY),
        scratch_shapes=[pltpu.SemaphoreType.DMA((2,))],
        compiler_params=params(1),
        name=name,
    )(place, *first, *second)


def pair_term(z, block, scale, bias, diagonal):
    half = dot_t(z, block) * (0.5 * scale) + 0.5 * bias
    coef = 0.5 * jnp.tanh(half) + 0.5
    if diagonal is not None:
        row_at = lax.broadcasted_iota(jnp.int32, coef.shape, 0) + diagonal
        col_at = lax.broadcasted_iota(jnp.int32, coef.shape, 1)
        coef = jnp.where(row_at == col_at, coef - 1.0, coef)
    return dot(coef.astype(BF16), block)


def own_chip_kernel(scale, bias, z, met, met_other, grad):
    step = pl.program_id(0)
    per_block = met.shape[0] // TILE
    here = step * TILE
    near = pair_term(z[...], met[...], scale[0], bias[0], here)
    other = pair_term(z[...], met_other[...], scale[0], bias[0], here - per_block * TILE)
    grad[...] = near + other


def first_phase_kernel(scale, bias, z, one, two, far_own, far_other, grad_in, grad):
    step = pl.program_id(0)
    per_block = one.shape[0] // TILE
    total = grad_in[...] + pair_term(z[...], one[...], scale[0], bias[0], None)
    total = total + pair_term(z[...], two[...], scale[0], bias[0], None)

    @pl.when(step < per_block)
    def _():
        grad[...] = total + pair_term(z[...], far_own[...], scale[0], bias[0], None)

    @pl.when(step >= per_block)
    def _():
        grad[...] = total + pair_term(z[...], far_other[...], scale[0], bias[0], None)


def relayed_kernel(scale, bias, z, block, grad_in, grad):
    grad[...] = grad_in[...] + pair_term(z[...], block[...], scale[0], bias[0], None)


def row_tiles(columns):
    return pl.BlockSpec((TILE, columns), lambda i: (i, 0))


def whole(array):
    return pl.BlockSpec(
        array.shape, lambda i: (0,) * len(array.shape), pipeline_mode=pl.Buffered(1)
    )


def call_tiles(kernel, scale, bias, z, blocks, grads, name, mib):
    rows, columns = z.shape
    return pl.pallas_call(
        kernel,
        grid=(rows // TILE,),
        out_shape=jax.ShapeDtypeStruct((rows, columns), F32),
        in_specs=[SMEM, SMEM, row_tiles(columns)]
        + [whole(b) for b in blocks]
        + [row_tiles(columns)] * len(grads),
        out_specs=row_tiles(columns),
        compiler_params=params(mib),
        name=name,
    )(scale, bias, z, *blocks, *grads)


def last_phase_kernel(
    place, scale, bias, z, block, grad_in, unit, inverse, emb_t, du, *rest
):
    half, (du_all, emb_v, sem) = rest[0], rest[1:]
    step = pl.program_id(0)
    fetch = pltpu.make_async_copy(emb_t, emb_v, sem)

    @pl.when(step == 0)
    def _():
        fetch.start()

    grad = grad_in[...] + pair_term(z[...], block[...], scale[0], bias[0], None)
    grad = scale[0] * grad
    units = unit[...]
    inner = jnp.sum(units * grad, axis=1, keepdims=True)
    rounded = ((grad - units * inner) * inverse[...]).astype(BF16)
    du[...] = rounded
    du_all[pl.ds(pl.multiple_of(step * TILE, TILE), TILE), :] = rounded

    @pl.when(step == pl.num_programs(0) - 1)
    def _():
        fetch.wait()
        height = half.shape[0]
        first = emb_v.shape[0] - 2 * height
        rows = piece_at(place[Z_LOW], 1, height, first)
        half[...] = dot(emb_v[rows, :], du_all[...]).astype(BF16)


def last_phase(place, scale, bias, z, block, grad, unit, inverse, emb_t):
    rows, columns = z.shape
    half = jax.ShapeDtypeStruct((columns // 6, columns), BF16)
    return pl.pallas_call(
        last_phase_kernel,
        grid=(rows // TILE,),
        out_shape=(jax.ShapeDtypeStruct((rows, columns), BF16), half),
        in_specs=[
            SMEM,
            SMEM,
            SMEM,
            row_tiles(columns),
            whole(block),
            row_tiles(columns),
            row_tiles(columns),
            row_tiles(1),
            HBM,
        ],
        out_specs=(row_tiles(columns), whole(half)),
        scratch_shapes=[
            pltpu.VMEM((rows, columns), BF16),
            pltpu.VMEM(emb_t.shape, BF16),
            pltpu.SemaphoreType.DMA,
        ],
        compiler_params=params(28),
        name="last_phase",
    )(place, scale, bias, z, block, grad, unit, inverse, emb_t)


def sent_parts_kernel(place, emb_t, du, *pieces):
    for m, out in enumerate(pieces):
        rows = piece_at(place[IN_PLANE], m + 1, out.shape[0])
        out[...] = dot(emb_t[rows, :], du[...]).astype(out.dtype)


def kept_parts_kernel(place, emb_t, du, keep_a, keep_b):
    height = keep_b.shape[0]
    at_b = emb_t.shape[0] - 2 * height
    for out, rows in (
        (keep_a, piece_at(place[IN_PLANE], 0, height)),
        (keep_b, piece_at(place[Z_LOW], 0, height, at_b)),
    ):
        out[...] = dot(emb_t[rows, :], du[...])


def parts(kernel, place, emb_t, du, kinds, name):
    shape = (emb_t.shape[0] // 6, emb_t.shape[0])
    return pl.pallas_call(
        kernel,
        out_shape=tuple(jax.ShapeDtypeStruct(shape, kind) for kind in kinds),
        in_specs=[SMEM] + [VMEM] * 2,
        out_specs=(VMEM,) * len(kinds),
        compiler_params=params(6),
        name=name,
    )(place, emb_t, du)


def rows_back_kernel(place, du, weight, own, other):
    back = dot_t(du[...], weight[...]).astype(BF16)
    mine = pl.program_id(0) == 1 - place[SAME]

    @pl.when(mine)
    def _():
        own[...] = back

    @pl.when(jnp.logical_not(mine))
    def _():
        other[...] = back


def rows_back(place, du, weight):
    rows, columns = du.shape
    out = jax.ShapeDtypeStruct((TILE, columns), BF16)
    return pl.pallas_call(
        rows_back_kernel,
        grid=(rows // TILE,),
        out_shape=(out, out),
        in_specs=[SMEM, row_tiles(columns), whole(weight)],
        out_specs=(whole(out), whole(out)),
        compiler_params=params(8),
        name="rows_back",
    )(place, du, weight)


def summed(refs):
    one, two, three, four = (ref[...].astype(F32) for ref in refs)
    return (one + two) + (three + four)


def small_call(kernel, place, arrays, outs, scratch, mib, name):
    return pl.pallas_call(
        kernel,
        out_shape=tuple(jax.ShapeDtypeStruct(shape, kind) for shape, kind in outs),
        in_specs=[SMEM] + [VMEM] * len(arrays),
        out_specs=(VMEM,) * len(outs),
        scratch_shapes=[pltpu.VMEM(shape, F32) for shape in scratch],
        compiler_params=params(mib),
        name=name,
    )(place, *arrays)


def cut(place, bit, total, mine, give, first=0):
    for m, out in enumerate((mine, give)):
        out[...] = total[piece_at(place[bit], m, out.shape[0], first), :].astype(out.dtype)


def middle_one_kernel(place, *refs):
    parts, (keep, got), outs, (total, total_b) = refs[:4], refs[4:6], refs[6:12], refs[12:]
    total[...] = summed(parts)
    total_b[...] = keep[...] + got[...].astype(F32)
    cut(place, Z_LOW, total, outs[0], outs[1])
    cut(place, Z_HIGH, total, outs[2], outs[3], total.shape[0] // 2)
    cut(place, X, total_b, outs[4], outs[5])


def middle_one(place, parts, keep, got, name):
    rows, columns = parts[0].shape
    shape = (rows // 4, columns)
    outs = [(shape, F32), (shape, BF16)] * 3
    scratch = [(rows, columns), keep.shape]
    return small_call(middle_one_kernel, place, [*parts, keep, got], outs, scratch, 5, name)


def middle_two_kernel(place, *refs):
    for k in range(3):
        refs[6 + k][...] = (refs[2 * k][...] + refs[2 * k + 1][...].astype(F32)).astype(BF16)


def middle_two(place, arrays, name):
    outs = [(array.shape, BF16) for array in arrays[::2]]
    return small_call(middle_two_kernel, place, arrays, outs, [], 3, name)


def middle_three_kernel(place, *refs):
    for k in range(3):
        refs[6 + k][...] = (refs[2 * k][...].astype(F32) + refs[2 * k + 1][...].astype(F32)).astype(BF16)


def middle_three(place, arrays, name):
    outs = [(array.shape, BF16) for array in arrays[::2]]
    return small_call(middle_three_kernel, place, arrays, outs, [], 2, name)


def middle_four_kernel(place, *refs):
    (high, got_high, low, got_low), (mine, got) = refs[:4], refs[4:6]
    out, out_b, total, total_b = refs[6:]
    height = low.shape[0]
    for m, piece in enumerate((low, got_low)):
        total[piece_at(place[Z_LOW], m, height), :] = piece[...].astype(F32)
    for m, piece in enumerate((high, got_high)):
        total[piece_at(place[Z_HIGH], m, height, 2 * height), :] = piece[...].astype(F32)
    out[...] = total[...].astype(BF16)
    for m, piece in enumerate((mine, got)):
        total_b[piece_at(place[X], m, mine.shape[0]), :] = piece[...].astype(F32)
    out_b[...] = total_b[...].astype(BF16)


def middle_four(place, arrays, pair, name):
    shapes = [(len(a) * a[0].shape[0], a[0].shape[1]) for a in (arrays, pair)]
    outs = [(shape, BF16) for shape in shapes]
    return small_call(middle_four_kernel, place, [*arrays, *pair], outs, shapes, 5, name)


def add_halve_kernel(bit, place, keep, got, mine, give, total):
    total[...] = keep[...] + got[...].astype(F32)
    for m, out in enumerate((mine, give)):
        out[...] = total[piece_at(place[bit], m, out.shape[0]), :].astype(out.dtype)


def add_halve(place, bit, keep, got, name):
    rows, columns = keep.shape
    outs = [((rows // 2, columns), kind) for kind in (F32, BF16)]
    kernel = functools.partial(add_halve_kernel, bit)
    return small_call(kernel, place, [keep, got], outs, [keep.shape], 3, name)


def join_two_kernel(bit, place, mine, got, out, total):
    for m, piece in enumerate((mine, got)):
        total[piece_at(place[bit], m, piece.shape[0]), :] = piece[...].astype(F32)
    out[...] = total[...].astype(BF16)


def join_two(place, bit, mine, got, name):
    shape = (2 * mine.shape[0], mine.shape[1])
    kernel = functools.partial(join_two_kernel, bit)
    return small_call(kernel, place, [mine, got], [(shape, BF16)], [shape], 5, name)[0]


def join_all_kernel(place, *refs):
    out = refs[6]
    for m, piece in enumerate(refs[:4]):
        out[piece_at(place[IN_PLANE], m, piece.shape[0]), :] = piece[...]
    height = refs[4].shape[0]
    for m, piece in enumerate(refs[4:6]):
        out[piece_at(place[Z_LOW], m, height, out.shape[0] - 2 * height), :] = piece[...]


def join_all(place, parts_a, parts_b):
    columns = parts_b[0].shape[1]
    arrays = [*parts_a, *parts_b]
    outs = [((columns, columns), BF16)]
    return small_call(join_all_kernel, place, arrays, outs, [], 3, "join_all")[0]


def widen_kernel(own, place, weight, *refs):
    img_out, txt_out, wide, sems = refs[-4:]
    count = sems.shape[0]
    height = weight.shape[0] // count
    for side, out in enumerate((img_out, txt_out)):

        @pl.when((place[SIDE] == side) == own)
        def _():
            copies = []
            for k in range(count):
                part = slice(k * height, (k + 1) * height)
                wide[part, :] = weight[part, :].astype(F32)
                copies.append(
                    pltpu.make_async_copy(wide.at[part, :], out.at[part, :], sems.at[k])
                )
                copies[-1].start()
            for copy in copies:
                copy.wait()


def widen(place, weight, own, outs, name):
    out = jax.ShapeDtypeStruct(weight.shape, F32)
    return pl.pallas_call(
        functools.partial(widen_kernel, own),
        out_shape=(out, out),
        in_specs=[SMEM, VMEM] + [ANY] * len(outs),
        out_specs=(ANY, ANY),
        scratch_shapes=[pltpu.VMEM(weight.shape, F32), pltpu.SemaphoreType.DMA((9,))],
        input_output_aliases={2: 0, 3: 1} if outs else {},
        compiler_params=params(9),
        name=name,
    )(place, weight, *outs)


def body(img_emb, txt_emb, img_proj, txt_proj, log_scale, bias):
    size = lax.axis_size("dp")
    columns = img_emb.shape[1]
    scale = jnp.exp(log_scale)
    here = lax.axis_index("dp").astype(jnp.int32)
    side, chip = here % 2, here // 2
    bits = [(chip // n) % 2 for n in (1, 2, 4, 8)]
    place = jnp.stack([side, chip % 4, (chip // 4) % 4, (chip + side + 1) % 2, *bits])
    place, scale = lax.optimization_barrier((place, scale))

    pair = lambda value: swap(value, size, 2)
    far_as_d = lambda value: shift(value, size, lambda chip, core: -2 if chip % 2 else 2)

    def raw_target(to_far, to_pair):
        pairs = []
        for i in range(size):
            chip, core = i // 2, i % 2
            if core == chip % 2:
                pairs.append((i, 2 * ((chip + 2 if core else chip - 2) % (size // 2)) + to_far))
            else:
                pairs.append((i, 2 * (chip ^ 1) + to_pair))
        return pairs

    same = (chip + side) % 2 == 0
    raw_one = jnp.where(same, txt_emb, img_emb)
    raw_two = jnp.where(same, img_emb, txt_emb)
    got_one = lax.ppermute(raw_one, "dp", raw_target(0, 1))
    got_two = lax.ppermute(raw_two, "dp", raw_target(1, 0))
    img_other, txt_other, _ = lax.optimization_barrier(
        (swap(img_emb, size, 1), swap(txt_emb, size, 1), raw_one)
    )
    met_s, met_d = met_units(
        place,
        (txt_emb, txt_other),
        (img_emb, img_other),
        img_proj,
        txt_proj,
        True,
        30,
        "own_met",
    )
    img_emb, txt_emb, img_other, txt_other, _ = lax.optimization_barrier(
        (img_emb, txt_emb, img_other, txt_other, met_s)
    )
    unit, inverse, z, weight, emb_t = second_units(
        place, img_emb, txt_emb, img_other, txt_other, img_proj, txt_proj
    )
    got_one, got_two, sent_s, sent_d, _ = lax.optimization_barrier(
        (got_one, got_two, met_s, met_d, emb_t)
    )
    pair_s, far_d = pair(sent_s), far_as_d(sent_d)
    pair_d, far_s = met_units(
        place,
        (got_two, got_one),
        (got_one, got_two),
        img_proj,
        txt_proj,
        False,
        14,
        "raw_met",
    )
    relay_far, relay_pair = pair(far_s), far_as_d(pair_d)
    z, _ = lax.optimization_barrier((z, (pair_d, far_s)))
    grad = call_tiles(own_chip_kernel, scale, bias, z, (met_s, met_d), (), "own_chip", 8)
    pair_s, far_d, _ = lax.optimization_barrier((pair_s, far_d, grad))
    grad = call_tiles(
        first_phase_kernel,
        scale,
        bias,
        z,
        (pair_s, pair_d, far_d, far_s),
        (grad,),
        "first_phase",
        12,
    )

    grad = call_tiles(relayed_kernel, scale, bias, z, (relay_far,), (grad,), "relayed", 10)
    du, give_b = last_phase(
        place, scale, bias, z, relay_pair, grad, unit, inverse, emb_t
    )

    def exchange(sends, masks):
        return [swap(s, size, m) for s, m in zip(sends, masks)]

    plane_masks, line_masks = (2, 4, 6), (8, 16, 24)
    x_bit, y_bit, low_bit, high_bit = (X, 2), (Y, 4), (Z_LOW, 8), (Z_HIGH, 16)

    def halve(keep, got, bit, name):
        keep, give = add_halve(place, bit[0], keep, got, name)
        return keep, swap(give, size, bit[1]), give

    def gather(mine, bit):
        return mine, swap(mine, size, bit[1])

    together = lax.optimization_barrier
    got_b = swap(give_b, size, low_bit[1])
    sends = parts(sent_parts_kernel, place, emb_t, du, (BF16,) * 3, "sent_parts")
    got_a = exchange(sends, plane_masks)
    keep_a, keep_b = parts(kept_parts_kernel, place, emb_t, du, (F32, F32), "kept_parts")
    parts_a = [keep_a, *got_a]
    keep_b, got_b, give_b = halve(keep_b, got_b, high_bit, "b_high")
    du, _ = together((du, give_b))
    d_emb, d_emb_send = rows_back(place, du, weight)
    parts_a, got_b, d_emb_send = together((parts_a, got_b, d_emb_send))
    d_emb_other = swap(d_emb_send, size, 1)

    near, far = low_bit[1], high_bit[1]
    keep_low, give_low, keep_high, give_high, keep_b, give_b = middle_one(
        place, parts_a, keep_b, got_b, "middle_one"
    )
    got_low, got_high = swap(give_low, size, near), swap(give_high, size, far)
    got_b = swap(give_b, size, x_bit[1])
    got_low, got_high, got_b = together((got_low, got_high, got_b))
    high, low, shard_b = middle_two(
        place, (keep_high, got_high, keep_low, got_low, keep_b, got_b), "middle_two"
    )
    got_low, got_high = swap(low, size, far), swap(high, size, near)
    got_b = swap(shard_b, size, y_bit[1])
    d_img_emb, d_txt_emb = pick(
        place, SIDE, (d_emb, d_emb_other), (d_emb_other, d_emb), "rows_pick"
    )
    got_low, got_high, got_b, d_img_emb, d_txt_emb = together(
        (got_low, got_high, got_b, d_img_emb, d_txt_emb)
    )
    low, high, shard_b = middle_three(
        place, (low, got_low, high, got_high, shard_b, got_b), "middle_three"
    )
    if size > 32:
        groups = [[i for i in range(size) if i % 32 == k] for k in range(32)]
        low, high, shard_b = lax.psum((low, high, shard_b), "dp", axis_index_groups=groups)
    got_high, got_low = swap(high, size, far), swap(low, size, near)
    got_b = swap(shard_b, size, x_bit[1])
    piece_a, shard_b = middle_four(
        place, (high, got_high, low, got_low), (shard_b, got_b), "middle_four"
    )
    got_b = swap(shard_b, size, high_bit[1])
    parts_a = [piece_a, *exchange([piece_a] * 3, plane_masks)]
    shard_b = join_two(place, high_bit[0], shard_b, got_b, "b_join_high")
    got_b = swap(shard_b, size, low_bit[1])
    parts_a, got_b = together((parts_a, got_b))

    d_weight = join_all(place, parts_a, (shard_b, got_b))
    d_weight_other = swap(d_weight, size, 1)
    outs = widen(place, d_weight, True, (), "widen_own")
    d_img_proj, d_txt_proj = widen(place, d_weight_other, False, outs, "widen_other")
    return (d_img_emb, d_txt_emb, d_img_proj, d_txt_proj)


def solution(mesh):
    return jax.shard_map(
        body,
        mesh=mesh,
        in_specs=(P("dp", None), P("dp", None), P(), P(), P(), P()),
        out_specs=(P("dp", None), P("dp", None), P(), P()),
        check_vma=False,
    )
```

```python
import functools

import jax
import jax.numpy as jnp
from jax import lax
from jax.experimental import pallas as pl
from jax.experimental.pallas import tpu as pltpu
from jax.sharding import PartitionSpec as P

REACH = 3
BF16, F32 = jnp.bfloat16, jnp.float32
TILE = 512
SIDE, IN_PLANE, IN_LINE, SAME, X, Y, Z_LOW, Z_HIGH = range(8)
VMEM = pl.BlockSpec(memory_space=pltpu.VMEM)
SMEM = pl.BlockSpec(memory_space=pltpu.SMEM)
HBM = pl.BlockSpec(memory_space=pltpu.HBM)
ANY = pl.BlockSpec(memory_space=pl.ANY)


def params(mib):
    return pltpu.CompilerParams(vmem_limit_bytes=mib * 1024 * 1024)


def dot_t(left, right):
    return lax.dot_general(left, right, (((1,), (1,)), ((), ())), preferred_element_type=F32)


def dot(left, right):
    return lax.dot_general(left, right, (((1,), (0,)), ((), ())), preferred_element_type=F32)


def shift(value, size, chips):
    pairs = []
    for i in range(size):
        chip, core = i // 2, i % 2
        pairs.append((i, 2 * ((chip + chips(chip, core)) % (size // 2)) + core))
    return lax.ppermute(value, "dp", pairs)


def swap(value, size, mask):
    return lax.ppermute(value, "dp", [(i, i ^ mask) for i in range(size)])


def met_kernel(own_chip, place, *refs):
    sides, projs, (z_one, z_two, emb_v, proj_v, sems) = (refs[:2], refs[2:4]), refs[4:6], refs[6:]
    cut = proj_v.shape[0] // 256 * 128 + 128
    parts = [slice(0, cut), slice(cut, proj_v.shape[0])]
    for side, (embs, proj) in enumerate(zip(sides, projs)):

        @pl.when(place[SIDE] == side)
        def _():
            first = 1 - place[SAME] if own_chip else 0
            copies = [pltpu.make_async_copy(embs[0], emb_v.at[first], sems.at[2])]
            for k, part in enumerate(parts):
                copies.append(
                    pltpu.make_async_copy(proj.at[part, :], proj_v.at[part, :], sems.at[k])
                )
            copies.append(pltpu.make_async_copy(embs[1], emb_v.at[1 - first], sems.at[3]))
            for copy in copies:
                copy.start()
            for copy in copies:
                copy.wait()

    for k, z in enumerate((z_one, z_two)):
        raw = dot(emb_v[k], proj_v[...])
        scale = lax.rsqrt(jnp.sum(raw * raw, axis=1, keepdims=True) + 1e-06)
        z[...] = (raw * scale).astype(BF16)


def met_units(place, text_side, image_side, img_proj, txt_proj, own_chip, mib, name):
    out = jax.ShapeDtypeStruct(text_side[0].shape, BF16)
    return pl.pallas_call(
        functools.partial(met_kernel, own_chip),
        out_shape=(out, out),
        in_specs=[SMEM] + [HBM] * 6,
        out_specs=(VMEM, VMEM),
        scratch_shapes=[
            pltpu.VMEM((2, *out.shape), BF16),
            pltpu.VMEM(img_proj.shape, BF16),
            pltpu.SemaphoreType.DMA((4,)),
        ],
        compiler_params=params(mib),
        name=name,
    )(place, *text_side, *image_side, txt_proj, img_proj)


def second_kernel(place, *refs):
    sides, (unit, inverse, z, weight, emb_t, emb_v, sems) = (refs[:3], refs[3:6]), refs[6:]
    rows = emb_v.shape[1]
    for side in range(2):

        @pl.when(place[SIDE] == side)
        def _():
            copies = [
                pltpu.make_async_copy(src, dst, sems.at[at])
                for at, (src, dst) in enumerate(
                    zip(sides[side], (weight, emb_v.at[1 - place[SAME]], emb_v.at[place[SAME]]))
                )
            ]
            for copy in copies:
                copy.start()
            for copy in copies:
                copy.wait()

    for half in range(2):
        here = slice(half * rows, (half + 1) * rows)
        raw = dot(emb_v[half], weight[...])
        scale = lax.rsqrt(jnp.sum(raw * raw, axis=1, keepdims=True) + 1e-06)
        inverse[here, :] = scale
        units = raw * scale
        unit[here, :] = units
        z[here, :] = units.astype(BF16)
        emb_t[:, here] = emb_v[half].T


def second_units(place, img_emb, txt_emb, img_other, txt_other, img_proj, txt_proj):
    rows, columns = img_emb.shape
    return pl.pallas_call(
        second_kernel,
        out_shape=(
            jax.ShapeDtypeStruct((2 * rows, columns), F32),
            jax.ShapeDtypeStruct((2 * rows, 1), F32),
            jax.ShapeDtypeStruct((2 * rows, columns), BF16),
            jax.ShapeDtypeStruct(img_proj.shape, BF16),
            jax.ShapeDtypeStruct((columns, 2 * rows), BF16),
        ),
        in_specs=[SMEM] + [HBM] * 6,
        out_specs=(VMEM,) * 5,
        scratch_shapes=[
            pltpu.VMEM((2, rows, columns), BF16),
            pltpu.SemaphoreType.DMA((3,)),
        ],
        compiler_params=params(18),
        name="second_units",
    )(place, img_proj, img_emb, img_other, txt_proj, txt_emb, txt_other)


def piece_at(digit, m, height, first=0):
    return pl.ds(pl.multiple_of(first + (digit ^ m) * height, 8), height)


def pick_kernel(at, place, *refs):
    sources, outs, sems = (refs[:2], refs[2:4]), refs[4:6], refs[6]
    for flag in range(2):

        @pl.when(place[at] == flag)
        def _():
            copies = [
                pltpu.make_async_copy(pair[flag], out, sems.at[k])
                for k, (pair, out) in enumerate(zip(sources, outs))
            ]
            for copy in copies:
                copy.start()
            for copy in copies:
                copy.wait()


def pick(place, at, first, second, name):
    return pl.pallas_call(
        functools.partial(pick_kernel, at),
        out_shape=tuple(jax.ShapeDtypeStruct(p[0].shape, p[0].dtype) for p in (first, second)),
        in_specs=[SMEM] + [ANY] * 4,
        out_specs=(ANY, ANY),
        scratch_shapes=[pltpu.SemaphoreType.DMA((2,))],
        compiler_params=params(1),
        name=name,
    )(place, *first, *second)


def pair_term(z, block, scale, bias, diagonal):
    half = dot_t(z, block) * (0.5 * scale) + 0.5 * bias
    coef = 0.5 * jnp.tanh(half) + 0.5
    if diagonal is not None:
        row_at = lax.broadcasted_iota(jnp.int32, coef.shape, 0) + diagonal
        col_at = lax.broadcasted_iota(jnp.int32, coef.shape, 1)
        coef = jnp.where(row_at == col_at, coef - 1.0, coef)
    return dot(coef.astype(BF16), block)


def own_chip_kernel(scale, bias, z, met, met_other, grad):
    step = pl.program_id(0)
    per_block = met.shape[0] // TILE
    here = step * TILE
    near = pair_term(z[...], met[...], scale[0], bias[0], here)
    other = pair_term(z[...], met_other[...], scale[0], bias[0], here - per_block * TILE)
    grad[...] = near + other


def first_phase_kernel(scale, bias, z, one, two, far_own, far_other, grad_in, grad):
    step = pl.program_id(0)
    per_block = one.shape[0] // TILE
    total = grad_in[...] + pair_term(z[...], one[...], scale[0], bias[0], None)
    total = total + pair_term(z[...], two[...], scale[0], bias[0], None)

    @pl.when(step < per_block)
    def _():
        grad[...] = total + pair_term(z[...], far_own[...], scale[0], bias[0], None)

    @pl.when(step >= per_block)
    def _():
        grad[...] = total + pair_term(z[...], far_other[...], scale[0], bias[0], None)


def relayed_kernel(scale, bias, z, block, grad_in, grad):
    grad[...] = grad_in[...] + pair_term(z[...], block[...], scale[0], bias[0], None)


def row_tiles(columns):
    return pl.BlockSpec((TILE, columns), lambda i: (i, 0))


def whole(array):
    return pl.BlockSpec(
        array.shape, lambda i: (0,) * len(array.shape), pipeline_mode=pl.Buffered(1)
    )


def call_tiles(kernel, scale, bias, z, blocks, grads, name, mib):
    rows, columns = z.shape
    return pl.pallas_call(
        kernel,
        grid=(rows // TILE,),
        out_shape=jax.ShapeDtypeStruct((rows, columns), F32),
        in_specs=[SMEM, SMEM, row_tiles(columns)]
        + [whole(b) for b in blocks]
        + [row_tiles(columns)] * len(grads),
        out_specs=row_tiles(columns),
        compiler_params=params(mib),
        name=name,
    )(scale, bias, z, *blocks, *grads)


def last_phase_kernel(
    place, scale, bias, z, block, grad_in, unit, inverse, emb_t, du, *rest
):
    half, (du_all, emb_v, sem) = rest[0], rest[1:]
    step = pl.program_id(0)
    fetch = pltpu.make_async_copy(emb_t, emb_v, sem)

    @pl.when(step == 0)
    def _():
        fetch.start()

    grad = grad_in[...] + pair_term(z[...], block[...], scale[0], bias[0], None)
    grad = scale[0] * grad
    units = unit[...]
    inner = jnp.sum(units * grad, axis=1, keepdims=True)
    rounded = ((grad - units * inner) * inverse[...]).astype(BF16)
    du[...] = rounded
    du_all[pl.ds(pl.multiple_of(step * TILE, TILE), TILE), :] = rounded

    @pl.when(step == pl.num_programs(0) - 1)
    def _():
        fetch.wait()
        height = half.shape[0]
        first = emb_v.shape[0] - 2 * height
        rows = piece_at(place[Z_LOW], 1, height, first)
        half[...] = dot(emb_v[rows, :], du_all[...]).astype(BF16)


def last_phase(place, scale, bias, z, block, grad, unit, inverse, emb_t):
    rows, columns = z.shape
    half = jax.ShapeDtypeStruct((columns // 6, columns), BF16)
    return pl.pallas_call(
        last_phase_kernel,
        grid=(rows // TILE,),
        out_shape=(jax.ShapeDtypeStruct((rows, columns), BF16), half),
        in_specs=[
            SMEM,
            SMEM,
            SMEM,
            row_tiles(columns),
            whole(block),
            row_tiles(columns),
            row_tiles(columns),
            row_tiles(1),
            HBM,
        ],
        out_specs=(row_tiles(columns), whole(half)),
        scratch_shapes=[
            pltpu.VMEM((rows, columns), BF16),
            pltpu.VMEM(emb_t.shape, BF16),
            pltpu.SemaphoreType.DMA,
        ],
        compiler_params=params(28),
        name="last_phase",
    )(place, scale, bias, z, block, grad, unit, inverse, emb_t)


def sent_parts_kernel(place, emb_t, du, *pieces):
    for m, out in enumerate(pieces):
        rows = piece_at(place[IN_PLANE], m + 1, out.shape[0])
        out[...] = dot(emb_t[rows, :], du[...]).astype(out.dtype)


def kept_parts_kernel(place, emb_t, du, keep_a, keep_b):
    height = keep_b.shape[0]
    at_b = emb_t.shape[0] - 2 * height
    for out, rows in (
        (keep_a, piece_at(place[IN_PLANE], 0, height)),
        (keep_b, piece_at(place[Z_LOW], 0, height, at_b)),
    ):
        out[...] = dot(emb_t[rows, :], du[...])


def parts(kernel, place, emb_t, du, kinds, name):
    shape = (emb_t.shape[0] // 6, emb_t.shape[0])
    return pl.pallas_call(
        kernel,
        out_shape=tuple(jax.ShapeDtypeStruct(shape, kind) for kind in kinds),
        in_specs=[SMEM] + [VMEM] * 2,
        out_specs=(VMEM,) * len(kinds),
        compiler_params=params(6),
        name=name,
    )(place, emb_t, du)


def rows_back_kernel(place, du, weight, own, other):
    back = dot_t(du[...], weight[...]).astype(BF16)
    mine = pl.program_id(0) == 1 - place[SAME]

    @pl.when(mine)
    def _():
        own[...] = back

    @pl.when(jnp.logical_not(mine))
    def _():
        other[...] = back


def rows_back(place, du, weight):
    rows, columns = du.shape
    out = jax.ShapeDtypeStruct((TILE, columns), BF16)
    return pl.pallas_call(
        rows_back_kernel,
        grid=(rows // TILE,),
        out_shape=(out, out),
        in_specs=[SMEM, row_tiles(columns), whole(weight)],
        out_specs=(whole(out), whole(out)),
        compiler_params=params(8),
        name="rows_back",
    )(place, du, weight)


def summed(refs):
    one, two, three, four = (ref[...].astype(F32) for ref in refs)
    return (one + two) + (three + four)


def small_call(kernel, place, arrays, outs, scratch, mib, name):
    return pl.pallas_call(
        kernel,
        out_shape=tuple(jax.ShapeDtypeStruct(shape, kind) for shape, kind in outs),
        in_specs=[SMEM] + [VMEM] * len(arrays),
        out_specs=(VMEM,) * len(outs),
        scratch_shapes=[pltpu.VMEM(shape, F32) for shape in scratch],
        compiler_params=params(mib),
        name=name,
    )(place, *arrays)


def cut(place, bit, total, mine, give, first=0):
    for m, out in enumerate((mine, give)):
        out[...] = total[piece_at(place[bit], m, out.shape[0], first), :].astype(out.dtype)


def middle_one_kernel(place, *refs):
    parts, (keep, got), outs, (total, total_b) = refs[:4], refs[4:6], refs[6:12], refs[12:]
    total[...] = summed(parts)
    total_b[...] = keep[...] + got[...].astype(F32)
    cut(place, Z_LOW, total, outs[0], outs[1])
    cut(place, Z_HIGH, total, outs[2], outs[3], total.shape[0] // 2)
    cut(place, X, total_b, outs[4], outs[5])


def middle_one(place, parts, keep, got, name):
    rows, columns = parts[0].shape
    shape = (rows // 4, columns)
    outs = [(shape, F32), (shape, BF16)] * 3
    scratch = [(rows, columns), keep.shape]
    return small_call(middle_one_kernel, place, [*parts, keep, got], outs, scratch, 5, name)


def middle_two_kernel(place, *refs):
    for k in range(3):
        refs[6 + k][...] = (refs[2 * k][...] + refs[2 * k + 1][...].astype(F32)).astype(BF16)


def middle_two(place, arrays, name):
    outs = [(array.shape, BF16) for array in arrays[::2]]
    return small_call(middle_two_kernel, place, arrays, outs, [], 3, name)


def middle_three_kernel(place, *refs):
    for k in range(3):
        refs[6 + k][...] = (refs[2 * k][...].astype(F32) + refs[2 * k + 1][...].astype(F32)).astype(BF16)


def middle_three(place, arrays, name):
    outs = [(array.shape, BF16) for array in arrays[::2]]
    return small_call(middle_three_kernel, place, arrays, outs, [], 2, name)


def middle_four_kernel(place, *refs):
    (high, got_high, low, got_low), (mine, got) = refs[:4], refs[4:6]
    out, out_b, total, total_b = refs[6:]
    height = low.shape[0]
    for m, piece in enumerate((low, got_low)):
        total[piece_at(place[Z_LOW], m, height), :] = piece[...].astype(F32)
    for m, piece in enumerate((high, got_high)):
        total[piece_at(place[Z_HIGH], m, height, 2 * height), :] = piece[...].astype(F32)
    out[...] = total[...].astype(BF16)
    for m, piece in enumerate((mine, got)):
        total_b[piece_at(place[X], m, mine.shape[0]), :] = piece[...].astype(F32)
    out_b[...] = total_b[...].astype(BF16)


def middle_four(place, arrays, pair, name):
    shapes = [(len(a) * a[0].shape[0], a[0].shape[1]) for a in (arrays, pair)]
    outs = [(shape, BF16) for shape in shapes]
    return small_call(middle_four_kernel, place, [*arrays, *pair], outs, shapes, 5, name)


def add_halve_kernel(bit, place, keep, got, mine, give, total):
    total[...] = keep[...] + got[...].astype(F32)
    for m, out in enumerate((mine, give)):
        out[...] = total[piece_at(place[bit], m, out.shape[0]), :].astype(out.dtype)


def add_halve(place, bit, keep, got, name):
    rows, columns = keep.shape
    outs = [((rows // 2, columns), kind) for kind in (F32, BF16)]
    kernel = functools.partial(add_halve_kernel, bit)
    return small_call(kernel, place, [keep, got], outs, [keep.shape], 3, name)


def join_two_kernel(bit, place, mine, got, out, total):
    for m, piece in enumerate((mine, got)):
        total[piece_at(place[bit], m, piece.shape[0]), :] = piece[...].astype(F32)
    out[...] = total[...].astype(BF16)


def join_two(place, bit, mine, got, name):
    shape = (2 * mine.shape[0], mine.shape[1])
    kernel = functools.partial(join_two_kernel, bit)
    return small_call(kernel, place, [mine, got], [(shape, BF16)], [shape], 5, name)[0]


def stack_rows_kernel(place, *refs):
    out, first = refs[-1], 0
    for ref in refs[:-1]:
        out[first : first + ref.shape[0], :] = ref[...]
        first += ref.shape[0]


def stack_rows(place, arrays, name):
    shape = (sum(a.shape[0] for a in arrays), arrays[0].shape[1])
    return small_call(stack_rows_kernel, place, arrays, [(shape, BF16)], [], 3, name)[0]


def widen_kernel(own, places, count, place, *refs):
    arrays, (img_out, txt_out, wide, sems) = refs[:count], refs[-4:]
    height = wide.shape[0] // len(places)
    sources = [a.at[pl.ds(first, height), :] for a in arrays for first in range(0, a.shape[0], height)]
    for side, out in enumerate((img_out, txt_out)):

        @pl.when((place[SIDE] == side) == own)
        def _():
            copies = []
            for k, (source, (digit, m, first)) in enumerate(zip(sources, places)):
                part = slice(k * height, (k + 1) * height)
                goal = piece_at(place[digit], m, height, first)
                wide[part, :] = source[...].astype(F32)
                copies.append(
                    pltpu.make_async_copy(wide.at[part, :], out.at[goal, :], sems.at[k])
                )
                copies[-1].start()
            for copy in copies:
                copy.wait()


def widen(place, arrays, places, own, outs, name):
    columns = arrays[0].shape[1]
    out = jax.ShapeDtypeStruct((columns, columns), F32)
    count = len(arrays)
    return pl.pallas_call(
        functools.partial(widen_kernel, own, places, count),
        out_shape=(out, out),
        in_specs=[SMEM] + [VMEM] * count + [ANY] * len(outs),
        out_specs=(ANY, ANY),
        scratch_shapes=[
            pltpu.VMEM((columns, columns), F32),
            pltpu.SemaphoreType.DMA((len(places),)),
        ],
        input_output_aliases={1 + count: 0, 2 + count: 1} if outs else {},
        compiler_params=params(9),
        name=name,
    )(place, *arrays, *outs)


def body(img_emb, txt_emb, img_proj, txt_proj, log_scale, bias):
    size = lax.axis_size("dp")
    columns = img_emb.shape[1]
    scale = jnp.exp(log_scale)
    here = lax.axis_index("dp").astype(jnp.int32)
    side, chip = here % 2, here // 2
    bits = [(chip // n) % 2 for n in (1, 2, 4, 8)]
    place = jnp.stack([side, chip % 4, (chip // 4) % 4, (chip + side + 1) % 2, *bits])
    place, scale = lax.optimization_barrier((place, scale))

    pair = lambda value: swap(value, size, 2)
    far_as_d = lambda value: shift(value, size, lambda chip, core: -2 if chip % 2 else 2)

    def raw_target(to_far, to_pair):
        pairs = []
        for i in range(size):
            chip, core = i // 2, i % 2
            if core == chip % 2:
                pairs.append((i, 2 * ((chip + 2 if core else chip - 2) % (size // 2)) + to_far))
            else:
                pairs.append((i, 2 * (chip ^ 1) + to_pair))
        return pairs

    same = (chip + side) % 2 == 0
    raw_one = jnp.where(same, txt_emb, img_emb)
    raw_two = jnp.where(same, img_emb, txt_emb)
    got_one = lax.ppermute(raw_one, "dp", raw_target(0, 1))
    got_two = lax.ppermute(raw_two, "dp", raw_target(1, 0))
    img_other, txt_other, _ = lax.optimization_barrier(
        (swap(img_emb, size, 1), swap(txt_emb, size, 1), raw_one)
    )
    met_s, met_d = met_units(
        place,
        (txt_emb, txt_other),
        (img_emb, img_other),
        img_proj,
        txt_proj,
        True,
        30,
        "own_met",
    )
    img_emb, txt_emb, img_other, txt_other, _ = lax.optimization_barrier(
        (img_emb, txt_emb, img_other, txt_other, met_s)
    )
    unit, inverse, z, weight, emb_t = second_units(
        place, img_emb, txt_emb, img_other, txt_other, img_proj, txt_proj
    )
    got_one, got_two, sent_s, sent_d, _ = lax.optimization_barrier(
        (got_one, got_two, met_s, met_d, emb_t)
    )
    pair_s, far_d = pair(sent_s), far_as_d(sent_d)
    pair_d, far_s = met_units(
        place,
        (got_two, got_one),
        (got_one, got_two),
        img_proj,
        txt_proj,
        False,
        14,
        "raw_met",
    )
    relay_far, relay_pair = pair(far_s), far_as_d(pair_d)
    z, _ = lax.optimization_barrier((z, (pair_d, far_s)))
    grad = call_tiles(own_chip_kernel, scale, bias, z, (met_s, met_d), (), "own_chip", 8)
    pair_s, far_d, _ = lax.optimization_barrier((pair_s, far_d, grad))
    grad = call_tiles(
        first_phase_kernel,
        scale,
        bias,
        z,
        (pair_s, pair_d, far_d, far_s),
        (grad,),
        "first_phase",
        12,
    )

    grad = call_tiles(relayed_kernel, scale, bias, z, (relay_far,), (grad,), "relayed", 10)
    du, give_b = last_phase(
        place, scale, bias, z, relay_pair, grad, unit, inverse, emb_t
    )

    def exchange(sends, masks):
        return [swap(s, size, m) for s, m in zip(sends, masks)]

    plane_masks, line_masks = (2, 4, 6), (8, 16, 24)
    x_bit, y_bit, low_bit, high_bit = (X, 2), (Y, 4), (Z_LOW, 8), (Z_HIGH, 16)

    def halve(keep, got, bit, name):
        keep, give = add_halve(place, bit[0], keep, got, name)
        return keep, swap(give, size, bit[1]), give

    def gather(mine, bit):
        return mine, swap(mine, size, bit[1])

    together = lax.optimization_barrier
    got_b = swap(give_b, size, low_bit[1])
    sends = parts(sent_parts_kernel, place, emb_t, du, (BF16,) * 3, "sent_parts")
    got_a = exchange(sends, plane_masks)
    keep_a, keep_b = parts(kept_parts_kernel, place, emb_t, du, (F32, F32), "kept_parts")
    parts_a = [keep_a, *got_a]
    keep_b, got_b, give_b = halve(keep_b, got_b, high_bit, "b_high")
    du, _ = together((du, give_b))
    d_emb, d_emb_send = rows_back(place, du, weight)
    parts_a, got_b, d_emb_send = together((parts_a, got_b, d_emb_send))
    d_emb_other = swap(d_emb_send, size, 1)

    near, far = low_bit[1], high_bit[1]
    keep_low, give_low, keep_high, give_high, keep_b, give_b = middle_one(
        place, parts_a, keep_b, got_b, "middle_one"
    )
    got_low, got_high = swap(give_low, size, near), swap(give_high, size, far)
    got_b = swap(give_b, size, x_bit[1])
    got_low, got_high, got_b = together((got_low, got_high, got_b))
    high, low, shard_b = middle_two(
        place, (keep_high, got_high, keep_low, got_low, keep_b, got_b), "middle_two"
    )
    got_low, got_high = swap(low, size, far), swap(high, size, near)
    got_b = swap(shard_b, size, y_bit[1])
    d_img_emb, d_txt_emb = pick(
        place, SIDE, (d_emb, d_emb_other), (d_emb_other, d_emb), "rows_pick"
    )
    got_low, got_high, got_b, d_img_emb, d_txt_emb = together(
        (got_low, got_high, got_b, d_img_emb, d_txt_emb)
    )
    low, high, shard_b = middle_three(
        place, (low, got_low, high, got_high, shard_b, got_b), "middle_three"
    )
    if size > 32:
        groups = [[i for i in range(size) if i % 32 == k] for k in range(32)]
        low, high, shard_b = lax.psum((low, high, shard_b), "dp", axis_index_groups=groups)
    got_high, got_low = swap(high, size, far), swap(low, size, near)
    got_b = swap(shard_b, size, x_bit[1])
    piece_a, shard_b = middle_four(
        place, (high, got_high, low, got_low), (shard_b, got_b), "middle_four"
    )
    got_b = swap(shard_b, size, high_bit[1])
    parts_a = exchange([piece_a] * 3, plane_masks)
    shard_b = join_two(place, high_bit[0], shard_b, got_b, "b_join_high")
    got_b = swap(shard_b, size, low_bit[1])
    other_a, other_b = swap(piece_a, size, 1), swap(shard_b, size, 1)
    late, other_a, other_b = together(((*parts_a, got_b), other_a, other_b))

    late_other = swap(stack_rows(place, late, "late"), size, 1)
    at_b = columns - 2 * shard_b.shape[0]
    places = ((IN_PLANE, 0, 0), (Z_LOW, 0, at_b), *((IN_PLANE, m, 0) for m in (1, 2, 3)))
    places += ((Z_LOW, 1, at_b),)
    outs = widen(place, (piece_a, shard_b, *late), places, True, (), "widen_own")
    d_img_proj, d_txt_proj = widen(
        place, (other_a, other_b, late_other), places, False, outs, "widen_other"
    )
    return (d_img_emb, d_txt_emb, d_img_proj, d_txt_proj)


def solution(mesh):
    return jax.shard_map(
        body,
        mesh=mesh,
        in_specs=(P("dp", None), P("dp", None), P(), P(), P(), P()),
        out_specs=(P("dp", None), P("dp", None), P(), P()),
        check_vma=False,
    )
```
